256 devices in a mesh: shard: 64 (over x, z, core), rep: 4 (over y).
Axes of the slice: x: 4, y: 4, z: 8, core: 2. Of those that a mesh axis runs over, the one named last changes fastest.
Arguments:
- embeddings: float32 [196608, 1024], P('shard'), may hold values from -6 to 6
- labels: int32 [196608], replicated, may hold values from 0 to 191, never falling along the last dimension, each value on 1 to 4096 neighbouring positions
- holder: int32 [13056, 1], P('shard'), may hold values from 0 to 4; in each aligned block of 204 rows (0 to 203, 204 to 407, ...) at most 61 rows name the same one
Outputs:
- best: float32 [196608], P('shard')
The draws below stay inside these ranges and needn't reach their ends.
Inputs may be any that keep to these rules, and one draw needn't show every extreme that they name: `labels`: labels never fall along the documents; every cluster has 1 to 4096 documents and one has exactly 4096. `holder`: among the 204 rows of one index of shard, at most 61 name any one value, a bound that some of them reach.
All inputs are finite; a program needn't handle non-finite values.
Results may differ from the reference program's by a relative error of at most 0.0012.
Values may be sent and summed in bfloat16 or wider, within the bound.
No kernel may reach another device: no remote copies, remote signals or barrier semaphores. Data moves between devices by JAX's collectives and lax.ppermute only.
A program may use at most 128 MiB of HBM per device.

```python
import math
import jax
import jax.numpy as jnp
import numpy as np
from jax import lax

D = 1024
BLOCK = 256
SPANS = 17
BLK_DEV = 12
NBLK = 768
NDOC = 196608
MOST = 4096
CLUSTERS = 192
PCAP = 61
N_REP = 4


def levels(own_key, shape, cuts, low, top_value):
    loudness = 1.0
    for dim, shards_of in cuts:
        heights = jax.random.uniform(jax.random.fold_in(jax.random.fold_in(own_key, 6), dim), (shards_of,), jnp.float32, low / len(cuts), top_value / len(cuts))
        loudness = loudness * jnp.repeat(jnp.exp(heights), shape[dim] // shards_of).reshape((-1,) + (1,) * (len(shape) - 1 - dim))
    return loudness


def length_profile(amount, total, reach, skew):
    loads = [(1 << 20) // math.isqrt(grade ** skew) + 1 for grade in range(2, amount + 1)]
    surplus, counts = total - reach - (amount - 1), [1] * (amount - 1)
    while surplus > 0:
        free = [i for i in range(amount - 1) if counts[i] < reach]
        pool, remaining = sum([loads[i] for i in free]), surplus
        for i in free:
            addition = min(reach - counts[i], max(1, remaining * loads[i] // pool), surplus)
            counts[i] = counts[i] + addition
            surplus = surplus - addition
    return np.array([reach] + counts)


def ragged(rng, count, total, reach, skew):
    if count == 2:
        one = jax.random.randint(rng, (), max(1, total - reach), min(reach, total - 1) + 1)
        return jnp.stack([one, total - one])
    sizes = jnp.asarray(length_profile(count, total, reach, skew), jnp.int32)
    twos = (count - 1) // 2
    donor, taker = sizes[1:1 + 2 * twos:2], sizes[2:2 + 2 * twos:2]
    slack = jnp.minimum(donor - 1, reach - taker)
    moved = jax.random.randint(jax.random.fold_in(rng, 1), (twos,), 0, 1 << 20) % (slack + 1)
    sizes = sizes.at[1:1 + 2 * twos:2].set(donor - moved).at[2:2 + 2 * twos:2].set(taker + moved)
    return sizes[jax.random.permutation(jax.random.fold_in(rng, 2), count)]


def deal_out(key, own, number, rows, number_of, top, most, skew):
    ranking = jax.random.permutation(key, number_of)
    heavy_load, common = load_shares(number_of, rows * top, most, skew, True), load_shares(number_of, rows * top, most, skew, False)
    places = jnp.arange(number_of)

    def named(sizes, rotation):
        used = int((sizes > 0).sum())
        fixed = max(1, used // 4)
        shifted = fixed + (places - fixed + rotation * (used - fixed)) % max(1, number_of - fixed)
        return jnp.zeros((number_of,), jnp.int32).at[ranking[jnp.where(places < fixed, places, shifted)]].set(jnp.asarray(sizes, jnp.int32))

    sizes = jnp.where(number % 4 == 0, named(heavy_load, number // 4), named(common, number - number // 4 - 1))
    mixed = jax.random.permutation(jax.random.fold_in(own, 3), number_of)
    source_of, receiver = mixed[0:number_of // 2 * 2:2], mixed[1:number_of // 2 * 2:2]
    slack = jnp.minimum(sizes[source_of] - 1, most - sizes[receiver]) // 2
    slack = jnp.where((source_of == ranking[0]) | (receiver == ranking[0]) | (sizes[receiver] == 0), 0, jnp.maximum(slack, 0))
    shifted = jax.random.randint(jax.random.fold_in(own, 4), (number_of // 2,), 0, 1 << 20) % (slack + 1)
    sizes = sizes.at[source_of].add(-shifted).at[receiver].add(shifted)
    items = jnp.searchsorted(jnp.cumsum(sizes), jnp.arange(rows * top), side="right").astype(jnp.int32)
    listing = items.reshape(top, rows).T
    listing = listing[jax.random.permutation(jax.random.fold_in(own, 1), rows)]
    rotation = jax.random.randint(jax.random.fold_in(own, 2), (rows, 1), 0, top)
    return jnp.take_along_axis(listing, (jnp.arange(top)[None, :] + rotation) % top, axis=1)


def load_shares(count, total, reach, lean, full):
    loads = [(1 << 20) // math.isqrt(standing ** lean) + 1 for standing in range(1, count + 1)]
    largest = reach if full else min(reach, max(-(-total // count), total * loads[0] // sum(loads)))
    least = 1 if total - largest >= count - 1 else 0
    counts, rest = [largest] + [least] * (count - 1), total - largest - least * (count - 1)
    while rest > 0:
        movable = [i for i in range(1, count) if counts[i] < largest] or [i for i in range(1, count) if counts[i] < reach]
        mass, budget = sum([loads[i] for i in movable]), rest
        for i in movable:
            more = min(reach - counts[i], max(1, budget * loads[i] // mass), rest)
            counts[i] = counts[i] + more
            rest = rest - more
    return np.array(counts)


def noise(rng, dims, width, most, split=(), kind=jnp.bfloat16):
    factor_of = levels(rng, dims, split, -0.22, 0.18) if split else 1.0
    array = jax.random.normal(rng, dims, jnp.float32) * width * factor_of
    return jnp.minimum(jnp.maximum(array, -most), most).astype(kind)


def setup_inputs(seed: int = 0) -> dict:
    key_of = jax.random.split(jax.random.key(seed), 4)
    embeddings = noise(key_of[0], (NDOC, D), 1.0, 6.0, ((0, 64),), jnp.float32)
    labels = jnp.searchsorted(jnp.cumsum(ragged(key_of[1], CLUSTERS, NDOC, MOST, 2)), jnp.arange(NDOC), side="right").astype(jnp.int32)
    holder_keys = jax.random.split(jax.random.fold_in(key_of[2], 1), (NBLK * SPANS) // (BLK_DEV * SPANS))
    holder_turns = jax.random.permutation(jax.random.fold_in(key_of[2], 3), (NBLK * SPANS) // (BLK_DEV * SPANS))
    holder = jax.vmap(lambda own, number: deal_out(jax.random.fold_in(key_of[2], 2), own, number, BLK_DEV * SPANS, N_REP + 1, 1, PCAP, 1))(holder_keys, holder_turns).reshape((NBLK * SPANS, 1))
    return dict(embeddings=embeddings, labels=labels, holder=holder)


epsilon = 1e-06

def reference(embeddings, labels, holder):
    squares = lax.optimization_barrier(jnp.sum(embeddings * embeddings, axis=1, keepdims=True))
    unit = (embeddings / jnp.sqrt(squares + epsilon)).astype(jnp.bfloat16).astype(jnp.float32)
    padding = (SPANS - 1) * BLOCK
    units_padded = jnp.concatenate([unit, jnp.zeros((padding, D), jnp.float32)], axis=0)
    tags_padded = jnp.concatenate([labels + 1, jnp.zeros((padding,), jnp.int32)], axis=0)
    listed = (holder[:, 0] != N_REP).reshape(NBLK, SPANS)
    span_of = jnp.arange(SPANS * BLOCK, dtype=jnp.int32) // BLOCK
    column_ids = jnp.arange(SPANS * BLOCK, dtype=jnp.int32)
    row_ids = jnp.arange(BLOCK, dtype=jnp.int32)

    def visit(running, block_index):
        start = (block_index * BLOCK).astype(jnp.int32)
        left_rows = lax.dynamic_slice_in_dim(units_padded, start, BLOCK, 0)
        right_rows = lax.dynamic_slice_in_dim(units_padded, start, SPANS * BLOCK, 0)
        left_tags = lax.dynamic_slice_in_dim(tags_padded, start, BLOCK, 0)
        right_tags = lax.dynamic_slice_in_dim(tags_padded, start, SPANS * BLOCK, 0)
        similarity = jnp.dot(left_rows, right_rows.T, precision=lax.Precision.HIGHEST, preferred_element_type=jnp.float32)
        pair_listed = listed[block_index][span_of]
        allowed = (left_tags[:, None] == right_tags[None, :]) & pair_listed[None, :] & (column_ids[None, :] != row_ids[:, None])
        scored = jnp.where(allowed, similarity, jnp.float32(-1.0))
        row_best = lax.optimization_barrier(jnp.max(scored, axis=1))
        column_best = lax.optimization_barrier(jnp.max(scored, axis=0)).reshape(SPANS, BLOCK)
        previous = lax.dynamic_slice_in_dim(running, block_index, SPANS, 0)
        running = lax.dynamic_update_slice_in_dim(running, jnp.maximum(previous, column_best), block_index, 0)
        return (running, row_best)
    initial = jnp.full((NBLK + SPANS - 1, BLOCK), -1.0, jnp.float32)
    running, row_bests = lax.scan(visit, initial, jnp.arange(NBLK, dtype=jnp.int32))
    return jnp.maximum(row_bests, running[:NBLK]).reshape(NDOC)
```

```python
import functools

import jax
import jax.numpy as jnp
from jax import lax
from jax.experimental import pallas as pl
from jax.experimental.pallas import tpu as pltpu
from jax.sharding import PartitionSpec as P

BLOCK = 256
SPANS = 17
WIDTH = 1024
OWN = 12
REPS = 4
NEAR = 4
CHIP_SLOTS = NEAR + 1
FAR_SLOTS = 2
TAIL = 16
WINDOW = OWN + 2 * (SPANS - 1)
EPS = 1e-6
VMEM_LIMIT = 48 * 1024 * 1024

HBM = pl.BlockSpec(memory_space=pl.ANY)
SMEM = pl.BlockSpec(memory_space=pltpu.SMEM)
VMEM = pl.BlockSpec(memory_space=pltpu.VMEM)


def unit_rows(rows):
    squares = jnp.sum(rows * rows, axis=1, keepdims=True)
    return (rows * lax.rsqrt(squares + EPS)).astype(jnp.bfloat16)


def rows_of(slot, count=BLOCK):
    return pl.ds(pl.multiple_of(slot * BLOCK, BLOCK), count)


def far_local(core, m):
    return jnp.where(core == 0, m - 1, OWN - m)


def chip_local(core, m):
    return jnp.where(core == 0, OWN - m, m - 1)


def far_index(rep, slot):
    return jnp.where(slot == 0, rep + 1, 8 - rep)


def chip_index(rep, slot):
    return jnp.where(slot < NEAR, slot + 1, 8 - rep)


def send_kernel(place, holder, emb, far_out, chip_out, raw, out, tails, in_sems, out_sems, tail_sems):
    core, rep = place[0] % 2, place[1]
    total = FAR_SLOTS + CHIP_SLOTS

    def local(slot):
        return jnp.where(
            slot < FAR_SLOTS,
            far_local(core, far_index(rep, slot)),
            chip_local(core, chip_index(rep, slot - FAR_SLOTS)),
        )

    def fetch(slot):
        return pltpu.make_async_copy(
            emb.at[rows_of(local(slot))], raw.at[rows_of(slot)], in_sems.at[slot]
        )

    @pl.loop(0, total)
    def _(slot):
        fetch(slot).start()

    lane = lax.broadcasted_iota(jnp.int32, (TAIL, 128), 1)
    row = lax.broadcasted_iota(jnp.int32, (TAIL, 128), 0)
    for part, (first, count) in enumerate(((0, FAR_SLOTS), (FAR_SLOTS, CHIP_SLOTS))):
        flags = jnp.zeros((TAIL, 128), jnp.float32)
        for slot in range(count):
            base = local(jnp.int32(first + slot)) * SPANS
            for k in range(SPANS):
                listed = jnp.where(holder[base + k] != REPS, 1.0, 0.0)
                flags = jnp.where((row == slot) & (lane == k), listed, flags)
        tails[part] = jnp.zeros((TAIL, WIDTH), jnp.bfloat16)
        tails[part, :, 0:128] = flags.astype(jnp.bfloat16)
    far_tail = pltpu.make_async_copy(
        tails.at[0], far_out.at[pl.ds(FAR_SLOTS * BLOCK, TAIL)], tail_sems.at[0]
    )
    chip_tail = pltpu.make_async_copy(
        tails.at[1], chip_out.at[pl.ds(CHIP_SLOTS * BLOCK, TAIL)], tail_sems.at[1]
    )
    far_tail.start()
    chip_tail.start()

    def far_push(slot):
        return pltpu.make_async_copy(
            out.at[rows_of(slot)], far_out.at[rows_of(slot)], out_sems.at[slot]
        )

    def chip_push(slot):
        return pltpu.make_async_copy(
            out.at[rows_of(slot)], chip_out.at[rows_of(slot - FAR_SLOTS)], out_sems.at[slot]
        )

    @pl.loop(0, FAR_SLOTS)
    def _(slot):
        fetch(slot).wait()
        out[rows_of(slot), :] = unit_rows(raw[rows_of(slot), :])
        far_push(slot).start()

    @pl.loop(FAR_SLOTS, total)
    def _(slot):
        fetch(slot).wait()
        out[rows_of(slot), :] = unit_rows(raw[rows_of(slot), :])
        chip_push(slot).start()

    @pl.loop(0, FAR_SLOTS)
    def _(slot):
        far_push(slot).wait()

    @pl.loop(FAR_SLOTS, total)
    def _(slot):
        chip_push(slot).wait()

    far_tail.wait()
    chip_tail.wait()


def send_payloads(place, holder, emb):
    total = FAR_SLOTS + CHIP_SLOTS
    return pl.pallas_call(
        send_kernel,
        out_shape=(
            jax.ShapeDtypeStruct((FAR_SLOTS * BLOCK + TAIL, WIDTH), jnp.bfloat16),
            jax.ShapeDtypeStruct((CHIP_SLOTS * BLOCK + TAIL, WIDTH), jnp.bfloat16),
        ),
        in_specs=[SMEM, SMEM, HBM],
        out_specs=(HBM, HBM),
        scratch_shapes=[
            pltpu.VMEM((total * BLOCK, WIDTH), jnp.float32),
            pltpu.VMEM((total * BLOCK, WIDTH), jnp.bfloat16),
            pltpu.VMEM((2, TAIL, WIDTH), jnp.bfloat16),
            pltpu.SemaphoreType.DMA((total,)),
            pltpu.SemaphoreType.DMA((total,)),
            pltpu.SemaphoreType.DMA((2,)),
        ],
        compiler_params=pltpu.CompilerParams(vmem_limit_bytes=VMEM_LIMIT),
        name="send_rows",
    )(place, holder, emb)


def similarity(left, right):
    return lax.dot_general(
        left, right, (((1,), (1,)), ((), ())), preferred_element_type=jnp.float32
    )


def inside(scored, row_low, row_count, col_low, col_count):
    rows = lax.broadcasted_iota(jnp.int32, (BLOCK, BLOCK), 0)
    cols = lax.broadcasted_iota(jnp.int32, (BLOCK, BLOCK), 1)
    keep = (rows >= row_low) & (rows < row_low + row_count)
    keep = keep & (cols >= col_low) & (cols < col_low + col_count)
    return jnp.where(keep, scored, -1.0)


def fold_rows(scored):
    return jnp.maximum(scored[:, 0:128], scored[:, 128:256])


def fold_cols(scored):
    return jnp.max(scored.reshape(BLOCK // 8, 8, BLOCK), axis=0)


def as_lanes(column):
    rows = lax.broadcasted_iota(jnp.int32, (BLOCK, BLOCK), 0)
    cols = lax.broadcasted_iota(jnp.int32, (BLOCK, BLOCK), 1)
    return jnp.max(jnp.where(rows == cols, column, -1.0), axis=0, keepdims=True)


def label_stats(stats, block):
    slot = jnp.clip(block - stats[0], 0, WINDOW - 1)
    return [stats[1 + part * WINDOW + slot] for part in range(4)]


def local_kernel(place, holder, stats, tags, emb, units_out, best, raw, units, row_acc, col_acc, in_sems, out_sems):
    shard, rep = place[0], place[1]
    first_block = shard * OWN

    def fetch(block):
        return pltpu.make_async_copy(
            emb.at[rows_of(block)], raw.at[rows_of(block)], in_sems.at[block]
        )

    def push(block):
        return pltpu.make_async_copy(
            units.at[rows_of(block)], units_out.at[rows_of(block)], out_sems.at[block]
        )

    @pl.loop(0, OWN)
    def _(block):
        fetch(block).start()

    col_acc[...] = jnp.full(col_acc.shape, -1.0, jnp.float32)
    best[...] = jnp.full(best.shape, -1.0, jnp.float32)

    @pl.loop(0, OWN)
    def _(block):
        fetch(block).wait()
        units[rows_of(block), :] = unit_rows(raw[rows_of(block), :])
        push(block).start()

        turn = lax.rem(block, 4)
        mine = jnp.where(lax.rem(block // 4, 2) == 0, turn, 3 - turn) == rep

        @pl.when(mine)
        def _():
            b_first, _, b_count, _ = label_stats(stats, first_block + block)
            row_acc[...] = jnp.full(row_acc.shape, -1.0, jnp.float32)

            @pl.loop(0, block)
            def _(other):
                _, a_last, _, a_start = label_stats(stats, first_block + other)
                listed = holder[other * SPANS + (block - other)] != REPS

                @pl.when(listed & (a_last == b_first))
                def _():
                    scored = similarity(units[rows_of(block), :], units[rows_of(other), :])
                    scored = inside(scored, 0, b_count, a_start, BLOCK - a_start)
                    row_acc[...] = jnp.maximum(row_acc[...], fold_rows(scored))
                    col_acc[other] = jnp.maximum(col_acc[other], fold_cols(scored))

            found = as_lanes(jnp.max(row_acc[...], axis=1, keepdims=True))
            best[pl.ds(block, 1), :] = found

            @pl.when(holder[block * SPANS] != REPS)
            def _():
                tag_row = tags[pl.ds(first_block - stats[0] + block, 1), :].astype(jnp.float32)
                rows = lax.broadcasted_iota(jnp.int32, (BLOCK, BLOCK), 0)
                cols = lax.broadcasted_iota(jnp.int32, (BLOCK, BLOCK), 1)
                spread = jnp.broadcast_to(tag_row, (BLOCK, BLOCK))
                tag_col = jnp.max(
                    jnp.where(rows == cols, spread, -1.0), axis=1, keepdims=True
                )
                scored = similarity(units[rows_of(block), :], units[rows_of(block), :])
                scored = jnp.where((tag_col == tag_row) & (rows != cols), scored, -1.0)
                col_acc[block] = jnp.maximum(col_acc[block], fold_cols(scored))

    for block in range(OWN):
        found = jnp.max(col_acc[block], axis=0, keepdims=True)
        best[block : block + 1, :] = jnp.maximum(best[block : block + 1, :], found)

    @pl.loop(0, OWN)
    def _(block):
        push(block).wait()


def local_pairs(place, holder, stats, tags, emb):
    return pl.pallas_call(
        local_kernel,
        out_shape=(
            jax.ShapeDtypeStruct((OWN * BLOCK, WIDTH), jnp.bfloat16),
            jax.ShapeDtypeStruct((OWN, BLOCK), jnp.float32),
        ),
        in_specs=[SMEM, SMEM, SMEM, VMEM, HBM],
        out_specs=(HBM, VMEM),
        scratch_shapes=[
            pltpu.VMEM((OWN * BLOCK, WIDTH), jnp.float32),
            pltpu.VMEM((OWN * BLOCK, WIDTH), jnp.bfloat16),
            pltpu.VMEM((BLOCK, 128), jnp.float32),
            pltpu.VMEM((OWN, 8, BLOCK), jnp.float32),
            pltpu.SemaphoreType.DMA((OWN,)),
            pltpu.SemaphoreType.DMA((OWN,)),
        ],
        compiler_params=pltpu.CompilerParams(vmem_limit_bytes=VMEM_LIMIT),
        cost_estimate=pl.CostEstimate(
            flops=20 * 2 * BLOCK * BLOCK * WIDTH, bytes_accessed=18 << 20, transcendentals=0
        ),
        name="local_pairs",
    )(place, holder, stats, tags, emb)


def flag_bits(tail, slot):
    lane = lax.broadcasted_iota(jnp.int32, (TAIL, 128), 1)
    row = lax.broadcasted_iota(jnp.int32, (TAIL, 128), 0)
    weight = lax.shift_left(jnp.int32(1), jnp.minimum(lane, SPANS)).astype(jnp.float32)
    weight = jnp.where((row == slot) & (lane < SPANS), weight, 0.0)
    return jnp.sum(tail[:, 0:128].astype(jnp.float32) * weight).astype(jnp.int32)


def cross_kernel(
    far, block_count, place, holder, stats, best_in, units_hbm, chip_hbm, *rest
):
    if far:
        far_hbm, best, returned, units, chip, moved, bits, row_acc, col_acc, unit_sems, in_sems = rest
    else:
        best, units, chip, bits, row_acc, col_acc, unit_sems, in_sems = rest
        moved = chip
    shard, rep = place[0], place[1]
    core = lax.rem(shard, 2)
    side = core if far else 1 - core
    columns = OWN + NEAR if far else OWN
    first_block = shard * OWN
    chip_rows = CHIP_SLOTS * BLOCK + TAIL

    def local(m):
        return far_local(core, m) if far else chip_local(core, m)

    def fetch(m):
        block = rows_of(local(m))
        return pltpu.make_async_copy(units_hbm.at[block], units.at[block], unit_sems.at[m - 1])

    fetch_chip = pltpu.make_async_copy(chip_hbm, chip, in_sems.at[0])
    fetch_chip.start()
    if far:
        fetch_far = pltpu.make_async_copy(far_hbm, moved, in_sems.at[1])
        fetch_far.start()

    @pl.loop(1, OWN + 1)
    def _(m):
        fetch(m).start()

    col_acc[...] = jnp.full(col_acc.shape, -1.0, jnp.float32)
    row_acc[...] = jnp.full(row_acc.shape, -1.0, jnp.float32)
    fetch_chip.wait()
    chip_tail = chip[pl.ds(CHIP_SLOTS * BLOCK, TAIL), :]
    for slot in range(CHIP_SLOTS):
        bits[slot] = flag_bits(chip_tail, slot)
    if far:
        fetch_far.wait()
        far_tail = moved[pl.ds(FAR_SLOTS * BLOCK, TAIL), :]
        for slot in range(FAR_SLOTS):
            bits[CHIP_SLOTS + slot] = flag_bits(far_tail, slot)

    def moved_slot(which):
        if far:
            return which
        return jnp.where(which == 0, rep, NEAR)

    def compare(which, m, column):
        near = far_index(rep, which)
        moved_block = jnp.where(side == 0, first_block - near, first_block + OWN - 1 + near)
        column_block = jnp.where(side == 0, first_block + m - 1, first_block + OWN - m)
        offset = near + m - 1
        tie = lax.rem(near, 2) == 1 - side
        wanted = (m > near) | ((m == near) & tie)
        wanted = wanted & (offset < SPANS)
        wanted = wanted & (moved_block >= 0) & (moved_block < block_count)
        offset = jnp.minimum(offset, SPANS - 1)
        bit_slot = moved_slot(which) + (CHIP_SLOTS if far else 0)
        own_flag = holder[jnp.minimum(local(jnp.minimum(m, OWN)), OWN - 1) * SPANS + offset] != REPS
        bit_source = jnp.where(side == 0, bit_slot, jnp.clip(m - OWN - 1, 0, NEAR - 1))
        bit_flag = lax.rem(lax.shift_right_logical(bits[bit_source], offset), 2) == 1
        listed = jnp.where((side == 0) | (m > OWN), bit_flag, own_flag)
        m_first, m_last, m_count, m_start = label_stats(stats, moved_block)
        c_first, c_last, c_count, c_start = label_stats(stats, column_block)
        shared = jnp.where(side == 0, m_last == c_first, c_last == m_first)

        @pl.when(wanted & listed & shared)
        def _():
            scored = similarity(moved[rows_of(moved_slot(which)), :], column)
            scored = inside(
                scored,
                jnp.where(side == 0, m_start, 0),
                jnp.where(side == 0, BLOCK - m_start, m_count),
                jnp.where(side == 0, 0, c_start),
                jnp.where(side == 0, c_count, BLOCK - c_start),
            )
            row_acc[which] = jnp.maximum(row_acc[which], fold_rows(scored))
            col_acc[m - 1] = jnp.maximum(col_acc[m - 1], fold_cols(scored))

    @pl.loop(1, OWN + 1)
    def _(m):
        fetch(m).wait()

        @pl.loop(0, 2)
        def _(which):
            compare(which, m, units[rows_of(local(m)), :])

    if far:
        @pl.loop(OWN + 1, OWN + NEAR + 1)
        def _(m):
            compare(jnp.int32(0), m, chip[rows_of(m - OWN - 1), :])

    best[...] = best_in[...]

    def improve(place_core, block, found):
        here = (place_core, pl.ds(block, 1), slice(None))
        best[here] = jnp.maximum(best[here], found)

    for m in range(1, OWN + 1):
        improve(core, local(m), jnp.max(col_acc[m - 1], axis=0, keepdims=True))
    if far:
        for m in range(OWN + 1, OWN + NEAR + 1):
            found = jnp.max(col_acc[m - 1], axis=0, keepdims=True)
            improve(1 - core, chip_local(1 - core, m - OWN), found)
    for which in range(2):
        found = as_lanes(jnp.max(row_acc[which], axis=1, keepdims=True))
        if far:
            returned[which : which + 1, :] = found
        else:
            improve(1 - core, chip_local(1 - core, far_index(rep, which)), found)


def cross_pairs(far, block_count, place, holder, stats, best, units, chip, *more):
    columns = OWN + NEAR if far else OWN
    best_shape = jax.ShapeDtypeStruct((2, OWN, BLOCK), jnp.float32)
    chip_rows = CHIP_SLOTS * BLOCK + TAIL
    far_rows = FAR_SLOTS * BLOCK + TAIL
    return pl.pallas_call(
        functools.partial(cross_kernel, far, block_count),
        out_shape=(best_shape, jax.ShapeDtypeStruct((2, BLOCK), jnp.float32)) if far else best_shape,
        in_specs=[SMEM, SMEM, SMEM, VMEM] + [HBM] * (3 if far else 2),
        out_specs=(VMEM, VMEM) if far else VMEM,
        scratch_shapes=[
            pltpu.VMEM((OWN * BLOCK, WIDTH), jnp.bfloat16),
            pltpu.VMEM((chip_rows, WIDTH), jnp.bfloat16),
        ]
        + ([pltpu.VMEM((far_rows, WIDTH), jnp.bfloat16)] if far else [])
        + [
            pltpu.SMEM((CHIP_SLOTS + FAR_SLOTS,), jnp.int32),
            pltpu.VMEM((2, BLOCK, 128), jnp.float32),
            pltpu.VMEM((columns, 8, BLOCK), jnp.float32),
            pltpu.SemaphoreType.DMA((OWN,)),
            pltpu.SemaphoreType.DMA((2,)),
        ],
        compiler_params=pltpu.CompilerParams(vmem_limit_bytes=VMEM_LIMIT),
        cost_estimate=pl.CostEstimate(
            flops=14 * 2 * BLOCK * BLOCK * WIDTH, bytes_accessed=9 << 20, transcendentals=0
        ),
        name="far_pairs" if far else "chip_pairs",
    )(place, holder, stats, best, units, chip, *more)


def shards(embeddings, labels, holder):
    count = lax.axis_size("shard")
    block_count = count * OWN
    shard = lax.axis_index("shard")
    rep = lax.axis_index("rep")
    core = shard % 2
    place = jnp.stack([shard, rep]).astype(jnp.int32)
    listing = holder.reshape(-1)

    far_out, chip_out = send_payloads(place, listing, embeddings)
    across = [(s, s + 1) for s in range(1, count - 1, 2)]
    across = across + [(b, a) for a, b in across]
    within = [(s, s ^ 1) for s in range(count)]
    far_in = lax.ppermute(far_out, "shard", across)
    chip_in = lax.ppermute(chip_out, "shard", within)

    start = jnp.clip(shard * OWN - (SPANS - 1), 0, block_count - WINDOW)
    tags = lax.dynamic_slice_in_dim(labels, start * BLOCK, WINDOW * BLOCK, 0)
    tags = tags.reshape(WINDOW, BLOCK)
    first, last = tags[:, 0], tags[:, BLOCK - 1]
    of_first = jnp.sum((tags == first[:, None]).astype(jnp.int32), axis=1)
    before_last = jnp.sum((tags < last[:, None]).astype(jnp.int32), axis=1)
    stats = jnp.concatenate([start[None].astype(jnp.int32), first, last, of_first, before_last])

    units, own_best = local_pairs(place, listing, stats, tags, embeddings)
    mine = (jnp.arange(2) == core)[:, None, None]
    best = jnp.where(mine, own_best[None], -1.0)
    best = cross_pairs(False, block_count, place, listing, stats, best, units, chip_in)
    best, returned = cross_pairs(
        True, block_count, place, listing, stats, best, units, chip_in, far_in
    )

    back = lax.ppermute(returned, "shard", across)
    has_far = (shard > 0) & (shard < count - 1)
    back = jnp.where(has_far, back, -1.0)
    blocks = jnp.arange(OWN)[None, :, None]
    for which in range(2):
        target = far_local(core, far_index(rep, which))
        best = jnp.maximum(best, jnp.where(mine & (blocks == target), back[which], -1.0))
    outgoing = jnp.broadcast_to(best[:, None], (2, REPS, OWN, BLOCK)).reshape(-1, OWN, BLOCK)
    groups = [list(range(c * 2 * REPS, (c + 1) * 2 * REPS)) for c in range(count // 2)]
    parts = lax.all_to_all(outgoing, ("shard", "rep"), 0, 0, axis_index_groups=groups)
    return jnp.max(parts, axis=0).reshape(OWN * BLOCK)


def solution(mesh):
    return jax.shard_map(
        shards,
        mesh=mesh,
        in_specs=(P("shard", None), P(), P("shard", None)),
        out_specs=P("shard"),
        check_vma=False,
    )
```

```python
import functools

import jax
import jax.numpy as jnp
from jax import lax
from jax.experimental import pallas as pl
from jax.experimental.pallas import tpu as pltpu
from jax.sharding import PartitionSpec as P

BLOCK = 256
SPANS = 17
WIDTH = 1024
OWN = 12
REPS = 4
CHIP_SLOTS = 4
FAR_SLOTS = 2
TAIL = 16
FAR_ROWS = FAR_SLOTS * BLOCK + 2 * TAIL
CHIP_ROWS = 2 * BLOCK + TAIL
EXTRA_ROWS = 2 * BLOCK
WINDOW = OWN + 2 * (SPANS - 1)
GROUP = 8 * 128 // BLOCK
CHUNK = 64
BATCH = 4
FIELDS = 8
EPS = 1e-6
VMEM_LIMIT = 20 * 1024 * 1024

HBM = pl.BlockSpec(memory_space=pltpu.HBM)
ANY = pl.BlockSpec(memory_space=pl.ANY)
SMEM = pl.BlockSpec(memory_space=pltpu.SMEM)
VMEM = pl.BlockSpec(memory_space=pltpu.VMEM)


def cost(us):
    return pl.CostEstimate(flops=0, bytes_accessed=us * 3_000_000, transcendentals=0)


PARAMS = pltpu.CompilerParams(vmem_limit_bytes=VMEM_LIMIT)


def rows_of(slot, count=BLOCK):
    return pl.ds(pl.multiple_of(slot * BLOCK, BLOCK), count)


def unit_rows(rows):
    squares = jnp.sum(rows * rows, axis=1, keepdims=True)
    return (rows * lax.rsqrt(squares + EPS)).astype(jnp.bfloat16)


def normalise(raw, raw_slot, out, out_slot):
    for step in range(BLOCK // CHUNK):
        source = pl.ds(pl.multiple_of(raw_slot * BLOCK + step * CHUNK, CHUNK), CHUNK)
        target = pl.ds(pl.multiple_of(out_slot * BLOCK + step * CHUNK, CHUNK), CHUNK)
        out[target, :] = unit_rows(raw[source, :])


def far_local(core, m):
    return jnp.where(core == 0, m - 1, OWN - m)


def chip_local(core, m):
    return jnp.where(core == 0, OWN - m, m - 1)


def far_index(rep, slot):
    return jnp.where(slot == 0, rep + 1, 8 - rep)


CHIP_INDEX = ((3, 4, 1, 2), (2, 7, 1, 3), (5, 6, 1, 2), (1, 8, 2, 3))


def chip_index(rep, slot):
    picked = jnp.int32(CHIP_INDEX[REPS - 1][slot])
    for other in range(REPS - 1):
        picked = jnp.where(rep == other, CHIP_INDEX[other][slot], picked)
    return picked


def flag_rows(holder, locals_of_slots):
    lane = lax.broadcasted_iota(jnp.int32, (TAIL, 128), 1)
    row = lax.broadcasted_iota(jnp.int32, (TAIL, 128), 0)
    flags = jnp.zeros((TAIL, 128), jnp.float32)
    for slot, local in enumerate(locals_of_slots):
        for k in range(SPANS):
            listed = jnp.where(holder[local * SPANS + k] != REPS, 1.0, 0.0)
            flags = jnp.where((row == slot) & (lane == k), listed, flags)
    return flags.astype(jnp.bfloat16)


def far_rows_kernel(place, holder_hbm, emb, far_out, raw, holder, sems, holder_sem):
    core, rep = place[0] % 2, place[1]
    local = [far_local(core, far_index(rep, slot)) for slot in range(FAR_SLOTS)]
    listing = pltpu.make_async_copy(holder_hbm, holder, holder_sem)
    listing.start()
    fetches = [
        pltpu.make_async_copy(emb.at[rows_of(local[slot])], raw.at[rows_of(slot)], sems.at[slot])
        for slot in range(FAR_SLOTS)
    ]
    for fetch in fetches:
        fetch.start()
    far_out[FAR_SLOTS * BLOCK :, :] = jnp.zeros((2 * TAIL, WIDTH), jnp.bfloat16)
    listing.wait()
    far_out[pl.ds(FAR_SLOTS * BLOCK, TAIL), 0:128] = flag_rows(holder, local)
    for slot in range(FAR_SLOTS):
        fetches[slot].wait()
        normalise(raw, slot, far_out, slot)


def far_rows(place, holder, emb):
    return pl.pallas_call(
        far_rows_kernel,
        out_shape=pltpu.VMEM((FAR_ROWS, WIDTH), jnp.bfloat16),
        in_specs=[SMEM, HBM, HBM],
        out_specs=VMEM,
        scratch_shapes=[
            pltpu.VMEM((FAR_SLOTS * BLOCK, WIDTH), jnp.float32),
            pltpu.SMEM(holder.shape, jnp.int32),
            pltpu.SemaphoreType.DMA((FAR_SLOTS,)),
            pltpu.SemaphoreType.DMA,
        ],
        compiler_params=PARAMS,
        cost_estimate=cost(1),
        name="far_rows",
    )(place, pltpu.with_memory_space_constraint(holder, pltpu.HBM), emb)


def similarity(left, right):
    return lax.dot_general(
        left, right, (((1,), (1,)), ((), ())), preferred_element_type=jnp.float32
    )


def inside(scored, row_low, row_end, col_low, col_end):
    rows = lax.broadcasted_iota(jnp.int32, (BLOCK, BLOCK), 0)
    cols = lax.broadcasted_iota(jnp.int32, (BLOCK, BLOCK), 1)
    keep = (rows >= row_low) & (rows < row_end) & (cols >= col_low) & (cols < col_end)
    return jnp.where(keep, scored, -1.0)


def fold_rows(scored):
    return jnp.maximum(scored[:, 0:128], scored[:, 128:256])


def fold_cols(scored):
    return jnp.max(scored.reshape(BLOCK // 8, 8, BLOCK), axis=0)


def as_lanes(column):
    rows = lax.broadcasted_iota(jnp.int32, (BLOCK, BLOCK), 0)
    cols = lax.broadcasted_iota(jnp.int32, (BLOCK, BLOCK), 1)
    return jnp.max(jnp.where(rows == cols, column, -1.0), axis=0, keepdims=True)


def first_group(shard, block_count):
    own = OWN // GROUP
    return jnp.clip(
        shard * own - (SPANS - 1) // GROUP, 0, (block_count - WINDOW) // GROUP
    )


def label_stats(stats, block_count, shard, block):
    slot = jnp.clip(block - first_group(shard, block_count) * GROUP, 0, WINDOW - 1)
    return [stats[part, slot] for part in range(4)]


def write_stats(tags, table):
    halves = [tags[pl.ds(half, WINDOW, stride=2), :].astype(jnp.float32) for half in range(2)]
    first, last = halves[0][:, 0:1], halves[1][:, 127:128]
    of_first = sum(jnp.where(half == first, 1.0, 0.0) for half in halves)
    before_last = sum(jnp.where(half < last, 1.0, 0.0) for half in halves)
    columns = [
        first,
        last,
        jnp.sum(of_first, axis=1, keepdims=True),
        jnp.sum(before_last, axis=1, keepdims=True),
    ]
    lane = lax.broadcasted_iota(jnp.int32, (WINDOW, 128), 1)
    spread = jnp.zeros((WINDOW, 128), jnp.float32)
    for part, column in enumerate(columns):
        spread = jnp.where(lane == part, column, spread)
    spread = jnp.concatenate([spread, jnp.zeros((128 - WINDOW, 128), jnp.float32)], axis=0)
    table[...] = spread.T[0:8, :].astype(jnp.int32)


def put_task(tasks, count, active, *fields):
    for place, field in enumerate(fields):
        tasks[count * FIELDS + place] = field
    return count + active.astype(jnp.int32)


def run_tasks(tasks, count, left, right, row_acc, col_acc):
    for extra in range(BATCH - 1):
        for field in range(FIELDS):
            tasks[(count + extra) * FIELDS + field] = 0

    @pl.loop(0, (count + BATCH - 1) // BATCH)
    def _(step):
        found = []
        for lane in range(BATCH):
            base = (step * BATCH + lane) * FIELDS
            task = [tasks[base + field] for field in range(FIELDS)]
            scored = similarity(left[rows_of(task[0]), :], right[rows_of(task[1]), :])
            scored = inside(scored, *task[2:6])
            found.append((task[6], task[7], fold_rows(scored), fold_cols(scored)))
        for row_slot, col_slot, rows, cols in found:
            row_acc[row_slot] = jnp.maximum(row_acc[row_slot], rows)
            col_acc[col_slot] = jnp.maximum(col_acc[col_slot], cols)


def task_scratch(most):
    return pltpu.SMEM(((most + BATCH) * FIELDS,), jnp.int32)


def local_class(rep, turn):
    return (rep, 7 - rep, 8 + rep)[turn]


def own_kernel(
    block_count, place, holder, labels, far, emb,
    units, chip_out, extra_out, best, stats,
    raw, tags, table, row_acc, col_acc, tasks, sems, out_sems, tag_sem, table_sem,
):
    shard, rep = place[0], place[1]
    core = lax.rem(shard, 2)
    first_block = shard * OWN
    group = first_group(shard, block_count)

    def fetch(block):
        return pltpu.make_async_copy(
            emb.at[rows_of(block)], raw.at[rows_of(block)], sems.at[block]
        )

    rows = pl.ds(pl.multiple_of(group * 8, 8), WINDOW * 2)
    fetch_tags = pltpu.make_async_copy(labels.at[rows], tags, tag_sem)
    fetch_tags.start()

    @pl.loop(1, OWN + 1)
    def _(m):
        fetch(chip_local(core, m)).start()

    local = [chip_local(core, chip_index(rep, slot)) for slot in range(CHIP_SLOTS)]
    chip_out[2 * BLOCK :, :] = jnp.zeros((TAIL, WIDTH), jnp.bfloat16)
    chip_out[2 * BLOCK :, 0:128] = flag_rows(holder, local)
    col_acc[...] = jnp.full(col_acc.shape, -1.0, jnp.float32)
    row_acc[...] = jnp.full(row_acc.shape, -1.0, jnp.float32)
    fetch_tags.wait()
    write_stats(tags, table)
    to_scalars = pltpu.make_async_copy(table, stats, table_sem)
    to_scalars.start()
    to_scalars.wait()

    def label_facts(block):
        return label_stats(stats, block_count, shard, first_block + block)

    def diagonal(block):
        at = (first_block + block - group * GROUP) * 2
        tag_row = jnp.concatenate([tags[pl.ds(at, 1), :], tags[pl.ds(at + 1, 1), :]], axis=1)
        tag_row = tag_row.astype(jnp.float32)
        rows = lax.broadcasted_iota(jnp.int32, (BLOCK, BLOCK), 0)
        cols = lax.broadcasted_iota(jnp.int32, (BLOCK, BLOCK), 1)
        spread = jnp.broadcast_to(tag_row, (BLOCK, BLOCK))
        tag_col = jnp.max(jnp.where(rows == cols, spread, -1.0), axis=1, keepdims=True)
        scored = similarity(units[rows_of(block), :], units[rows_of(block), :])
        keep = (tag_col == tag_row) & (rows != cols)
        found = fold_cols(jnp.where(keep, scored, -1.0))
        found = jnp.where(holder[block * SPANS] != REPS, found, -1.0)
        col_acc[block] = jnp.maximum(col_acc[block], found)

    def push(slot):
        target = (chip_out, extra_out)[slot // 2]
        return pltpu.make_async_copy(
            units.at[rows_of(local[slot])], target.at[rows_of(slot % 2)], out_sems.at[slot]
        )

    for phase in range(3):

        @pl.loop(4 * phase + 1, 4 * phase + 5)
        def _(m):
            block = chip_local(core, m)
            fetch(block).wait()
            normalise(raw, block, units, block)
            mine = block == local_class(rep, 0)
            for turn in range(1, 3):
                mine = mine | (block == local_class(rep, turn))
            pl.when(mine)(functools.partial(diagonal, block))

        if phase == 1:
            for slot in range(CHIP_SLOTS):
                push(slot).start()
        low = OWN - 4 - 4 * phase
        count = jnp.int32(0)
        for turn in range(3):
            if turn != phase and turn < 2 - phase:
                continue
            block = local_class(rep, turn)
            b_first, _, b_count, _ = label_facts(block)

            def visit(other, count, block=block, turn=turn, b_first=b_first, b_count=b_count):
                _, a_last, _, a_start = label_facts(other)
                listed = holder[other * SPANS + (block - other)] != REPS
                return put_task(
                    tasks, count, listed & (a_last == b_first),
                    block, other, 0, b_count, a_start, BLOCK, turn, other,
                )

            begin_0 = low if turn >= 2 - phase else 0
            end_0 = jnp.minimum(block, low + 4) if turn >= 2 - phase else 0
            end_1 = block if turn == phase else 0
            begin = jnp.where(core == 0, begin_0, 0)
            end = jnp.where(core == 0, end_0, end_1)
            count = lax.fori_loop(begin, end, visit, count)
        run_tasks(tasks, count, units, units, row_acc, col_acc)

    best[...] = jnp.max(col_acc[...], axis=1)
    for turn in range(3):
        here = (pl.ds(local_class(rep, turn), 1), slice(None))
        found = as_lanes(jnp.max(row_acc[turn], axis=1, keepdims=True))
        best[here] = jnp.maximum(best[here], found)
    for slot in range(CHIP_SLOTS):
        push(slot).wait()


def own_pairs(block_count, place, holder, labels, far, emb):
    return pl.pallas_call(
        functools.partial(own_kernel, block_count),
        out_shape=(
            pltpu.VMEM((OWN * BLOCK, WIDTH), jnp.bfloat16),
            pltpu.VMEM((CHIP_ROWS, WIDTH), jnp.bfloat16),
            pltpu.VMEM((EXTRA_ROWS, WIDTH), jnp.bfloat16),
            pltpu.VMEM((OWN, BLOCK), jnp.float32),
            jax.ShapeDtypeStruct((8, 128), jnp.int32),
        ),
        in_specs=[SMEM, SMEM, HBM, ANY, HBM],
        out_specs=(VMEM, VMEM, VMEM, VMEM, SMEM),
        scratch_shapes=[
            pltpu.VMEM((OWN * BLOCK, WIDTH), jnp.float32),
            pltpu.VMEM((WINDOW * 2, 128), jnp.int32),
            pltpu.VMEM((8, 128), jnp.int32),
            pltpu.VMEM((3, BLOCK, 128), jnp.float32),
            pltpu.VMEM((OWN, 8, BLOCK), jnp.float32),
            task_scratch(3 * 4),
            pltpu.SemaphoreType.DMA((OWN,)),
            pltpu.SemaphoreType.DMA((CHIP_SLOTS,)),
            pltpu.SemaphoreType.DMA,
            pltpu.SemaphoreType.DMA,
        ],
        compiler_params=PARAMS,
        cost_estimate=cost(6),
        name="own_pairs",
    )(place, holder, labels, far, emb)


def flag_bits(tail, slot):
    lane = lax.broadcasted_iota(jnp.int32, (TAIL, 128), 1)
    row = lax.broadcasted_iota(jnp.int32, (TAIL, 128), 0)
    weight = lax.shift_left(jnp.int32(1), jnp.minimum(lane, SPANS)).astype(jnp.float32)
    weight = jnp.where((row == slot) & (lane < SPANS), weight, 0.0)
    return jnp.sum(tail[:, 0:128].astype(jnp.float32) * weight).astype(jnp.int32)


class Boundary:
    def __init__(self, far, block_count, place, stats):
        self.far, self.block_count, self.stats = far, block_count, stats
        self.shard, self.rep = place[0], place[1]
        self.core = lax.rem(self.shard, 2)
        self.side = self.core if far else 1 - self.core
        self.tie = 1 - self.side

    def local(self, m):
        return far_local(self.core, m) if self.far else chip_local(self.core, m)

    def near(self, which):
        return far_index(self.rep, which) if self.far else chip_index(self.rep, which)

    def pair(self, which, m, moved_bits, column_flag):
        near = self.near(which)
        first_block = self.shard * OWN
        before = self.side == 0
        moved_block = jnp.where(before, first_block - near, first_block + OWN - 1 + near)
        column_block = jnp.where(before, first_block + m - 1, first_block + OWN - m)
        offset = near + m - 1
        wanted = (m > near) | ((m == near) & (lax.rem(near, 2) == self.tie))
        wanted = wanted & (offset < SPANS)
        wanted = wanted & (moved_block >= 0) & (moved_block < self.block_count)
        offset = jnp.minimum(offset, SPANS - 1)
        moved_flag = lax.rem(lax.shift_right_logical(moved_bits, offset), 2) == 1
        listed = jnp.where(before, moved_flag, column_flag(offset))
        facts = functools.partial(label_stats, self.stats, self.block_count, self.shard)
        m_first, m_last, m_count, m_start = facts(moved_block)
        c_first, c_last, c_count, c_start = facts(column_block)
        shared = jnp.where(before, m_last == c_first, c_last == m_first)
        return wanted & listed & shared, (
            jnp.where(before, m_start, 0), jnp.where(before, BLOCK, m_count),
            jnp.where(before, 0, c_start), jnp.where(before, c_count, BLOCK),
        )

    def own_tasks(self, tasks, holder, moved_bits):
        count = jnp.int32(0)
        for which in range(2):

            def visit(m, count, which=which):
                column = self.local(m)

                def flag(offset):
                    return holder[column * SPANS + offset] != REPS

                active, area = self.pair(which, m, moved_bits[which], flag)
                return put_task(tasks, count, active, which, column, *area, which, column)

            count = lax.fori_loop(self.near(which), OWN + 1, visit, count)
        return count


def far_kernel(
    block_count, place, holder, stats, best, units, far, mine, returned, row_acc, col_acc, tasks
):
    edge = Boundary(True, block_count, place, stats)
    col_acc[...] = jnp.full(col_acc.shape, -1.0, jnp.float32)
    row_acc[...] = jnp.full(row_acc.shape, -1.0, jnp.float32)
    tail = far[pl.ds(FAR_SLOTS * BLOCK, TAIL), :]
    bits = [flag_bits(tail, slot) for slot in range(2)]
    count = edge.own_tasks(tasks, holder, bits)
    run_tasks(tasks, count, far, units, row_acc, col_acc)
    mine[...] = jnp.maximum(best[...], jnp.max(col_acc[...], axis=1))
    for which in range(2):
        returned[which : which + 1, :] = as_lanes(
            jnp.max(row_acc[which], axis=1, keepdims=True)
        )


def bridge_kernel(block_count, place, stats, found, far, chip, extra, returned, other):
    edge = Boundary(True, block_count, place, stats)
    returned[...] = found[...]
    other[...] = jnp.full(other.shape, -1.0, jnp.float32)
    far_bits = flag_bits(far[pl.ds(FAR_SLOTS * BLOCK, TAIL), :], 0)
    tail = chip[pl.ds(2 * BLOCK, TAIL), :]
    pairs = []
    for slot in range(CHIP_SLOTS):
        bits = flag_bits(tail, slot)

        def flag(offset, bits=bits):
            return lax.rem(lax.shift_right_logical(bits, offset), 2) == 1

        pairs.append(edge.pair(0, OWN + chip_index(edge.rep, slot), far_bits, flag))
    some = pairs[0][0]
    for active, _ in pairs[1:]:
        some = some | active

    @pl.when(some)
    def _():
        rows, cols = [], []
        for slot, (active, area) in enumerate(pairs):
            column = (chip, extra)[slot // 2][rows_of(slot % 2), :]
            scored = inside(similarity(far[0:BLOCK, :], column), *area)
            scored = jnp.where(active, scored, -1.0)
            rows.append(fold_rows(scored))
            cols.append(fold_cols(scored))
        for slot in range(CHIP_SLOTS):
            block = chip_local(1 - edge.core, chip_index(edge.rep, slot))
            other[pl.ds(block, 1), :] = jnp.max(cols[slot], axis=0, keepdims=True)
        best = functools.reduce(jnp.maximum, rows)
        best = as_lanes(jnp.max(best, axis=1, keepdims=True))
        returned[0:1, :] = jnp.maximum(returned[0:1, :], best)


def chip_kernel(
    block_count, place, holder, stats, mine_in, other_in, units, chip,
    mine, other, row_acc, col_acc, tasks,
):
    edge = Boundary(False, block_count, place, stats)
    col_acc[...] = jnp.full(col_acc.shape, -1.0, jnp.float32)
    row_acc[...] = jnp.full(row_acc.shape, -1.0, jnp.float32)
    tail = chip[pl.ds(2 * BLOCK, TAIL), :]
    bits = [flag_bits(tail, slot) for slot in range(2)]
    count = edge.own_tasks(tasks, holder, bits)
    run_tasks(tasks, count, chip, units, row_acc, col_acc)
    mine[...] = jnp.maximum(mine_in[...], jnp.max(col_acc[...], axis=1))
    other[...] = other_in[...]
    for which in range(2):
        here = (pl.ds(chip_local(1 - edge.core, edge.near(which)), 1), slice(None))
        found = as_lanes(jnp.max(row_acc[which], axis=1, keepdims=True))
        other[here] = jnp.maximum(other[here], found)


BEST = pltpu.VMEM((OWN, BLOCK), jnp.float32)
RETURNED = pltpu.VMEM((2, BLOCK), jnp.float32)


def pair_call(kernel, name, us, outs, scalars, scratch, args):
    return pl.pallas_call(
        kernel,
        out_shape=outs,
        in_specs=[SMEM] * scalars + [VMEM] * (len(args) - scalars),
        out_specs=(VMEM,) * len(outs),
        scratch_shapes=scratch,
        compiler_params=PARAMS,
        cost_estimate=cost(us),
        name=name,
    )(*args)


PAIR_SCRATCH = [
    pltpu.VMEM((2, BLOCK, 128), jnp.float32),
    pltpu.VMEM((OWN, 8, BLOCK), jnp.float32),
    task_scratch(2 * OWN),
]


def finish_kernel(block_count, place, mine, other, back, outgoing, merged):
    shard, rep = place[0], place[1]
    core = lax.rem(shard, 2)
    has_far = (shard > 0) & (shard < block_count // OWN - 1)
    merged[...] = mine[...]
    for which in range(2):
        here = (pl.ds(far_local(core, far_index(rep, which)), 1), slice(None))
        found = jnp.where(has_far, back[which : which + 1, :], -1.0)
        merged[here] = jnp.maximum(merged[here], found)
    for target in range(2):
        share = jnp.where(core == target, merged[...], other[...])
        for copy in range(REPS):
            outgoing[target * REPS + copy] = share


def finish(block_count, place, mine, other, back):
    return pl.pallas_call(
        functools.partial(finish_kernel, block_count),
        out_shape=jax.ShapeDtypeStruct((2 * REPS, OWN, BLOCK), jnp.float32),
        in_specs=[SMEM, VMEM, VMEM, VMEM],
        out_specs=VMEM,
        scratch_shapes=[pltpu.VMEM((OWN, BLOCK), jnp.float32)],
        compiler_params=PARAMS,
        cost_estimate=cost(1),
        name="finish",
    )(place, mine, other, back)


def shards(embeddings, labels, holder):
    count = lax.axis_size("shard")
    block_count = count * OWN
    place = jnp.stack([lax.axis_index("shard"), lax.axis_index("rep")]).astype(jnp.int32)
    listing = holder.reshape(-1)
    labels = pltpu.with_memory_space_constraint(labels.reshape(-1, 128), pltpu.HBM)
    embeddings = pltpu.with_memory_space_constraint(embeddings, pltpu.HBM)
    across = [(s, s + 1) for s in range(1, count - 1, 2)]
    across = across + [(b, a) for a, b in across]
    within = [(s, s ^ 1) for s in range(count)]

    def in_vmem(array):
        return pltpu.with_memory_space_constraint(array, pltpu.VMEM)

    far_out = far_rows(place, listing, embeddings)
    far_in = in_vmem(lax.ppermute(far_out, "shard", across))
    units, chip_out, extra_out, best, stats = own_pairs(
        block_count, place, listing, labels, far_out, embeddings
    )
    chip_in = in_vmem(lax.ppermute(chip_out, "shard", within))
    extra_in = in_vmem(lax.ppermute(extra_out, "shard", within))

    mine, found = pair_call(
        functools.partial(far_kernel, block_count), "far_pairs", 4, (BEST, RETURNED),
        3, PAIR_SCRATCH, (place, listing, stats, best, units, far_in),
    )
    returned, other = pair_call(
        functools.partial(bridge_kernel, block_count), "bridge_pairs", 1, (RETURNED, BEST),
        2, [], (place, stats, found, far_in, chip_in, extra_in),
    )
    back = lax.ppermute(returned, "shard", across)
    mine, other = pair_call(
        functools.partial(chip_kernel, block_count), "chip_pairs", 4, (BEST, BEST),
        3, PAIR_SCRATCH, (place, listing, stats, mine, other, units, chip_in),
    )
    outgoing = finish(block_count, place, mine, other, back)
    groups = [list(range(c * 2 * REPS, (c + 1) * 2 * REPS)) for c in range(count // 2)]
    parts = lax.all_to_all(outgoing, ("shard", "rep"), 0, 0, axis_index_groups=groups)
    return jnp.max(parts, axis=0).reshape(OWN * BLOCK)


def solution(mesh):
    return jax.shard_map(
        shards,
        mesh=mesh,
        in_specs=(P("shard", None), P(), P("shard", None)),
        out_specs=P("shard"),
        check_vma=False,
    )
```

```python
import functools

import jax
import jax.numpy as jnp
from jax import lax
from jax.experimental import pallas as pl
from jax.experimental.pallas import tpu as pltpu
from jax.sharding import PartitionSpec as P

BLOCK = 256
SPANS = 17
WIDTH = 1024
OWN = 12
REPS = 4
CHIP_SLOTS = 4
FAR_SLOTS = 2
TAIL = 16
FAR_ROWS = FAR_SLOTS * BLOCK + TAIL
CHIP_ROWS = CHIP_SLOTS * BLOCK + TAIL
WINDOW = OWN + 2 * (SPANS - 1)
GROUP = 8 * 128 // BLOCK
CHUNK = 64
WIDE, NARROW = 8, 4
FIELDS = 8
EPS = 1e-6
VMEM_LIMIT = 20 * 1024 * 1024

HBM = pl.BlockSpec(memory_space=pltpu.HBM)
ANY = pl.BlockSpec(memory_space=pl.ANY)
SMEM = pl.BlockSpec(memory_space=pltpu.SMEM)
VMEM = pl.BlockSpec(memory_space=pltpu.VMEM)


def cost(us, flops=0):
    return pl.CostEstimate(flops=flops, bytes_accessed=us * 3_000_000, transcendentals=0)


PARAMS = pltpu.CompilerParams(vmem_limit_bytes=VMEM_LIMIT)


def rows_of(slot, count=BLOCK):
    return pl.ds(pl.multiple_of(slot * BLOCK, BLOCK), count)


def unit_rows(rows):
    squares = jnp.sum(rows * rows, axis=1, keepdims=True)
    return (rows * lax.rsqrt(squares + EPS)).astype(jnp.bfloat16)


def normalise(raw, raw_slot, out, out_slot):
    for step in range(BLOCK // CHUNK):
        source = pl.ds(pl.multiple_of(raw_slot * BLOCK + step * CHUNK, CHUNK), CHUNK)
        target = pl.ds(pl.multiple_of(out_slot * BLOCK + step * CHUNK, CHUNK), CHUNK)
        out[target, :] = unit_rows(raw[source, :])


def far_local(core, m):
    return jnp.where(core == 0, m - 1, OWN - m)


def chip_local(core, m):
    return jnp.where(core == 0, OWN - m, m - 1)


def far_index(rep, slot):
    return jnp.where(slot == 0, rep + 1, 8 - rep)


CHIP_INDEX = ((3, 4, 1, 2), (2, 7, 1, 3), (5, 6, 1, 2), (1, 8, 2, 3))


def chip_index(rep, slot):
    picked = jnp.int32(CHIP_INDEX[REPS - 1][slot])
    for other in range(REPS - 1):
        picked = jnp.where(rep == other, CHIP_INDEX[other][slot], picked)
    return picked


def flag_rows(holder, locals_of_slots):
    lane = lax.broadcasted_iota(jnp.int32, (TAIL, 128), 1)
    row = lax.broadcasted_iota(jnp.int32, (TAIL, 128), 0)
    flags = jnp.zeros((TAIL, 128), jnp.float32)
    for slot, local in enumerate(locals_of_slots):
        for k in range(SPANS):
            listed = jnp.where(holder[local * SPANS + k] != REPS, 1.0, 0.0)
            flags = jnp.where((row == slot) & (lane == k), listed, flags)
    return flags.astype(jnp.bfloat16)


def far_rows_kernel(place, holder_hbm, emb, far_out, raw, holder, sems, holder_sem):
    core, rep = place[0] % 2, place[1]
    local = [far_local(core, far_index(rep, slot)) for slot in range(FAR_SLOTS)]
    listing = pltpu.make_async_copy(holder_hbm, holder, holder_sem)
    listing.start()
    fetches = []
    for slot in range(FAR_SLOTS):
        for step in range(BLOCK // CHUNK):
            source = pl.ds(pl.multiple_of(local[slot] * BLOCK + step * CHUNK, CHUNK), CHUNK)
            part = pl.ds(slot * BLOCK + step * CHUNK, CHUNK)
            sem = sems.at[len(fetches)]
            fetches.append((part, pltpu.make_async_copy(emb.at[source], raw.at[part], sem)))
    for _, fetch in fetches:
        fetch.start()
    far_out[FAR_SLOTS * BLOCK :, :] = jnp.zeros((TAIL, WIDTH), jnp.bfloat16)
    listing.wait()
    far_out[pl.ds(FAR_SLOTS * BLOCK, TAIL), 0:128] = flag_rows(holder, local)
    for part, fetch in fetches:
        fetch.wait()
        far_out[part, :] = unit_rows(raw[part, :])


def far_rows(place, holder, emb):
    return pl.pallas_call(
        far_rows_kernel,
        out_shape=pltpu.VMEM((FAR_ROWS, WIDTH), jnp.bfloat16),
        in_specs=[SMEM, HBM, HBM],
        out_specs=VMEM,
        scratch_shapes=[
            pltpu.VMEM((FAR_SLOTS * BLOCK, WIDTH), jnp.float32),
            pltpu.SMEM(holder.shape, jnp.int32),
            pltpu.SemaphoreType.DMA((FAR_SLOTS * BLOCK // CHUNK,)),
            pltpu.SemaphoreType.DMA,
        ],
        compiler_params=PARAMS,
        cost_estimate=cost(1),
        name="far_rows",
    )(place, pltpu.with_memory_space_constraint(holder, pltpu.HBM), emb)


def similarity(left, right):
    return lax.dot_general(
        left, right, (((1,), (1,)), ((), ())), preferred_element_type=jnp.float32
    )


def inside(scored, row_low, row_end, col_low, col_end):
    rows = lax.broadcasted_iota(jnp.int32, (BLOCK, BLOCK), 0)
    cols = lax.broadcasted_iota(jnp.int32, (BLOCK, BLOCK), 1)
    keep = (rows >= row_low) & (rows < row_end) & (cols >= col_low) & (cols < col_end)
    return jnp.where(keep, scored, -1.0)


def fold_rows(scored):
    return jnp.maximum(scored[:, 0:128], scored[:, 128:256])


def fold_cols(scored):
    return jnp.max(scored.reshape(BLOCK // 8, 8, BLOCK), axis=0)


def as_lanes(column):
    rows = lax.broadcasted_iota(jnp.int32, (BLOCK, BLOCK), 0)
    cols = lax.broadcasted_iota(jnp.int32, (BLOCK, BLOCK), 1)
    return jnp.max(jnp.where(rows == cols, column, -1.0), axis=0, keepdims=True)


def first_group(shard, block_count):
    own = OWN // GROUP
    return jnp.clip(
        shard * own - (SPANS - 1) // GROUP, 0, (block_count - WINDOW) // GROUP
    )


def label_stats(stats, block_count, shard, block):
    slot = jnp.clip(block - first_group(shard, block_count) * GROUP, 0, WINDOW - 1)
    return [stats[part, slot] for part in range(4)]


def write_stats(tags, table):
    halves = [tags[pl.ds(half, WINDOW, stride=2), :].astype(jnp.float32) for half in range(2)]
    first, last = halves[0][:, 0:1], halves[1][:, 127:128]
    of_first = sum(jnp.where(half == first, 1.0, 0.0) for half in halves)
    before_last = sum(jnp.where(half < last, 1.0, 0.0) for half in halves)
    columns = [
        first,
        last,
        jnp.sum(of_first, axis=1, keepdims=True),
        jnp.sum(before_last, axis=1, keepdims=True),
    ]
    lane = lax.broadcasted_iota(jnp.int32, (WINDOW, 128), 1)
    spread = jnp.zeros((WINDOW, 128), jnp.float32)
    for part, column in enumerate(columns):
        spread = jnp.where(lane == part, column, spread)
    spread = jnp.concatenate([spread, jnp.zeros((128 - WINDOW, 128), jnp.float32)], axis=0)
    table[...] = spread.T[0:8, :].astype(jnp.int32)


def put_task(tasks, count, active, *fields):
    for place, field in enumerate(fields):
        tasks[count * FIELDS + place] = field
    return count + active.astype(jnp.int32)


def pad_tasks(tasks, count):
    for extra in range(WIDE - 1):
        for field in range(FIELDS):
            tasks[(count + extra) * FIELDS + field] = 0


def run_tasks(tasks, count, left, right, row_acc, col_acc):

    def run(first, width):
        found = []
        for lane in range(width):
            base = (first + lane) * FIELDS
            task = [tasks[base + field] for field in range(FIELDS)]
            scored = similarity(left[rows_of(task[0]), :], right[rows_of(task[1]), :])
            scored = inside(scored, *task[2:6])
            found.append((task[6], task[7], fold_rows(scored), fold_cols(scored)))
        for row_slot, col_slot, rows, cols in found:
            row_acc[row_slot] = jnp.maximum(row_acc[row_slot], rows)
            col_acc[col_slot] = jnp.maximum(col_acc[col_slot], cols)

    steps = (count + WIDE - NARROW - 1) // WIDE

    @pl.loop(0, steps)
    def _(step):
        run(step * WIDE, WIDE)

    @pl.when(count > steps * WIDE)
    def _():
        run(steps * WIDE, NARROW)


def task_words(most):
    return (most + WIDE) * FIELDS


OWN_TASKS = task_words(OWN * (OWN - 1) // 2)


def local_class(rep, turn):
    return (rep, 7 - rep, 8 + rep)[turn]


def rows_kernel(
    block_count, place, holder, labels, far, emb,
    units, chip_out, best, stats, tasks,
    raw, tags, table, sems, far_sems, out_sems, tag_sem, table_sem,
):
    shard, rep = place[0], place[1]
    core = lax.rem(shard, 2)
    group = first_group(shard, block_count)
    sent = [far_local(core, far_index(rep, slot)) for slot in range(FAR_SLOTS)]
    local = [chip_local(core, chip_index(rep, slot)) for slot in range(CHIP_SLOTS)]

    def fetch(block):
        return pltpu.make_async_copy(
            emb.at[rows_of(block)], raw.at[rows_of(block)], sems.at[block]
        )

    def reuse(slot):
        return pltpu.make_async_copy(
            far.at[rows_of(slot)], units.at[rows_of(sent[slot])], far_sems.at[slot]
        )

    def push(slot):
        return pltpu.make_async_copy(
            units.at[rows_of(local[slot])], chip_out.at[rows_of(slot)], out_sems.at[slot]
        )

    def is_new(block):
        return (block != sent[0]) & (block != sent[1])

    window = pl.ds(pl.multiple_of(group * 8, 8), WINDOW * 2)
    fetch_tags = pltpu.make_async_copy(labels.at[window], tags, tag_sem)
    fetch_tags.start()

    @pl.loop(1, OWN + 1)
    def _(m):
        block = chip_local(core, m)
        pl.when(is_new(block))(lambda: fetch(block).start())

    for slot in range(FAR_SLOTS):
        reuse(slot).start()
    chip_out[CHIP_SLOTS * BLOCK :, :] = jnp.zeros((TAIL, WIDTH), jnp.bfloat16)
    chip_out[CHIP_SLOTS * BLOCK :, 0:128] = flag_rows(holder, local)
    best[...] = jnp.full(best.shape, -1.0, jnp.float32)
    fetch_tags.wait()
    write_stats(tags, table)
    to_scalars = pltpu.make_async_copy(table, stats, table_sem)
    to_scalars.start()
    for slot in range(FAR_SLOTS):
        reuse(slot).wait()

    def diagonal(block):
        at = (shard * OWN + block - group * GROUP) * 2
        tag_row = jnp.concatenate([tags[pl.ds(at, 1), :], tags[pl.ds(at + 1, 1), :]], axis=1)
        tag_row = tag_row.astype(jnp.float32)
        rows = lax.broadcasted_iota(jnp.int32, (BLOCK, BLOCK), 0)
        cols = lax.broadcasted_iota(jnp.int32, (BLOCK, BLOCK), 1)
        spread = jnp.broadcast_to(tag_row, (BLOCK, BLOCK))
        tag_col = jnp.max(jnp.where(rows == cols, spread, -1.0), axis=1, keepdims=True)
        scored = similarity(units[rows_of(block), :], units[rows_of(block), :])
        keep = (tag_col == tag_row) & (rows != cols)
        found = jnp.max(jnp.where(keep, scored, -1.0), axis=0, keepdims=True)
        best[pl.ds(block, 1), :] = jnp.where(holder[block * SPANS] != REPS, found, -1.0)

    def arrive(m):
        block = chip_local(core, m)

        @pl.when(is_new(block))
        def _():
            fetch(block).wait()
            normalise(raw, block, units, block)

        mine = block == local_class(rep, 0)
        for turn in range(1, 3):
            mine = mine | (block == local_class(rep, turn))
        pl.when(mine)(lambda: diagonal(block))

    pl.loop(1, 9)(arrive)
    for slot in range(CHIP_SLOTS):
        push(slot).start()

    to_scalars.wait()

    def label_facts(block):
        return label_stats(stats, block_count, shard, shard * OWN + block)

    count = jnp.int32(0)
    for turn in range(3):
        block = local_class(rep, turn)
        b_first, _, b_count, _ = label_facts(block)

        def visit(other, count, block=block, turn=turn, b_first=b_first, b_count=b_count):
            _, a_last, _, a_start = label_facts(other)
            listed = holder[other * SPANS + (block - other)] != REPS
            return put_task(
                tasks, count, listed & (a_last == b_first),
                block, other, 0, b_count, a_start, BLOCK, turn, other,
            )

        count = lax.fori_loop(0, block, visit, count)
    pad_tasks(tasks, count)
    tasks[OWN_TASKS] = count

    pl.loop(9, OWN + 1)(arrive)
    for slot in range(CHIP_SLOTS):
        push(slot).wait()


def own_rows(block_count, place, holder, labels, far, emb):
    return pl.pallas_call(
        functools.partial(rows_kernel, block_count),
        out_shape=(
            pltpu.VMEM((OWN * BLOCK, WIDTH), jnp.bfloat16),
            pltpu.VMEM((CHIP_ROWS, WIDTH), jnp.bfloat16),
            pltpu.VMEM((OWN, BLOCK), jnp.float32),
            jax.ShapeDtypeStruct((8, 128), jnp.int32),
            jax.ShapeDtypeStruct((OWN_TASKS + 1,), jnp.int32),
        ),
        in_specs=[SMEM, SMEM, HBM, VMEM, HBM],
        out_specs=(VMEM, VMEM, VMEM, SMEM, SMEM),
        scratch_shapes=[
            pltpu.VMEM((OWN * BLOCK, WIDTH), jnp.float32),
            pltpu.VMEM((WINDOW * 2, 128), jnp.int32),
            pltpu.VMEM((8, 128), jnp.int32),
            pltpu.SemaphoreType.DMA((OWN,)),
            pltpu.SemaphoreType.DMA((FAR_SLOTS,)),
            pltpu.SemaphoreType.DMA((CHIP_SLOTS,)),
            pltpu.SemaphoreType.DMA,
            pltpu.SemaphoreType.DMA,
        ],
        compiler_params=PARAMS,
        cost_estimate=cost(5),
        name="own_rows",
    )(place, holder, labels, far, emb)


def flag_bits(tail, slot):
    lane = lax.broadcasted_iota(jnp.int32, (TAIL, 128), 1)
    row = lax.broadcasted_iota(jnp.int32, (TAIL, 128), 0)
    weight = lax.shift_left(jnp.int32(1), jnp.minimum(lane, SPANS)).astype(jnp.float32)
    weight = jnp.where((row == slot) & (lane < SPANS), weight, 0.0)
    return jnp.sum(tail[:, 0:128].astype(jnp.float32) * weight).astype(jnp.int32)


class Boundary:
    def __init__(self, far, block_count, place, stats):
        self.far, self.block_count, self.stats = far, block_count, stats
        self.shard, self.rep = place[0], place[1]
        self.core = lax.rem(self.shard, 2)
        self.side = self.core if far else 1 - self.core
        self.tie = 1 - self.side

    def local(self, m):
        return far_local(self.core, m) if self.far else chip_local(self.core, m)

    def near(self, which):
        return far_index(self.rep, which) if self.far else chip_index(self.rep, which)

    def pair(self, which, m, moved_bits, column_flag):
        near = self.near(which)
        first_block = self.shard * OWN
        before = self.side == 0
        moved_block = jnp.where(before, first_block - near, first_block + OWN - 1 + near)
        column_block = jnp.where(before, first_block + m - 1, first_block + OWN - m)
        offset = near + m - 1
        wanted = (m > near) | ((m == near) & (lax.rem(near, 2) == self.tie))
        wanted = wanted & (offset < SPANS)
        wanted = wanted & (moved_block >= 0) & (moved_block < self.block_count)
        offset = jnp.minimum(offset, SPANS - 1)
        moved_flag = lax.rem(lax.shift_right_logical(moved_bits, offset), 2) == 1
        listed = jnp.where(before, moved_flag, column_flag(offset))
        facts = functools.partial(label_stats, self.stats, self.block_count, self.shard)
        m_first, m_last, m_count, m_start = facts(moved_block)
        c_first, c_last, c_count, c_start = facts(column_block)
        shared = jnp.where(before, m_last == c_first, c_last == m_first)
        return wanted & listed & shared, (
            jnp.where(before, m_start, 0), jnp.where(before, BLOCK, m_count),
            jnp.where(before, 0, c_start), jnp.where(before, c_count, BLOCK),
        )

    def own_tasks(self, tasks, holder, moved_bits):
        count = jnp.int32(0)
        for which in moved_bits:

            def visit(m, count, which=which):
                column = self.local(m)

                def flag(offset):
                    return holder[column * SPANS + offset] != REPS

                active, area = self.pair(which, m, moved_bits[which], flag)
                return put_task(tasks, count, active, which, column, *area, which, column)

            count = lax.fori_loop(self.near(which), OWN + 1, visit, count)
        return count


def far_kernel(
    block_count, place, holder, stats, best, units, far, mine, returned, row_acc, col_acc, tasks
):
    edge = Boundary(True, block_count, place, stats)
    col_acc[...] = jnp.full(col_acc.shape, -1.0, jnp.float32)
    row_acc[...] = jnp.full(row_acc.shape, -1.0, jnp.float32)
    tail = far[pl.ds(FAR_SLOTS * BLOCK, TAIL), :]
    bits = {slot: flag_bits(tail, slot) for slot in range(2)}
    count = edge.own_tasks(tasks, holder, bits)
    pad_tasks(tasks, count)
    run_tasks(tasks, count, far, units, row_acc, col_acc)
    mine[...] = jnp.maximum(best[...], jnp.max(col_acc[...], axis=1))
    for which in range(2):
        returned[which : which + 1, :] = as_lanes(
            jnp.max(row_acc[which], axis=1, keepdims=True)
        )


def bridge_kernel(
    block_count, place, stats, found, far, chip, returned, other
):
    edge = Boundary(True, block_count, place, stats)
    returned[...] = found[...]
    other[...] = jnp.full(other.shape, -1.0, jnp.float32)
    far_bits = flag_bits(far[pl.ds(FAR_SLOTS * BLOCK, TAIL), :], 0)
    tail = chip[pl.ds(CHIP_SLOTS * BLOCK, TAIL), :]
    pairs = []
    for slot in range(CHIP_SLOTS):
        bits = flag_bits(tail, slot)

        def flag(offset, bits=bits):
            return lax.rem(lax.shift_right_logical(bits, offset), 2) == 1

        pairs.append(edge.pair(0, OWN + chip_index(edge.rep, slot), far_bits, flag))
    some = pairs[0][0]
    for active, _ in pairs[1:]:
        some = some | active

    @pl.when(some)
    def _():
        rows, cols = [], []
        for slot, (active, area) in enumerate(pairs):
            scored = inside(similarity(far[0:BLOCK, :], chip[rows_of(slot), :]), *area)
            scored = jnp.where(active, scored, -1.0)
            rows.append(fold_rows(scored))
            cols.append(fold_cols(scored))
        for slot in range(CHIP_SLOTS):
            block = chip_local(1 - edge.core, chip_index(edge.rep, slot))
            here = (pl.ds(block, 1), slice(None))
            other[here] = jnp.max(cols[slot], axis=0, keepdims=True)
        best = functools.reduce(jnp.maximum, rows)
        best = as_lanes(jnp.max(best, axis=1, keepdims=True))
        returned[0:1, :] = jnp.maximum(returned[0:1, :], best)


def own_kernel(place, own_tasks, best, units, mine, row_acc, col_acc):
    col_acc[...] = jnp.full(col_acc.shape, -1.0, jnp.float32)
    row_acc[...] = jnp.full(row_acc.shape, -1.0, jnp.float32)
    run_tasks(own_tasks, own_tasks[OWN_TASKS], units, units, row_acc, col_acc)
    mine[...] = jnp.maximum(best[...], jnp.max(col_acc[...], axis=1))
    for turn in range(3):
        here = (pl.ds(local_class(place[1], turn), 1), slice(None))
        found = as_lanes(jnp.max(row_acc[turn], axis=1, keepdims=True))
        mine[here] = jnp.maximum(mine[here], found)


def chip_kernel(
    block_count, place, holder, stats, mine_in, other_in, units, chip,
    mine, other, row_acc, col_acc, tasks,
):
    edge = Boundary(False, block_count, place, stats)
    col_acc[...] = jnp.full(col_acc.shape, -1.0, jnp.float32)
    row_acc[...] = jnp.full(row_acc.shape, -1.0, jnp.float32)
    tail = chip[pl.ds(CHIP_SLOTS * BLOCK, TAIL), :]
    bits = {slot: flag_bits(tail, slot) for slot in range(2)}
    count = edge.own_tasks(tasks, holder, bits)
    pad_tasks(tasks, count)
    run_tasks(tasks, count, chip, units, row_acc, col_acc)
    mine[...] = jnp.maximum(mine_in[...], jnp.max(col_acc[...], axis=1))
    other[...] = other_in[...]
    for which in range(2):
        here = (pl.ds(chip_local(1 - edge.core, edge.near(which)), 1), slice(None))
        found = as_lanes(jnp.max(row_acc[which], axis=1, keepdims=True))
        other[here] = jnp.maximum(other[here], found)


BEST = pltpu.VMEM((OWN, BLOCK), jnp.float32)
RETURNED = pltpu.VMEM((2, BLOCK), jnp.float32)


def pair_call(kernel, name, estimate, outs, scalars, scratch, args):
    return pl.pallas_call(
        kernel,
        out_shape=outs,
        in_specs=[SMEM] * scalars + [VMEM] * (len(args) - scalars),
        out_specs=(VMEM,) * len(outs),
        scratch_shapes=scratch,
        compiler_params=PARAMS,
        cost_estimate=estimate,
        name=name,
    )(*args)


OWN_SCRATCH = [
    pltpu.VMEM((3, BLOCK, 128), jnp.float32),
    pltpu.VMEM((OWN, 8, BLOCK), jnp.float32),
]
EDGE_SCRATCH = [
    pltpu.VMEM((2, BLOCK, 128), jnp.float32),
    pltpu.VMEM((OWN, 8, BLOCK), jnp.float32),
    pltpu.SMEM((task_words(2 * OWN),), jnp.int32),
]


def finish_kernel(block_count, place, mine, other, back, outgoing, merged):
    shard, rep = place[0], place[1]
    core = lax.rem(shard, 2)
    has_far = (shard > 0) & (shard < block_count // OWN - 1)
    merged[...] = mine[...]
    for which in range(2):
        here = (pl.ds(far_local(core, far_index(rep, which)), 1), slice(None))
        found = jnp.where(has_far, back[which : which + 1, :], -1.0)
        merged[here] = jnp.maximum(merged[here], found)
    for target in range(2):
        share = jnp.where(core == target, merged[...], other[...])
        for copy in range(REPS):
            at = target * REPS + copy
            outgoing[at, pl.ds(0, OWN, stride=2), :] = share[:, 0:128]
            outgoing[at, pl.ds(1, OWN, stride=2), :] = share[:, 128:256]


def finish(block_count, place, mine, other, back):
    return pl.pallas_call(
        functools.partial(finish_kernel, block_count),
        out_shape=jax.ShapeDtypeStruct((2 * REPS, OWN * 2, 128), jnp.float32),
        in_specs=[SMEM, VMEM, VMEM, VMEM],
        out_specs=VMEM,
        scratch_shapes=[pltpu.VMEM((OWN, BLOCK), jnp.float32)],
        compiler_params=PARAMS,
        cost_estimate=cost(1),
        name="finish",
    )(place, mine, other, back)


def shards(embeddings, labels, holder):
    count = lax.axis_size("shard")
    block_count = count * OWN
    place = jnp.stack([lax.axis_index("shard"), lax.axis_index("rep")]).astype(jnp.int32)
    listing = holder.reshape(-1)
    labels = pltpu.with_memory_space_constraint(labels.reshape(-1, 128), pltpu.HBM)
    embeddings = pltpu.with_memory_space_constraint(embeddings, pltpu.HBM)
    across = [(s, s + 1) for s in range(1, count - 1, 2)]
    across = across + [(b, a) for a, b in across]
    within = [(s, s ^ 1) for s in range(count)]

    def in_vmem(array):
        return pltpu.with_memory_space_constraint(array, pltpu.VMEM)

    far_out = far_rows(place, listing, embeddings)
    far_in = in_vmem(lax.ppermute(far_out, "shard", across))
    units, chip_out, best, stats, tasks = own_rows(
        block_count, place, listing, labels, far_out, embeddings
    )
    chip_in = in_vmem(lax.ppermute(chip_out, "shard", within))

    (mine,) = pair_call(
        own_kernel, "own_pairs", cost(3), (BEST,), 2, OWN_SCRATCH, (place, tasks, best, units)
    )
    mine, found = pair_call(
        functools.partial(far_kernel, block_count), "far_pairs", cost(4, 10**11),
        (BEST, RETURNED), 3, EDGE_SCRATCH, (place, listing, stats, mine, units, far_in),
    )
    returned, other = pair_call(
        functools.partial(bridge_kernel, block_count), "bridge_pairs", cost(1),
        (RETURNED, BEST), 2, [], (place, stats, found, far_in, chip_in),
    )
    back = lax.ppermute(returned, "shard", across)
    mine, other = pair_call(
        functools.partial(chip_kernel, block_count), "chip_pairs", cost(4), (BEST, BEST),
        3, EDGE_SCRATCH, (place, listing, stats, mine, other, units, chip_in),
    )
    outgoing = finish(block_count, place, mine, other, back)
    groups = [list(range(c * 2 * REPS, (c + 1) * 2 * REPS)) for c in range(count // 2)]
    parts = lax.all_to_all(outgoing, ("shard", "rep"), 0, 0, axis_index_groups=groups)
    return jnp.max(parts, axis=0).reshape(OWN * BLOCK)


def solution(mesh):
    return jax.shard_map(
        shards,
        mesh=mesh,
        in_specs=(P("shard", None), P(), P("shard", None)),
        out_specs=P("shard"),
        check_vma=False,
    )
```

```python
import functools

import jax
import jax.numpy as jnp
from jax import lax
from jax.experimental import pallas as pl
from jax.experimental.pallas import tpu as pltpu
from jax.sharding import PartitionSpec as P

BLOCK = 256
SPANS = 17
WIDTH = 1024
OWN = 12
REPS = 4
NEAR = 4
CHIP_SLOTS = 2 + NEAR - 1
FAR_SLOTS = 2
TAIL = 16
FAR_ROWS = FAR_SLOTS * BLOCK + TAIL
CHIP_ROWS = CHIP_SLOTS * BLOCK + TAIL
WINDOW = OWN + 2 * (SPANS - 1)
GROUP = 8 * 128 // BLOCK
CHUNK = 64
WIDE, NARROW = 8, 4
FIELDS = 9
EPS = 1e-6
VMEM_LIMIT = 20 * 1024 * 1024

HBM = pl.BlockSpec(memory_space=pltpu.HBM)
ANY = pl.BlockSpec(memory_space=pl.ANY)
SMEM = pl.BlockSpec(memory_space=pltpu.SMEM)
VMEM = pl.BlockSpec(memory_space=pltpu.VMEM)


def cost(us, flops=0):
    return pl.CostEstimate(flops=flops, bytes_accessed=us * 3_000_000, transcendentals=0)


PARAMS = pltpu.CompilerParams(vmem_limit_bytes=VMEM_LIMIT)


def rows_of(slot, count=BLOCK):
    return pl.ds(pl.multiple_of(slot * BLOCK, BLOCK), count)


def unit_rows(rows):
    squares = jnp.sum(rows * rows, axis=1, keepdims=True)
    return (rows * lax.rsqrt(squares + EPS)).astype(jnp.bfloat16)


def normalise(raw, raw_slot, out, out_slot):
    for step in range(BLOCK // CHUNK):
        source = pl.ds(pl.multiple_of(raw_slot * BLOCK + step * CHUNK, CHUNK), CHUNK)
        target = pl.ds(pl.multiple_of(out_slot * BLOCK + step * CHUNK, CHUNK), CHUNK)
        out[target, :] = unit_rows(raw[source, :])


def far_local(core, m):
    return jnp.where(core == 0, m - 1, OWN - m)


def chip_local(core, m):
    return jnp.where(core == 0, OWN - m, m - 1)


def far_index(rep, slot):
    return jnp.where(slot == 0, rep + 1, 8 - rep)


def chip_index(rep, slot):
    if slot < 2:
        return far_index(rep, slot)
    return slot - 1 + (slot - 1 > rep).astype(jnp.int32)


def flag_rows(holder, locals_of_slots):
    lane = lax.broadcasted_iota(jnp.int32, (TAIL, 128), 1)
    row = lax.broadcasted_iota(jnp.int32, (TAIL, 128), 0)
    flags = jnp.zeros((TAIL, 128), jnp.float32)
    for slot, local in enumerate(locals_of_slots):
        for k in range(SPANS):
            listed = jnp.where(holder[local * SPANS + k] != REPS, 1.0, 0.0)
            flags = jnp.where((row == slot) & (lane == k), listed, flags)
    return flags.astype(jnp.bfloat16)


def far_rows_kernel(place, holder_hbm, emb, far_out, raw, holder, sems, holder_sem):
    core, rep = place[0] % 2, place[1]
    local = [far_local(core, far_index(rep, slot)) for slot in range(FAR_SLOTS)]
    listing = pltpu.make_async_copy(holder_hbm, holder, holder_sem)
    listing.start()
    fetches = []
    for slot in range(FAR_SLOTS):
        for step in range(BLOCK // CHUNK):
            source = pl.ds(pl.multiple_of(local[slot] * BLOCK + step * CHUNK, CHUNK), CHUNK)
            part = pl.ds(slot * BLOCK + step * CHUNK, CHUNK)
            sem = sems.at[len(fetches)]
            fetches.append((part, pltpu.make_async_copy(emb.at[source], raw.at[part], sem)))
    for _, fetch in fetches:
        fetch.start()
    far_out[FAR_SLOTS * BLOCK :, :] = jnp.zeros((TAIL, WIDTH), jnp.bfloat16)
    for part, fetch in fetches:
        fetch.wait()
        far_out[part, :] = unit_rows(raw[part, :])
    listing.wait()
    far_out[pl.ds(FAR_SLOTS * BLOCK, TAIL), 0:128] = flag_rows(holder, local)


def far_rows(place, holder, emb):
    return pl.pallas_call(
        far_rows_kernel,
        out_shape=pltpu.VMEM((FAR_ROWS, WIDTH), jnp.bfloat16),
        in_specs=[SMEM, HBM, HBM],
        out_specs=VMEM,
        scratch_shapes=[
            pltpu.VMEM((FAR_SLOTS * BLOCK, WIDTH), jnp.float32),
            pltpu.SMEM(holder.shape, jnp.int32),
            pltpu.SemaphoreType.DMA((FAR_SLOTS * BLOCK // CHUNK,)),
            pltpu.SemaphoreType.DMA,
        ],
        compiler_params=PARAMS,
        cost_estimate=cost(1),
        name="far_rows",
    )(place, pltpu.with_memory_space_constraint(holder, pltpu.HBM), emb)


def similarity(left, right):
    return lax.dot_general(
        left, right, (((1,), (1,)), ((), ())), preferred_element_type=jnp.float32
    )


def inside(scored, row_low, row_end, col_low, col_end):
    rows = lax.broadcasted_iota(jnp.int32, (BLOCK, BLOCK), 0)
    cols = lax.broadcasted_iota(jnp.int32, (BLOCK, BLOCK), 1)
    keep = (rows >= row_low) & (rows < row_end) & (cols >= col_low) & (cols < col_end)
    return jnp.where(keep, scored, -1.0)


def fold_rows(scored):
    return jnp.maximum(scored[:, 0:128], scored[:, 128:256])


def fold_cols(scored):
    return jnp.max(scored.reshape(BLOCK // 8, 8, BLOCK), axis=0)


def as_lanes(column):
    rows = lax.broadcasted_iota(jnp.int32, (BLOCK, BLOCK), 0)
    cols = lax.broadcasted_iota(jnp.int32, (BLOCK, BLOCK), 1)
    return jnp.max(jnp.where(rows == cols, column, -1.0), axis=0, keepdims=True)


def first_group(shard, block_count):
    own = OWN // GROUP
    return jnp.clip(
        shard * own - (SPANS - 1) // GROUP, 0, (block_count - WINDOW) // GROUP
    )


def label_stats(stats, block_count, shard, block):
    slot = jnp.clip(block - first_group(shard, block_count) * GROUP, 0, WINDOW - 1)
    return [stats[part, slot] for part in range(4)]


def write_stats(tags, table):
    halves = [tags[pl.ds(half, WINDOW, stride=2), :].astype(jnp.float32) for half in range(2)]
    first, last = halves[0][:, 0:1], halves[1][:, 127:128]
    of_first = sum(jnp.where(half == first, 1.0, 0.0) for half in halves)
    before_last = sum(jnp.where(half < last, 1.0, 0.0) for half in halves)
    columns = [
        first,
        last,
        jnp.sum(of_first, axis=1, keepdims=True),
        jnp.sum(before_last, axis=1, keepdims=True),
    ]
    lane = lax.broadcasted_iota(jnp.int32, (WINDOW, 128), 1)
    spread = jnp.zeros((WINDOW, 128), jnp.float32)
    for part, column in enumerate(columns):
        spread = jnp.where(lane == part, column, spread)
    spread = jnp.concatenate([spread, jnp.zeros((128 - WINDOW, 128), jnp.float32)], axis=0)
    table[...] = spread.T[0:8, :].astype(jnp.int32)


def put_task(tasks, count, active, *fields):
    for place, field in enumerate(fields):
        tasks[count * FIELDS + place] = field
    return count + active.astype(jnp.int32)


def pad_tasks(tasks, count):
    for extra in range(WIDE - 1):
        for field in range(FIELDS):
            tasks[(count + extra) * FIELDS + field] = 0


def run_tasks(tasks, count, left, right, row_acc, col_acc):

    def run(first, width):
        found = []
        for lane in range(width):
            base = (first + lane) * FIELDS
            task = [tasks[base + field] for field in range(FIELDS)]
            scored = similarity(left[rows_of(task[0]), :], right[rows_of(task[1]), :])
            scored = inside(scored, *task[2:6])
            found.append((task[6], task[7], fold_rows(scored), fold_cols(scored)))
        for row_slot, col_slot, rows, cols in found:
            row_acc[row_slot] = jnp.maximum(row_acc[row_slot], rows)
            col_acc[col_slot] = jnp.maximum(col_acc[col_slot], cols)

    steps = (count + WIDE - NARROW - 1) // WIDE

    @pl.loop(0, steps)
    def _(step):
        run(step * WIDE, WIDE)

    @pl.when(count > steps * WIDE)
    def _():
        run(steps * WIDE, NARROW)


def task_words(most):
    return (most + WIDE) * FIELDS


OWN_TASKS = task_words(OWN * (OWN - 1) // 2)
EDGE_TASKS = task_words(2 * OWN)


def local_class(rep, turn):
    return (rep, 7 - rep, 8 + rep)[turn]


def rows_kernel(
    block_count, place, holder, labels, far, emb,
    units, chip_out, best, stats, tasks,
    raw, tags, table, sems, far_sems, out_sems, tag_sem, table_sem,
):
    shard, rep = place[0], place[1]
    core = lax.rem(shard, 2)
    group = first_group(shard, block_count)
    sent = [far_local(core, far_index(rep, slot)) for slot in range(FAR_SLOTS)]
    local = [chip_local(core, chip_index(rep, slot)) for slot in range(CHIP_SLOTS)]

    def fetch(block):
        return pltpu.make_async_copy(
            emb.at[rows_of(block)], raw.at[rows_of(block)], sems.at[block]
        )

    def reuse(slot):
        return pltpu.make_async_copy(
            far.at[rows_of(slot)], units.at[rows_of(sent[slot])], far_sems.at[slot]
        )

    def push(slot):
        return pltpu.make_async_copy(
            units.at[rows_of(local[slot])], chip_out.at[rows_of(slot)], out_sems.at[slot]
        )

    def is_new(block):
        return (block != sent[0]) & (block != sent[1])

    window = pl.ds(pl.multiple_of(group * 8, 8), WINDOW * 2)
    fetch_tags = pltpu.make_async_copy(labels.at[window], tags, tag_sem)
    fetch_tags.start()

    @pl.loop(1, OWN + 1)
    def _(m):
        block = chip_local(core, m)
        pl.when(is_new(block))(lambda: fetch(block).start())

    for slot in range(FAR_SLOTS):
        reuse(slot).start()
    chip_out[CHIP_SLOTS * BLOCK :, :] = jnp.zeros((TAIL, WIDTH), jnp.bfloat16)
    chip_out[CHIP_SLOTS * BLOCK :, 0:128] = flag_rows(holder, local)
    best[...] = jnp.full(best.shape, -1.0, jnp.float32)
    fetch_tags.wait()
    write_stats(tags, table)
    to_scalars = pltpu.make_async_copy(table, stats, table_sem)
    to_scalars.start()
    for slot in range(FAR_SLOTS):
        reuse(slot).wait()

    def diagonal(block):
        at = (shard * OWN + block - group * GROUP) * 2
        tag_row = jnp.concatenate([tags[pl.ds(at, 1), :], tags[pl.ds(at + 1, 1), :]], axis=1)
        tag_row = tag_row.astype(jnp.float32)
        rows = lax.broadcasted_iota(jnp.int32, (BLOCK, BLOCK), 0)
        cols = lax.broadcasted_iota(jnp.int32, (BLOCK, BLOCK), 1)
        spread = jnp.broadcast_to(tag_row, (BLOCK, BLOCK))
        tag_col = jnp.max(jnp.where(rows == cols, spread, -1.0), axis=1, keepdims=True)
        scored = similarity(units[rows_of(block), :], units[rows_of(block), :])
        keep = (tag_col == tag_row) & (rows != cols)
        found = jnp.max(jnp.where(keep, scored, -1.0), axis=0, keepdims=True)
        best[pl.ds(block, 1), :] = jnp.where(holder[block * SPANS] != REPS, found, -1.0)

    def arrive(m):
        block = chip_local(core, m)

        @pl.when(is_new(block))
        def _():
            fetch(block).wait()
            normalise(raw, block, units, block)

        mine = block == local_class(rep, 0)
        for turn in range(1, 3):
            mine = mine | (block == local_class(rep, turn))
        pl.when(mine)(lambda: diagonal(block))

    pl.loop(1, 9)(arrive)
    for slot in range(CHIP_SLOTS):
        push(slot).start()

    to_scalars.wait()

    def label_facts(block):
        return label_stats(stats, block_count, shard, shard * OWN + block)

    count = jnp.int32(0)
    for turn in range(3):
        block = local_class(rep, turn)
        b_first, _, b_count, _ = label_facts(block)

        def shares(state, b_first=b_first):
            other, _ = state
            return (other >= 0) & (label_facts(jnp.maximum(other, 0))[1] == b_first)

        def visit(state, block=block, turn=turn, b_count=b_count):
            other, count = state
            listed = holder[other * SPANS + (block - other)] != REPS
            a_start = label_facts(other)[3]
            count = put_task(
                tasks, count, listed, block, other, 0, b_count, a_start, BLOCK, turn, other,
                block - other,
            )
            return other - 1, count

        _, count = lax.while_loop(shares, visit, (block - 1, count))
    pad_tasks(tasks, count)
    tasks[OWN_TASKS] = count

    pl.loop(9, OWN + 1)(arrive)
    for slot in range(CHIP_SLOTS):
        push(slot).wait()


def own_rows(block_count, place, holder, labels, far, emb):
    return pl.pallas_call(
        functools.partial(rows_kernel, block_count),
        out_shape=(
            pltpu.VMEM((OWN * BLOCK, WIDTH), jnp.bfloat16),
            pltpu.VMEM((CHIP_ROWS, WIDTH), jnp.bfloat16),
            pltpu.VMEM((OWN, BLOCK), jnp.float32),
            jax.ShapeDtypeStruct((8, 128), jnp.int32),
            jax.ShapeDtypeStruct((OWN_TASKS + 1,), jnp.int32),
        ),
        in_specs=[SMEM, SMEM, HBM, VMEM, HBM],
        out_specs=(VMEM, VMEM, VMEM, SMEM, SMEM),
        scratch_shapes=[
            pltpu.VMEM((OWN * BLOCK, WIDTH), jnp.float32),
            pltpu.VMEM((WINDOW * 2, 128), jnp.int32),
            pltpu.VMEM((8, 128), jnp.int32),
            pltpu.SemaphoreType.DMA((OWN,)),
            pltpu.SemaphoreType.DMA((FAR_SLOTS,)),
            pltpu.SemaphoreType.DMA((CHIP_SLOTS,)),
            pltpu.SemaphoreType.DMA,
            pltpu.SemaphoreType.DMA,
        ],
        compiler_params=PARAMS,
        cost_estimate=cost(5),
        name="own_rows",
    )(place, holder, labels, far, emb)


def flag_bits(tail, slot):
    lane = lax.broadcasted_iota(jnp.int32, (TAIL, 128), 1)
    row = lax.broadcasted_iota(jnp.int32, (TAIL, 128), 0)
    weight = lax.shift_left(jnp.int32(1), jnp.minimum(lane, SPANS)).astype(jnp.float32)
    weight = jnp.where((row == slot) & (lane < SPANS), weight, 0.0)
    return jnp.sum(tail[:, 0:128].astype(jnp.float32) * weight).astype(jnp.int32)


class Boundary:
    def __init__(self, far, block_count, place):
        self.far, self.block_count = far, block_count
        self.shard, self.rep = place[0], place[1]
        self.core = lax.rem(self.shard, 2)
        self.side = self.core if far else 1 - self.core

    def local(self, m):
        return far_local(self.core, m) if self.far else chip_local(self.core, m)

    def near(self, which):
        return far_index(self.rep, which) if self.far else chip_index(self.rep, which)

    def start(self, stats, which):
        first_block = self.shard * OWN
        near = self.near(which)
        before = self.side == 0
        block = jnp.where(before, first_block - near, first_block + OWN - 1 + near)
        facts = label_stats(stats, self.block_count, self.shard, block)
        present = (block >= 0) & (block < self.block_count)
        return near, before, present, facts

    def shares(self, stats, moved, m):
        _, before, _, (m_first, m_last, _, _) = moved
        c_first, c_last, _, _ = self.column(stats, m)
        return jnp.where(before, m_last == c_first, c_last == m_first)

    def column(self, stats, m):
        first_block = self.shard * OWN
        block = jnp.where(self.side == 0, first_block + m - 1, first_block + OWN - m)
        return label_stats(stats, self.block_count, self.shard, block)

    def area(self, stats, moved, m):
        _, before, _, (_, _, m_count, m_start) = moved
        _, _, c_count, c_start = self.column(stats, m)
        return (
            jnp.where(before, m_start, 0), jnp.where(before, BLOCK, m_count),
            jnp.where(before, 0, c_start), jnp.where(before, c_count, BLOCK),
        )

    def list_tasks(self, tasks, stats, holder):
        count = jnp.int32(0)
        for which in range(2):
            moved = self.start(stats, which)
            near, before, present, _ = moved
            last = jnp.where(present, jnp.minimum(OWN, SPANS - near), 0)

            def shares(state, moved=moved, last=last):
                m, _ = state
                return (m <= last) & self.shares(stats, moved, m)

            def visit(state, which=which, moved=moved, near=near, before=before):
                m, count = state
                column, offset = self.local(m), near + m - 1
                listed = before | (holder[column * SPANS + offset] != REPS)
                area = self.area(stats, moved, m)
                count = put_task(
                    tasks, count, listed, which, column, *area, which, column, offset
                )
                return m + 1, count

            tie = lax.rem(near, 2) == 1 - self.side
            first = jnp.where(tie, near, near + 1)
            _, count = lax.while_loop(shares, visit, (first, count))
        tasks[EDGE_TASKS] = count

    def keep_listed(self, found, tasks, bits):
        def visit(index, count):
            task = [found[index * FIELDS + field] for field in range(FIELDS)]
            flags = jnp.where(task[0] == 0, bits[0], bits[1])
            listed = lax.rem(lax.shift_right_logical(flags, task[8]), 2) == 1
            return put_task(tasks, count, (self.side == 1) | listed, *task)

        count = lax.fori_loop(0, found[EDGE_TASKS], visit, jnp.int32(0))
        pad_tasks(tasks, count)
        return count


def own_kernel(
    block_count, place, holder, stats, own_tasks, best, units,
    mine, far_list, chip_list, row_acc, col_acc,
):
    col_acc[...] = jnp.full(col_acc.shape, -1.0, jnp.float32)
    row_acc[...] = jnp.full(row_acc.shape, -1.0, jnp.float32)
    run_tasks(own_tasks, own_tasks[OWN_TASKS], units, units, row_acc, col_acc)
    mine[...] = jnp.maximum(best[...], jnp.max(col_acc[...], axis=1))
    for turn in range(3):
        here = (pl.ds(local_class(place[1], turn), 1), slice(None))
        found = as_lanes(jnp.max(row_acc[turn], axis=1, keepdims=True))
        mine[here] = jnp.maximum(mine[here], found)
    edge = Boundary(True, block_count, place)
    edge.list_tasks(far_list, stats, holder)
    moved = edge.start(stats, 0)
    bridged = moved[2] & edge.shares(stats, moved, OWN + 1)
    far_list[EDGE_TASKS + 1] = bridged.astype(jnp.int32)
    Boundary(False, block_count, place).list_tasks(chip_list, stats, holder)


def far_kernel(
    block_count, place, far_list, best, units, far, mine, returned, row_acc, col_acc, tasks
):
    edge = Boundary(True, block_count, place)
    col_acc[...] = jnp.full(col_acc.shape, -1.0, jnp.float32)
    row_acc[...] = jnp.full(row_acc.shape, -1.0, jnp.float32)
    tail = far[pl.ds(FAR_SLOTS * BLOCK, TAIL), :]
    bits = [flag_bits(tail, slot) for slot in range(2)]
    count = edge.keep_listed(far_list, tasks, bits)
    run_tasks(tasks, count, far, units, row_acc, col_acc)
    mine[...] = jnp.maximum(best[...], jnp.max(col_acc[...], axis=1))
    for which in range(2):
        returned[which : which + 1, :] = as_lanes(
            jnp.max(row_acc[which], axis=1, keepdims=True)
        )


def bridge_kernel(block_count, place, far_list, stats, found, far, chip, returned, other):
    returned[...] = found[...]
    other[...] = jnp.full(other.shape, -1.0, jnp.float32)

    @pl.when(far_list[EDGE_TASKS + 1] > 0)
    def _():
        edge = Boundary(True, block_count, place)
        far_bits = flag_bits(far[pl.ds(FAR_SLOTS * BLOCK, TAIL), :], 0)
        tail = chip[pl.ds(CHIP_SLOTS * BLOCK, TAIL), :]
        moved = edge.start(stats, 0)
        rows, cols = [], []
        for slot in range(CHIP_SLOTS):
            m = OWN + chip_index(edge.rep, slot)
            offset, area = moved[0] + m - 1, edge.area(stats, moved, m)
            active = moved[2] & (offset < SPANS) & edge.shares(stats, moved, m)
            offset = jnp.minimum(offset, SPANS - 1)
            bits = jnp.where(edge.side == 0, far_bits, flag_bits(tail, slot))
            listed = lax.rem(lax.shift_right_logical(bits, offset), 2) == 1
            scored = inside(similarity(far[0:BLOCK, :], chip[rows_of(slot), :]), *area)
            scored = jnp.where(active & listed, scored, -1.0)
            rows.append(fold_rows(scored))
            cols.append(fold_cols(scored))
        for slot in range(CHIP_SLOTS):
            block = chip_local(1 - edge.core, chip_index(edge.rep, slot))
            here = (pl.ds(block, 1), slice(None))
            other[here] = jnp.max(cols[slot], axis=0, keepdims=True)
        best = functools.reduce(jnp.maximum, rows)
        best = as_lanes(jnp.max(best, axis=1, keepdims=True))
        returned[0:1, :] = jnp.maximum(returned[0:1, :], best)


def chip_kernel(
    block_count, place, chip_list, mine_in, other_in, units, chip,
    mine, other, row_acc, col_acc, tasks,
):
    edge = Boundary(False, block_count, place)
    col_acc[...] = jnp.full(col_acc.shape, -1.0, jnp.float32)
    row_acc[...] = jnp.full(row_acc.shape, -1.0, jnp.float32)
    tail = chip[pl.ds(CHIP_SLOTS * BLOCK, TAIL), :]
    bits = [flag_bits(tail, slot) for slot in range(2)]
    count = edge.keep_listed(chip_list, tasks, bits)
    run_tasks(tasks, count, chip, units, row_acc, col_acc)
    mine[...] = jnp.maximum(mine_in[...], jnp.max(col_acc[...], axis=1))
    other[...] = other_in[...]
    for which in range(2):
        here = (pl.ds(chip_local(1 - edge.core, edge.near(which)), 1), slice(None))
        found = as_lanes(jnp.max(row_acc[which], axis=1, keepdims=True))
        other[here] = jnp.maximum(other[here], found)


BEST = pltpu.VMEM((OWN, BLOCK), jnp.float32)
LIST = jax.ShapeDtypeStruct((EDGE_TASKS + 2,), jnp.int32)
RETURNED = pltpu.VMEM((2, BLOCK), jnp.float32)


def pair_call(kernel, name, estimate, outs, scalars, scratch, args):
    return pl.pallas_call(
        kernel,
        out_shape=outs,
        in_specs=[SMEM] * scalars + [VMEM] * (len(args) - scalars),
        out_specs=tuple(SMEM if out is LIST else VMEM for out in outs),
        scratch_shapes=scratch,
        compiler_params=PARAMS,
        cost_estimate=estimate,
        name=name,
    )(*args)


OWN_SCRATCH = [
    pltpu.VMEM((3, BLOCK, 128), jnp.float32),
    pltpu.VMEM((OWN, 8, BLOCK), jnp.float32),
]
EDGE_SCRATCH = [
    pltpu.VMEM((2, BLOCK, 128), jnp.float32),
    pltpu.VMEM((OWN, 8, BLOCK), jnp.float32),
    pltpu.SMEM((EDGE_TASKS,), jnp.int32),
]


def finish_kernel(block_count, place, mine, other, back, outgoing, merged):
    shard, rep = place[0], place[1]
    core = lax.rem(shard, 2)
    has_far = (shard > 0) & (shard < block_count // OWN - 1)
    merged[...] = mine[...]
    for which in range(2):
        here = (pl.ds(far_local(core, far_index(rep, which)), 1), slice(None))
        found = jnp.where(has_far, back[which : which + 1, :], -1.0)
        merged[here] = jnp.maximum(merged[here], found)
    for target in range(2):
        share = jnp.where(core == target, merged[...], other[...])
        for copy in range(REPS):
            at = target * REPS + copy
            outgoing[at, pl.ds(0, OWN, stride=2), :] = share[:, 0:128]
            outgoing[at, pl.ds(1, OWN, stride=2), :] = share[:, 128:256]


def finish(block_count, place, mine, other, back):
    return pl.pallas_call(
        functools.partial(finish_kernel, block_count),
        out_shape=jax.ShapeDtypeStruct((2 * REPS, OWN * 2, 128), jnp.float32),
        in_specs=[SMEM, VMEM, VMEM, VMEM],
        out_specs=VMEM,
        scratch_shapes=[pltpu.VMEM((OWN, BLOCK), jnp.float32)],
        compiler_params=PARAMS,
        cost_estimate=cost(1),
        name="finish",
    )(place, mine, other, back)


def shards(embeddings, labels, holder):
    count = lax.axis_size("shard")
    block_count = count * OWN
    place = jnp.stack([lax.axis_index("shard"), lax.axis_index("rep")]).astype(jnp.int32)
    listing = holder.reshape(-1)
    labels = pltpu.with_memory_space_constraint(labels.reshape(-1, 128), pltpu.HBM)
    embeddings = pltpu.with_memory_space_constraint(embeddings, pltpu.HBM)
    across = [(s, s + 1) for s in range(1, count - 1, 2)]
    across = across + [(b, a) for a, b in across]
    within = [(s, s ^ 1) for s in range(count)]

    def in_vmem(array):
        return pltpu.with_memory_space_constraint(array, pltpu.VMEM)

    far_out = far_rows(place, listing, embeddings)
    far_in = in_vmem(lax.ppermute(far_out, "shard", across))
    units, chip_out, best, stats, tasks = own_rows(
        block_count, place, listing, labels, far_out, embeddings
    )
    chip_in = in_vmem(lax.ppermute(chip_out, "shard", within))

    mine, far_list, chip_list = pair_call(
        functools.partial(own_kernel, block_count), "own_pairs", cost(3), (BEST, LIST, LIST),
        4, OWN_SCRATCH, (place, listing, stats, tasks, best, units),
    )
    mine, found = pair_call(
        functools.partial(far_kernel, block_count), "far_pairs", cost(4, 10**11),
        (BEST, RETURNED), 2, EDGE_SCRATCH, (place, far_list, mine, units, far_in),
    )
    returned, other = pair_call(
        functools.partial(bridge_kernel, block_count), "bridge_pairs", cost(1),
        (RETURNED, BEST), 3, [], (place, far_list, stats, found, far_in, chip_in),
    )
    back = lax.ppermute(returned, "shard", across)
    mine, other = pair_call(
        functools.partial(chip_kernel, block_count), "chip_pairs", cost(4), (BEST, BEST),
        2, EDGE_SCRATCH, (place, chip_list, mine, other, units, chip_in),
    )
    outgoing = finish(block_count, place, mine, other, back)
    groups = [list(range(c * 2 * REPS, (c + 1) * 2 * REPS)) for c in range(count // 2)]
    parts = lax.all_to_all(outgoing, ("shard", "rep"), 0, 0, axis_index_groups=groups)
    return jnp.max(parts, axis=0).reshape(OWN * BLOCK)


def solution(mesh):
    return jax.shard_map(
        shards,
        mesh=mesh,
        in_specs=(P("shard", None), P(), P("shard", None)),
        out_specs=P("shard"),
        check_vma=False,
    )
```

```python
import functools

import jax
import jax.numpy as jnp
from jax import lax
from jax.experimental import pallas as pl
from jax.experimental.pallas import tpu as pltpu
from jax.sharding import PartitionSpec as P

BLOCK = 256
SPANS = 17
WIDTH = 1024
OWN = 12
REPS = 4
MOVED = 8
NEAR = 4
CHIP_SLOTS = 2 + NEAR - 1
FAR_SLOTS = 2
TAIL = 16
FAR_ROWS = FAR_SLOTS * BLOCK + TAIL
CHIP_ROWS = CHIP_SLOTS * BLOCK + TAIL
WINDOW = OWN + 2 * (SPANS - 1)
GROUP = 8 * 128 // BLOCK
CHUNK = 128
WIDE, NARROW = 8, 4
FIELDS = 9
EPS = 1e-6
VMEM_LIMIT = 20 * 1024 * 1024

HBM = pl.BlockSpec(memory_space=pltpu.HBM)
ANY = pl.BlockSpec(memory_space=pl.ANY)
SMEM = pl.BlockSpec(memory_space=pltpu.SMEM)
VMEM = pl.BlockSpec(memory_space=pltpu.VMEM)


def cost(us, flops=0):
    return pl.CostEstimate(flops=flops, bytes_accessed=us * 3_000_000, transcendentals=0)


PARAMS = pltpu.CompilerParams(vmem_limit_bytes=VMEM_LIMIT)


def rows_of(slot, count=BLOCK):
    return pl.ds(pl.multiple_of(slot * BLOCK, BLOCK), count)


def unit_rows(rows):
    squares = jnp.sum(rows * rows, axis=1, keepdims=True)
    return (rows * lax.rsqrt(squares + EPS)).astype(jnp.bfloat16)


def normalise(raw, raw_slot, out, out_slot):
    for step in range(BLOCK // CHUNK):
        source = pl.ds(pl.multiple_of(raw_slot * BLOCK + step * CHUNK, CHUNK), CHUNK)
        target = pl.ds(pl.multiple_of(out_slot * BLOCK + step * CHUNK, CHUNK), CHUNK)
        out[target, :] = unit_rows(raw[source, :])


def far_local(core, m):
    return jnp.where(core == 0, m - 1, OWN - m)


def chip_local(core, m):
    return jnp.where(core == 0, OWN - m, m - 1)


def far_index(rep, slot):
    return jnp.where(slot == 0, rep + 1, MOVED - rep)


def chip_index(rep, slot):
    if slot < 2:
        return far_index(rep, slot)
    return slot - 1 + (slot - 1 > rep).astype(jnp.int32)


def flag_rows(holder, locals_of_slots):
    lane = lax.broadcasted_iota(jnp.int32, (TAIL, 128), 1)
    row = lax.broadcasted_iota(jnp.int32, (TAIL, 128), 0)
    flags = jnp.zeros((TAIL, 128), jnp.float32)
    for slot, local in enumerate(locals_of_slots):
        for k in range(SPANS):
            listed = jnp.where(holder[local * SPANS + k] != REPS, 1.0, 0.0)
            flags = jnp.where((row == slot) & (lane == k), listed, flags)
    return flags.astype(jnp.bfloat16)


def far_rows_kernel(place, holder_hbm, emb, far_out, raw, holder, sems, holder_sem):
    core, rep = place[0] % 2, place[1]
    local = [far_local(core, far_index(rep, slot)) for slot in range(FAR_SLOTS)]
    listing = pltpu.make_async_copy(holder_hbm, holder, holder_sem)
    listing.start()
    fetches = []
    for slot in range(FAR_SLOTS):
        for step in range(BLOCK // CHUNK):
            source = pl.ds(pl.multiple_of(local[slot] * BLOCK + step * CHUNK, CHUNK), CHUNK)
            part = pl.ds(slot * BLOCK + step * CHUNK, CHUNK)
            sem = sems.at[len(fetches)]
            fetches.append((part, pltpu.make_async_copy(emb.at[source], raw.at[part], sem)))
    for _, fetch in fetches:
        fetch.start()
    far_out[FAR_SLOTS * BLOCK :, :] = jnp.zeros((TAIL, WIDTH), jnp.bfloat16)
    for part, fetch in fetches:
        fetch.wait()
        far_out[part, :] = unit_rows(raw[part, :])
    listing.wait()
    far_out[pl.ds(FAR_SLOTS * BLOCK, TAIL), 0:128] = flag_rows(holder, local)


def far_rows(place, holder, emb):
    return pl.pallas_call(
        far_rows_kernel,
        out_shape=pltpu.VMEM((FAR_ROWS, WIDTH), jnp.bfloat16),
        in_specs=[SMEM, HBM, HBM],
        out_specs=VMEM,
        scratch_shapes=[
            pltpu.VMEM((FAR_SLOTS * BLOCK, WIDTH), jnp.float32),
            pltpu.SMEM(holder.shape, jnp.int32),
            pltpu.SemaphoreType.DMA((FAR_SLOTS * BLOCK // CHUNK,)),
            pltpu.SemaphoreType.DMA,
        ],
        compiler_params=PARAMS,
        cost_estimate=cost(1),
        name="far_rows",
    )(place, pltpu.with_memory_space_constraint(holder, pltpu.HBM), emb)


def similarity(left, right):
    return lax.dot_general(
        left, right, (((1,), (1,)), ((), ())), preferred_element_type=jnp.float32
    )


def inside(scored, row_low, row_end, col_low, col_end):
    rows = lax.broadcasted_iota(jnp.int32, (BLOCK, BLOCK), 0)
    cols = lax.broadcasted_iota(jnp.int32, (BLOCK, BLOCK), 1)
    keep = (rows >= row_low) & (rows < row_end) & (cols >= col_low) & (cols < col_end)
    return jnp.where(keep, scored, -1.0)


def fold_rows(scored):
    return jnp.maximum(scored[:, 0:128], scored[:, 128:256])


def fold_cols(scored):
    return jnp.max(scored.reshape(BLOCK // 8, 8, BLOCK), axis=0)


def as_lanes(column):
    rows = lax.broadcasted_iota(jnp.int32, (BLOCK, BLOCK), 0)
    cols = lax.broadcasted_iota(jnp.int32, (BLOCK, BLOCK), 1)
    return jnp.max(jnp.where(rows == cols, column, -1.0), axis=0, keepdims=True)


def first_group(shard, block_count):
    own = OWN // GROUP
    return jnp.clip(
        shard * own - (SPANS - 1) // GROUP, 0, (block_count - WINDOW) // GROUP
    )


def label_stats(stats, block_count, shard, block):
    slot = jnp.clip(block - first_group(shard, block_count) * GROUP, 0, WINDOW - 1)
    return [stats[part, slot] for part in range(4)]


def write_stats(tags, table):
    halves = [tags[pl.ds(half, WINDOW, stride=2), :].astype(jnp.float32) for half in range(2)]
    first, last = halves[0][:, 0:1], halves[1][:, 127:128]
    of_first = sum(jnp.where(half == first, 1.0, 0.0) for half in halves)
    before_last = sum(jnp.where(half < last, 1.0, 0.0) for half in halves)
    columns = [
        first,
        last,
        jnp.sum(of_first, axis=1, keepdims=True),
        jnp.sum(before_last, axis=1, keepdims=True),
    ]
    lane = lax.broadcasted_iota(jnp.int32, (WINDOW, 128), 1)
    spread = jnp.zeros((WINDOW, 128), jnp.float32)
    for part, column in enumerate(columns):
        spread = jnp.where(lane == part, column, spread)
    spread = jnp.concatenate([spread, jnp.zeros((128 - WINDOW, 128), jnp.float32)], axis=0)
    table[...] = spread.T[0:8, :].astype(jnp.int32)


def put_task(tasks, count, active, *fields):
    for place, field in enumerate(fields):
        tasks[count * FIELDS + place] = field
    return count + active.astype(jnp.int32)


def pad_tasks(tasks, count):
    for extra in range(WIDE - 1):
        for field in range(FIELDS):
            tasks[(count + extra) * FIELDS + field] = 0


def run_tasks(tasks, count, left, right, row_acc, col_acc):

    def run(first, width):
        found = []
        for lane in range(width):
            base = (first + lane) * FIELDS
            task = [tasks[base + field] for field in range(FIELDS)]
            scored = similarity(left[rows_of(task[0]), :], right[rows_of(task[1]), :])
            scored = inside(scored, *task[2:6])
            found.append((task[6], task[7], fold_rows(scored), fold_cols(scored)))
        for row_slot, col_slot, rows, cols in found:
            row_acc[row_slot] = jnp.maximum(row_acc[row_slot], rows)
            col_acc[col_slot] = jnp.maximum(col_acc[col_slot], cols)

    steps = (count + WIDE - NARROW - 1) // WIDE

    @pl.loop(0, steps)
    def _(step):
        run(step * WIDE, WIDE)

    @pl.when(count > steps * WIDE)
    def _():
        run(steps * WIDE, NARROW)


def task_words(most):
    return (most + WIDE) * FIELDS


OWN_TASKS = task_words(OWN * (OWN - 1) // 2)
EDGE_TASKS = task_words(2 * OWN)


def local_class(rep, turn):
    return (rep, 7 - rep, 8 + rep)[turn]


def rows_kernel(
    block_count, place, holder, labels, far, emb,
    units, chip_out, best, stats, tasks,
    raw, tags, table, sems, far_sems, out_sems, tag_sem, table_sem,
):
    shard, rep = place[0], place[1]
    core = lax.rem(shard, 2)
    group = first_group(shard, block_count)
    sent = [far_local(core, far_index(rep, slot)) for slot in range(FAR_SLOTS)]
    local = [chip_local(core, chip_index(rep, slot)) for slot in range(CHIP_SLOTS)]

    def fetch(block):
        return pltpu.make_async_copy(
            emb.at[rows_of(block)], raw.at[rows_of(block)], sems.at[block]
        )

    def reuse(slot):
        return pltpu.make_async_copy(
            far.at[rows_of(slot)], units.at[rows_of(sent[slot])], far_sems.at[slot]
        )

    def push(slot):
        return pltpu.make_async_copy(
            units.at[rows_of(local[slot])], chip_out.at[rows_of(slot)], out_sems.at[slot]
        )

    def is_new(block):
        return (block != sent[0]) & (block != sent[1])

    window = pl.ds(pl.multiple_of(group * 8, 8), WINDOW * 2)
    fetch_tags = pltpu.make_async_copy(labels.at[window], tags, tag_sem)
    fetch_tags.start()

    @pl.loop(1, OWN + 1)
    def _(m):
        block = chip_local(core, m)
        pl.when(is_new(block))(lambda: fetch(block).start())

    for slot in range(FAR_SLOTS):
        reuse(slot).start()
    chip_out[CHIP_SLOTS * BLOCK :, :] = jnp.zeros((TAIL, WIDTH), jnp.bfloat16)
    chip_out[CHIP_SLOTS * BLOCK :, 0:128] = flag_rows(holder, local)
    best[...] = jnp.full(best.shape, -1.0, jnp.float32)
    fetch_tags.wait()
    write_stats(tags, table)
    to_scalars = pltpu.make_async_copy(table, stats, table_sem)
    to_scalars.start()
    for slot in range(FAR_SLOTS):
        reuse(slot).wait()

    def diagonal(block):
        at = (shard * OWN + block - group * GROUP) * 2
        tag_row = jnp.concatenate([tags[pl.ds(at, 1), :], tags[pl.ds(at + 1, 1), :]], axis=1)
        tag_row = tag_row.astype(jnp.float32)
        rows = lax.broadcasted_iota(jnp.int32, (BLOCK, BLOCK), 0)
        cols = lax.broadcasted_iota(jnp.int32, (BLOCK, BLOCK), 1)
        spread = jnp.broadcast_to(tag_row, (BLOCK, BLOCK))
        tag_col = jnp.max(jnp.where(rows == cols, spread, -1.0), axis=1, keepdims=True)
        scored = similarity(units[rows_of(block), :], units[rows_of(block), :])
        keep = (tag_col == tag_row) & (rows != cols)
        found = jnp.max(jnp.where(keep, scored, -1.0), axis=0, keepdims=True)
        best[pl.ds(block, 1), :] = jnp.where(holder[block * SPANS] != REPS, found, -1.0)

    def arrive(m):
        block = chip_local(core, m)

        @pl.when(is_new(block))
        def _():
            fetch(block).wait()
            normalise(raw, block, units, block)

        mine = block == local_class(rep, 0)
        for turn in range(1, 3):
            mine = mine | (block == local_class(rep, turn))
        pl.when(mine)(lambda: diagonal(block))

    pl.loop(1, 9)(arrive)
    for slot in range(CHIP_SLOTS):
        push(slot).start()

    to_scalars.wait()

    def label_facts(block):
        return label_stats(stats, block_count, shard, shard * OWN + block)

    count = jnp.int32(0)
    for turn in range(3):
        block = local_class(rep, turn)
        b_first, _, b_count, _ = label_facts(block)

        def shares(state, b_first=b_first):
            other, _ = state
            return (other >= 0) & (label_facts(jnp.maximum(other, 0))[1] == b_first)

        def visit(state, block=block, turn=turn, b_count=b_count):
            other, count = state
            listed = holder[other * SPANS + (block - other)] != REPS
            a_start = label_facts(other)[3]
            count = put_task(
                tasks, count, listed, block, other, 0, b_count, a_start, BLOCK, turn, other,
                block - other,
            )
            return other - 1, count

        _, count = lax.while_loop(shares, visit, (block - 1, count))
    pad_tasks(tasks, count)
    tasks[OWN_TASKS] = count

    pl.loop(9, OWN + 1)(arrive)
    for slot in range(CHIP_SLOTS):
        push(slot).wait()


def own_rows(block_count, place, holder, labels, far, emb):
    return pl.pallas_call(
        functools.partial(rows_kernel, block_count),
        out_shape=(
            pltpu.VMEM((OWN * BLOCK, WIDTH), jnp.bfloat16),
            pltpu.VMEM((CHIP_ROWS, WIDTH), jnp.bfloat16),
            pltpu.VMEM((OWN, BLOCK), jnp.float32),
            jax.ShapeDtypeStruct((8, 128), jnp.int32),
            jax.ShapeDtypeStruct((OWN_TASKS + 1,), jnp.int32),
        ),
        in_specs=[SMEM, SMEM, HBM, VMEM, HBM],
        out_specs=(VMEM, VMEM, VMEM, SMEM, SMEM),
        scratch_shapes=[
            pltpu.VMEM((OWN * BLOCK, WIDTH), jnp.float32),
            pltpu.VMEM((WINDOW * 2, 128), jnp.int32),
            pltpu.VMEM((8, 128), jnp.int32),
            pltpu.SemaphoreType.DMA((OWN,)),
            pltpu.SemaphoreType.DMA((FAR_SLOTS,)),
            pltpu.SemaphoreType.DMA((CHIP_SLOTS,)),
            pltpu.SemaphoreType.DMA,
            pltpu.SemaphoreType.DMA,
        ],
        compiler_params=PARAMS,
        cost_estimate=cost(5),
        name="own_rows",
    )(place, holder, labels, far, emb)


def flag_bits(tail, slot):
    lane = lax.broadcasted_iota(jnp.int32, (TAIL, 128), 1)
    row = lax.broadcasted_iota(jnp.int32, (TAIL, 128), 0)
    weight = lax.shift_left(jnp.int32(1), jnp.minimum(lane, SPANS)).astype(jnp.float32)
    weight = jnp.where((row == slot) & (lane < SPANS), weight, 0.0)
    return jnp.sum(tail[:, 0:128].astype(jnp.float32) * weight).astype(jnp.int32)


class Boundary:
    def __init__(self, far, block_count, place):
        self.far, self.block_count = far, block_count
        self.shard, self.rep = place[0], place[1]
        self.core = lax.rem(self.shard, 2)
        self.side = self.core if far else 1 - self.core

    def local(self, m):
        return far_local(self.core, m) if self.far else chip_local(self.core, m)

    def near(self, which):
        return far_index(self.rep, which) if self.far else chip_index(self.rep, which)

    def start(self, stats, which):
        first_block = self.shard * OWN
        near = self.near(which)
        before = self.side == 0
        block = jnp.where(before, first_block - near, first_block + OWN - 1 + near)
        facts = label_stats(stats, self.block_count, self.shard, block)
        present = (block >= 0) & (block < self.block_count)
        return near, before, present, facts

    def shares(self, stats, moved, m):
        _, before, _, (m_first, m_last, _, _) = moved
        c_first, c_last, _, _ = self.column(stats, m)
        return jnp.where(before, m_last == c_first, c_last == m_first)

    def column(self, stats, m):
        first_block = self.shard * OWN
        block = jnp.where(self.side == 0, first_block + m - 1, first_block + OWN - m)
        return label_stats(stats, self.block_count, self.shard, block)

    def area(self, stats, moved, m):
        _, before, _, (_, _, m_count, m_start) = moved
        _, _, c_count, c_start = self.column(stats, m)
        return (
            jnp.where(before, m_start, 0), jnp.where(before, BLOCK, m_count),
            jnp.where(before, 0, c_start), jnp.where(before, c_count, BLOCK),
        )

    def lean(self, stats):
        middle = self.shard * OWN + jnp.where(self.side == 0, 0, OWN)
        facts = functools.partial(label_stats, stats, self.block_count, self.shard)
        label = facts(middle - 1)[1]
        ahead = lax.while_loop(
            lambda n: (n < jnp.minimum(middle, SPANS - 1)) & (facts(middle - 1 - n)[1] == label),
            lambda n: n + 1,
            jnp.int32(0),
        )
        behind = lax.while_loop(
            lambda n: (n < jnp.minimum(self.block_count - middle, SPANS - 1))
            & (facts(middle + n)[0] == label),
            lambda n: n + 1,
            jnp.int32(0),
        )
        return behind - ahead

    def first_column(self, near, lean):
        half = lax.shift_right_arithmetic(lean, 1)
        even = lean - 2 * half == 0
        behind = near + half + jnp.where(even & (lax.rem(near, 2) == 1), 0, 1)
        equal = near - half
        tie = even & (lax.rem(equal + 32, 2) == 1)
        ahead = equal + jnp.where(tie, 1, 0)
        return jnp.clip(jnp.where(self.side == 0, behind, ahead), 1, MOVED + 1)

    def list_tasks(self, tasks, stats, holder):
        count = jnp.int32(0)
        lean = self.lean(stats)
        for which in range(2):
            moved = self.start(stats, which)
            near, before, present, _ = moved
            last = jnp.where(present, jnp.minimum(OWN, SPANS - near), 0)

            def shares(state, moved=moved, last=last):
                m, _ = state
                return (m <= last) & self.shares(stats, moved, m)

            def visit(state, which=which, moved=moved, near=near, before=before):
                m, count = state
                column, offset = self.local(m), near + m - 1
                listed = before | (holder[column * SPANS + offset] != REPS)
                area = self.area(stats, moved, m)
                count = put_task(
                    tasks, count, listed, which, column, *area, which, column, offset
                )
                return m + 1, count

            first = self.first_column(near, lean)
            _, count = lax.while_loop(shares, visit, (first, count))
        tasks[EDGE_TASKS] = count

    def keep_listed(self, found, tasks, bits):
        def visit(index, count):
            task = [found[index * FIELDS + field] for field in range(FIELDS)]
            flags = jnp.where(task[0] == 0, bits[0], bits[1])
            listed = lax.rem(lax.shift_right_logical(flags, task[8]), 2) == 1
            return put_task(tasks, count, (self.side == 1) | listed, *task)

        count = lax.fori_loop(0, found[EDGE_TASKS], visit, jnp.int32(0))
        pad_tasks(tasks, count)
        return count


def own_kernel(
    block_count, place, holder, stats, own_tasks, best, units,
    mine, far_list, chip_list, row_acc, col_acc,
):
    col_acc[...] = jnp.full(col_acc.shape, -1.0, jnp.float32)
    row_acc[...] = jnp.full(row_acc.shape, -1.0, jnp.float32)
    run_tasks(own_tasks, own_tasks[OWN_TASKS], units, units, row_acc, col_acc)
    mine[...] = jnp.maximum(best[...], jnp.max(col_acc[...], axis=1))
    for turn in range(3):
        here = (pl.ds(local_class(place[1], turn), 1), slice(None))
        found = as_lanes(jnp.max(row_acc[turn], axis=1, keepdims=True))
        mine[here] = jnp.maximum(mine[here], found)
    edge = Boundary(True, block_count, place)
    edge.list_tasks(far_list, stats, holder)
    moved = edge.start(stats, 0)
    bridged = moved[2] & edge.shares(stats, moved, OWN + 1)
    far_list[EDGE_TASKS + 1] = bridged.astype(jnp.int32)
    Boundary(False, block_count, place).list_tasks(chip_list, stats, holder)


def far_kernel(
    block_count, place, far_list, best, units, far, mine, returned, row_acc, col_acc, tasks
):
    edge = Boundary(True, block_count, place)
    col_acc[...] = jnp.full(col_acc.shape, -1.0, jnp.float32)
    row_acc[...] = jnp.full(row_acc.shape, -1.0, jnp.float32)
    tail = far[pl.ds(FAR_SLOTS * BLOCK, TAIL), :]
    bits = [flag_bits(tail, slot) for slot in range(2)]
    count = edge.keep_listed(far_list, tasks, bits)
    run_tasks(tasks, count, far, units, row_acc, col_acc)
    mine[...] = jnp.maximum(best[...], jnp.max(col_acc[...], axis=1))
    for which in range(2):
        returned[which : which + 1, :] = as_lanes(
            jnp.max(row_acc[which], axis=1, keepdims=True)
        )


def bridge_kernel(block_count, place, far_list, stats, found_in, far, chip, returned, other):
    returned[...] = found_in[...]
    other[...] = jnp.full(other.shape, -1.0, jnp.float32)

    @pl.when(far_list[EDGE_TASKS + 1] > 0)
    def _():
        edge = Boundary(True, block_count, place)
        far_bits = flag_bits(far[pl.ds(FAR_SLOTS * BLOCK, TAIL), :], 0)
        tail = chip[pl.ds(CHIP_SLOTS * BLOCK, TAIL), :]
        moved = edge.start(stats, 0)
        rows, cols = [], []
        slots = (0, 2, 3, 4)
        for slot in slots:
            m = OWN + chip_index(edge.rep, slot)
            offset, area = moved[0] + m - 1, edge.area(stats, moved, m)
            active = moved[2] & (offset < SPANS) & edge.shares(stats, moved, m)
            offset = jnp.minimum(offset, SPANS - 1)
            bits = jnp.where(edge.side == 0, far_bits, flag_bits(tail, slot))
            listed = lax.rem(lax.shift_right_logical(bits, offset), 2) == 1
            scored = inside(similarity(far[0:BLOCK, :], chip[rows_of(slot), :]), *area)
            scored = jnp.where(active & listed, scored, -1.0)
            rows.append(fold_rows(scored))
            cols.append(fold_cols(scored))
        for slot, found in zip(slots, cols):
            block = chip_local(1 - edge.core, chip_index(edge.rep, slot))
            other[pl.ds(block, 1), :] = jnp.max(found, axis=0, keepdims=True)
        best = functools.reduce(jnp.maximum, rows)
        best = as_lanes(jnp.max(best, axis=1, keepdims=True))
        returned[0:1, :] = jnp.maximum(returned[0:1, :], best)


def chip_kernel(
    block_count, place, chip_list, mine_in, other_in, units, chip,
    mine, other, row_acc, col_acc, tasks,
):
    edge = Boundary(False, block_count, place)
    col_acc[...] = jnp.full(col_acc.shape, -1.0, jnp.float32)
    row_acc[...] = jnp.full(row_acc.shape, -1.0, jnp.float32)
    tail = chip[pl.ds(CHIP_SLOTS * BLOCK, TAIL), :]
    bits = [flag_bits(tail, slot) for slot in range(2)]
    count = edge.keep_listed(chip_list, tasks, bits)
    run_tasks(tasks, count, chip, units, row_acc, col_acc)
    mine[...] = jnp.maximum(mine_in[...], jnp.max(col_acc[...], axis=1))
    other[...] = other_in[...]
    for which in range(2):
        here = (pl.ds(chip_local(1 - edge.core, edge.near(which)), 1), slice(None))
        found = as_lanes(jnp.max(row_acc[which], axis=1, keepdims=True))
        other[here] = jnp.maximum(other[here], found)


BEST = pltpu.VMEM((OWN, BLOCK), jnp.float32)
LIST = jax.ShapeDtypeStruct((EDGE_TASKS + 2,), jnp.int32)
RETURNED = pltpu.VMEM((2, BLOCK), jnp.float32)


def pair_call(kernel, name, estimate, outs, scalars, scratch, args):
    return pl.pallas_call(
        kernel,
        out_shape=outs,
        in_specs=[SMEM] * scalars + [VMEM] * (len(args) - scalars),
        out_specs=tuple(SMEM if out is LIST else VMEM for out in outs),
        scratch_shapes=scratch,
        compiler_params=PARAMS,
        cost_estimate=estimate,
        name=name,
    )(*args)


OWN_SCRATCH = [
    pltpu.VMEM((3, BLOCK, 128), jnp.float32),
    pltpu.VMEM((OWN, 8, BLOCK), jnp.float32),
]
EDGE_SCRATCH = [
    pltpu.VMEM((2, BLOCK, 128), jnp.float32),
    pltpu.VMEM((OWN, 8, BLOCK), jnp.float32),
    pltpu.SMEM((EDGE_TASKS,), jnp.int32),
]


def finish_kernel(block_count, place, mine, other, back, outgoing, merged):
    shard, rep = place[0], place[1]
    core = lax.rem(shard, 2)
    has_far = (shard > 0) & (shard < block_count // OWN - 1)
    merged[...] = mine[...]
    for which in range(2):
        here = (pl.ds(far_local(core, far_index(rep, which)), 1), slice(None))
        found = jnp.where(has_far, back[which : which + 1, :], -1.0)
        merged[here] = jnp.maximum(merged[here], found)
    for target in range(2):
        share = jnp.where(core == target, merged[...], other[...])
        for copy in range(REPS):
            at = target * REPS + copy
            outgoing[at, pl.ds(0, OWN, stride=2), :] = share[:, 0:128]
            outgoing[at, pl.ds(1, OWN, stride=2), :] = share[:, 128:256]


def finish(block_count, place, mine, other, back):
    return pl.pallas_call(
        functools.partial(finish_kernel, block_count),
        out_shape=jax.ShapeDtypeStruct((2 * REPS, OWN * 2, 128), jnp.float32),
        in_specs=[SMEM, VMEM, VMEM, VMEM],
        out_specs=VMEM,
        scratch_shapes=[pltpu.VMEM((OWN, BLOCK), jnp.float32)],
        compiler_params=PARAMS,
        cost_estimate=cost(1),
        name="finish",
    )(place, mine, other, back)


def shards(embeddings, labels, holder):
    count = lax.axis_size("shard")
    block_count = count * OWN
    place = jnp.stack([lax.axis_index("shard"), lax.axis_index("rep")]).astype(jnp.int32)
    listing = holder.reshape(-1)
    labels = pltpu.with_memory_space_constraint(labels.reshape(-1, 128), pltpu.HBM)
    embeddings = pltpu.with_memory_space_constraint(embeddings, pltpu.HBM)
    across = [(s, s + 1) for s in range(1, count - 1, 2)]
    across = across + [(b, a) for a, b in across]
    within = [(s, s ^ 1) for s in range(count)]

    def in_vmem(array):
        return pltpu.with_memory_space_constraint(array, pltpu.VMEM)

    far_out = far_rows(place, listing, embeddings)
    far_in = in_vmem(lax.ppermute(far_out, "shard", across))
    units, chip_out, best, stats, tasks = own_rows(
        block_count, place, listing, labels, far_out, embeddings
    )
    chip_in = in_vmem(lax.ppermute(chip_out, "shard", within))

    mine, far_list, chip_list = pair_call(
        functools.partial(own_kernel, block_count), "own_pairs", cost(3), (BEST, LIST, LIST),
        4, OWN_SCRATCH, (place, listing, stats, tasks, best, units),
    )
    mine, found = pair_call(
        functools.partial(far_kernel, block_count), "far_pairs", cost(4, 10**11),
        (BEST, RETURNED), 2, EDGE_SCRATCH, (place, far_list, mine, units, far_in),
    )
    returned, other = pair_call(
        functools.partial(bridge_kernel, block_count), "bridge_pairs", cost(1),
        (RETURNED, BEST), 3, [], (place, far_list, stats, found, far_in, chip_in),
    )
    back = lax.ppermute(returned, "shard", across)
    mine, other = pair_call(
        functools.partial(chip_kernel, block_count), "chip_pairs", cost(4), (BEST, BEST),
        2, EDGE_SCRATCH, (place, chip_list, mine, other, units, chip_in),
    )
    outgoing = finish(block_count, place, mine, other, back)
    groups = [list(range(c * 2 * REPS, (c + 1) * 2 * REPS)) for c in range(count // 2)]
    parts = lax.all_to_all(outgoing, ("shard", "rep"), 0, 0, axis_index_groups=groups)
    return jnp.max(parts, axis=0).reshape(OWN * BLOCK)


def solution(mesh):
    return jax.shard_map(
        shards,
        mesh=mesh,
        in_specs=(P("shard", None), P(), P("shard", None)),
        out_specs=P("shard"),
        check_vma=False,
    )
```

```python
import functools

import jax
import jax.numpy as jnp
from jax import lax
from jax.experimental import pallas as pl
from jax.experimental.pallas import tpu as pltpu
from jax.sharding import PartitionSpec as P

BLOCK = 256
SPANS = 17
WIDTH = 1024
OWN = 12
REPS = 4
MOVED = 8
NEAR = 4
CHIP_SLOTS = 2 + NEAR - 1
FAR_SLOTS = 2
TAIL = 16
FAR_ROWS = FAR_SLOTS * BLOCK + TAIL
CHIP_ROWS = CHIP_SLOTS * BLOCK + TAIL
WINDOW = OWN + 2 * (SPANS - 1)
GROUP = 8 * 128 // BLOCK
CHUNK = 128
WIDE, NARROW = 8, 4
FIELDS = 9
EPS = 1e-6
VMEM_LIMIT = 20 * 1024 * 1024

HBM = pl.BlockSpec(memory_space=pltpu.HBM)
ANY = pl.BlockSpec(memory_space=pl.ANY)
SMEM = pl.BlockSpec(memory_space=pltpu.SMEM)
VMEM = pl.BlockSpec(memory_space=pltpu.VMEM)


def cost(us, flops=0):
    return pl.CostEstimate(flops=flops, bytes_accessed=us * 3_000_000, transcendentals=0)


PARAMS = pltpu.CompilerParams(vmem_limit_bytes=VMEM_LIMIT)


def rows_of(slot, count=BLOCK):
    return pl.ds(pl.multiple_of(slot * BLOCK, BLOCK), count)


def unit_rows(rows):
    squares = jnp.sum(rows * rows, axis=1, keepdims=True)
    return (rows * lax.rsqrt(squares + EPS)).astype(jnp.bfloat16)


def normalise(raw, raw_slot, out, out_slot):
    for step in range(BLOCK // CHUNK):
        source = pl.ds(pl.multiple_of(raw_slot * BLOCK + step * CHUNK, CHUNK), CHUNK)
        target = pl.ds(pl.multiple_of(out_slot * BLOCK + step * CHUNK, CHUNK), CHUNK)
        out[target, :] = unit_rows(raw[source, :])


def far_local(core, m):
    return jnp.where(core == 0, m - 1, OWN - m)


def chip_local(core, m):
    return jnp.where(core == 0, OWN - m, m - 1)


def far_index(rep, slot):
    return jnp.where(slot == 0, rep + 1, MOVED - rep)


def chip_index(rep, slot):
    if slot < 2:
        return far_index(rep, slot)
    return slot - 1 + (slot - 1 > rep).astype(jnp.int32)


def flag_rows(holder, locals_of_slots):
    lane = lax.broadcasted_iota(jnp.int32, (TAIL, 128), 1)
    row = lax.broadcasted_iota(jnp.int32, (TAIL, 128), 0)
    flags = jnp.zeros((TAIL, 128), jnp.float32)
    for slot, local in enumerate(locals_of_slots):
        for k in range(SPANS):
            listed = jnp.where(holder[local * SPANS + k] != REPS, 1.0, 0.0)
            flags = jnp.where((row == slot) & (lane == k), listed, flags)
    return flags.astype(jnp.bfloat16)


def far_rows_kernel(place, holder_hbm, emb, far_out, raw, holder, sems, holder_sem):
    core, rep = place[0] % 2, place[1]
    local = [far_local(core, far_index(rep, slot)) for slot in range(FAR_SLOTS)]
    listing = pltpu.make_async_copy(holder_hbm, holder, holder_sem)
    listing.start()
    fetches = []
    for slot in range(FAR_SLOTS):
        for step in range(BLOCK // CHUNK):
            source = pl.ds(pl.multiple_of(local[slot] * BLOCK + step * CHUNK, CHUNK), CHUNK)
            part = pl.ds(slot * BLOCK + step * CHUNK, CHUNK)
            sem = sems.at[len(fetches)]
            fetches.append((part, pltpu.make_async_copy(emb.at[source], raw.at[part], sem)))
    for _, fetch in fetches:
        fetch.start()
    far_out[FAR_SLOTS * BLOCK :, :] = jnp.zeros((TAIL, WIDTH), jnp.bfloat16)
    for part, fetch in fetches:
        fetch.wait()
        far_out[part, :] = unit_rows(raw[part, :])
    listing.wait()
    far_out[pl.ds(FAR_SLOTS * BLOCK, TAIL), 0:128] = flag_rows(holder, local)


def far_rows(place, holder, emb):
    return pl.pallas_call(
        far_rows_kernel,
        out_shape=pltpu.VMEM((FAR_ROWS, WIDTH), jnp.bfloat16),
        in_specs=[SMEM, HBM, HBM],
        out_specs=VMEM,
        scratch_shapes=[
            pltpu.VMEM((FAR_SLOTS * BLOCK, WIDTH), jnp.float32),
            pltpu.SMEM(holder.shape, jnp.int32),
            pltpu.SemaphoreType.DMA((FAR_SLOTS * BLOCK // CHUNK,)),
            pltpu.SemaphoreType.DMA,
        ],
        compiler_params=PARAMS,
        cost_estimate=cost(1),
        name="far_rows",
    )(place, pltpu.with_memory_space_constraint(holder, pltpu.HBM), emb)


def similarity(left, right):
    return lax.dot_general(
        left, right, (((1,), (1,)), ((), ())), preferred_element_type=jnp.float32
    )


def inside(scored, row_low, row_end, col_low, col_end):
    rows = lax.broadcasted_iota(jnp.int32, (BLOCK, BLOCK), 0)
    cols = lax.broadcasted_iota(jnp.int32, (BLOCK, BLOCK), 1)
    keep = (rows >= row_low) & (rows < row_end) & (cols >= col_low) & (cols < col_end)
    return jnp.where(keep, scored, -1.0)


def fold_rows(scored):
    return jnp.maximum(scored[:, 0:128], scored[:, 128:256])


def fold_cols(scored):
    return jnp.max(scored.reshape(BLOCK // 8, 8, BLOCK), axis=0)


def as_lanes(column):
    rows = lax.broadcasted_iota(jnp.int32, (BLOCK, BLOCK), 0)
    cols = lax.broadcasted_iota(jnp.int32, (BLOCK, BLOCK), 1)
    return jnp.max(jnp.where(rows == cols, column, -1.0), axis=0, keepdims=True)


def first_group(shard, block_count):
    own = OWN // GROUP
    return jnp.clip(
        shard * own - (SPANS - 1) // GROUP, 0, (block_count - WINDOW) // GROUP
    )


def label_stats(stats, block_count, shard, block):
    slot = jnp.clip(block - first_group(shard, block_count) * GROUP, 0, WINDOW - 1)
    return [stats[part, slot] for part in range(4)]


def write_stats(tags, table):
    halves = [tags[pl.ds(half, WINDOW, stride=2), :].astype(jnp.float32) for half in range(2)]
    first, last = halves[0][:, 0:1], halves[1][:, 127:128]
    of_first = sum(jnp.where(half == first, 1.0, 0.0) for half in halves)
    before_last = sum(jnp.where(half < last, 1.0, 0.0) for half in halves)
    columns = [
        first,
        last,
        jnp.sum(of_first, axis=1, keepdims=True),
        jnp.sum(before_last, axis=1, keepdims=True),
    ]
    lane = lax.broadcasted_iota(jnp.int32, (WINDOW, 128), 1)
    spread = jnp.zeros((WINDOW, 128), jnp.float32)
    for part, column in enumerate(columns):
        spread = jnp.where(lane == part, column, spread)
    spread = jnp.concatenate([spread, jnp.zeros((128 - WINDOW, 128), jnp.float32)], axis=0)
    table[...] = spread.T[0:8, :].astype(jnp.int32)


def put_task(tasks, count, active, *fields):
    for place, field in enumerate(fields):
        tasks[count * FIELDS + place] = field
    return count + active.astype(jnp.int32)


def pad_tasks(tasks, count):
    for extra in range(WIDE - 1):
        for field in range(FIELDS):
            tasks[(count + extra) * FIELDS + field] = 0


def run_tasks(tasks, count, left, right, row_acc, col_acc):

    def run(first, width):
        found = []
        for lane in range(width):
            base = (first + lane) * FIELDS
            task = [tasks[base + field] for field in range(FIELDS)]
            scored = similarity(left[rows_of(task[0]), :], right[rows_of(task[1]), :])
            scored = inside(scored, *task[2:6])
            found.append((task[6], task[7], fold_rows(scored), fold_cols(scored)))
        for row_slot, col_slot, rows, cols in found:
            row_acc[row_slot] = jnp.maximum(row_acc[row_slot], rows)
            col_acc[col_slot] = jnp.maximum(col_acc[col_slot], cols)

    steps = (count + WIDE - NARROW - 1) // WIDE

    @pl.loop(0, steps)
    def _(step):
        run(step * WIDE, WIDE)

    @pl.when(count > steps * WIDE)
    def _():
        run(steps * WIDE, NARROW)


def task_words(most):
    return (most + WIDE) * FIELDS


OWN_TASKS = task_words(OWN * (OWN - 1) // 2)
EDGE_TASKS = task_words(2 * OWN)


def local_class(rep, turn):
    return (rep, 7 - rep, 8 + rep)[turn]


def rows_kernel(
    block_count, place, holder, labels, far, emb,
    units, chip_out, best, stats,
    raw, tags, sems, tag_sem,
):
    shard, rep = place[0], place[1]
    core = lax.rem(shard, 2)
    group = first_group(shard, block_count)
    sent = [far_local(core, far_index(rep, slot)) for slot in range(FAR_SLOTS)]
    local = [chip_local(core, chip_index(rep, slot)) for slot in range(CHIP_SLOTS)]

    def fetch(block):
        return pltpu.make_async_copy(
            emb.at[rows_of(block)], raw.at[rows_of(block)], sems.at[block]
        )

    def is_new(block):
        return (block != sent[0]) & (block != sent[1])

    window = pl.ds(pl.multiple_of(group * 8, 8), WINDOW * 2)
    fetch_tags = pltpu.make_async_copy(labels.at[window], tags, tag_sem)
    fetch_tags.start()

    def request(m):
        block = chip_local(core, m)
        pl.when(is_new(block))(lambda: fetch(block).start())

    pl.loop(1, 5)(request)
    chip_out[CHIP_SLOTS * BLOCK :, :] = jnp.zeros((TAIL, WIDTH), jnp.bfloat16)
    chip_out[CHIP_SLOTS * BLOCK :, 0:128] = flag_rows(holder, local)
    best[...] = jnp.full(best.shape, -1.0, jnp.float32)
    for slot in range(FAR_SLOTS):
        units[rows_of(sent[slot]), :] = far[rows_of(slot), :]
    fetch_tags.wait()
    write_stats(tags, stats)
    pl.loop(5, OWN + 1)(request)

    def diagonal(block):
        at = (shard * OWN + block - group * GROUP) * 2
        tag_row = jnp.concatenate([tags[pl.ds(at, 1), :], tags[pl.ds(at + 1, 1), :]], axis=1)
        tag_row = tag_row.astype(jnp.float32)
        rows = lax.broadcasted_iota(jnp.int32, (BLOCK, BLOCK), 0)
        cols = lax.broadcasted_iota(jnp.int32, (BLOCK, BLOCK), 1)
        spread = jnp.broadcast_to(tag_row, (BLOCK, BLOCK))
        tag_col = jnp.max(jnp.where(rows == cols, spread, -1.0), axis=1, keepdims=True)
        scored = similarity(units[rows_of(block), :], units[rows_of(block), :])
        keep = (tag_col == tag_row) & (rows != cols)
        found = jnp.max(jnp.where(keep, scored, -1.0), axis=0, keepdims=True)
        best[pl.ds(block, 1), :] = jnp.where(holder[block * SPANS] != REPS, found, -1.0)

    def arrive(m):
        block = chip_local(core, m)

        @pl.when(is_new(block))
        def _():
            fetch(block).wait()
            normalise(raw, block, units, block)

        mine = block == local_class(rep, 0)
        for turn in range(1, 3):
            mine = mine | (block == local_class(rep, turn))
        pl.when(mine)(lambda: diagonal(block))

    def arrive_and_send(m):
        arrive(m)
        block = chip_local(core, m)
        for slot in range(CHIP_SLOTS):

            @pl.when(block == local[slot])
            def _(slot=slot):
                chip_out[rows_of(slot), :] = units[rows_of(block), :]

    pl.loop(1, MOVED + 1)(arrive_and_send)
    pl.loop(MOVED + 1, OWN + 1)(arrive)


def own_rows(block_count, place, holder, labels, far, emb):
    return pl.pallas_call(
        functools.partial(rows_kernel, block_count),
        out_shape=(
            pltpu.VMEM((OWN * BLOCK, WIDTH), jnp.bfloat16),
            pltpu.VMEM((CHIP_ROWS, WIDTH), jnp.bfloat16),
            pltpu.VMEM((OWN, BLOCK), jnp.float32),
            pltpu.VMEM((8, 128), jnp.int32),
        ),
        in_specs=[SMEM, SMEM, HBM, VMEM, HBM],
        out_specs=(VMEM, VMEM, VMEM, VMEM),
        scratch_shapes=[
            pltpu.VMEM((OWN * BLOCK, WIDTH), jnp.float32),
            pltpu.VMEM((WINDOW * 2, 128), jnp.int32),
            pltpu.SemaphoreType.DMA((OWN,)),
            pltpu.SemaphoreType.DMA,
        ],
        compiler_params=PARAMS,
        cost_estimate=cost(5),
        name="own_rows",
    )(place, holder, labels, far, emb)


def flag_bits(tail, slot):
    lane = lax.broadcasted_iota(jnp.int32, (TAIL, 128), 1)
    row = lax.broadcasted_iota(jnp.int32, (TAIL, 128), 0)
    weight = lax.shift_left(jnp.int32(1), jnp.minimum(lane, SPANS)).astype(jnp.float32)
    weight = jnp.where((row == slot) & (lane < SPANS), weight, 0.0)
    return jnp.sum(tail[:, 0:128].astype(jnp.float32) * weight).astype(jnp.int32)


def has_bit(bits, offset):
    return lax.rem(lax.shift_right_logical(bits, offset), 2) == 1


class Boundary:
    def __init__(self, far, block_count, place):
        self.far, self.block_count = far, block_count
        self.shard, self.rep = place[0], place[1]
        self.core = lax.rem(self.shard, 2)
        self.side = self.core if far else 1 - self.core

    def local(self, m):
        return far_local(self.core, m) if self.far else chip_local(self.core, m)

    def near(self, which):
        return far_index(self.rep, which) if self.far else chip_index(self.rep, which)

    def start(self, stats, which):
        first_block = self.shard * OWN
        near = self.near(which)
        before = self.side == 0
        block = jnp.where(before, first_block - near, first_block + OWN - 1 + near)
        facts = label_stats(stats, self.block_count, self.shard, block)
        present = (block >= 0) & (block < self.block_count)
        return near, before, present, facts

    def shares(self, stats, moved, m):
        _, before, _, (m_first, m_last, _, _) = moved
        c_first, c_last, _, _ = self.column(stats, m)
        return jnp.where(before, m_last == c_first, c_last == m_first)

    def column(self, stats, m):
        first_block = self.shard * OWN
        block = jnp.where(self.side == 0, first_block + m - 1, first_block + OWN - m)
        return label_stats(stats, self.block_count, self.shard, block)

    def area(self, stats, moved, m):
        _, before, _, (_, _, m_count, m_start) = moved
        _, _, c_count, c_start = self.column(stats, m)
        return (
            jnp.where(before, m_start, 0), jnp.where(before, BLOCK, m_count),
            jnp.where(before, 0, c_start), jnp.where(before, c_count, BLOCK),
        )

    def lean(self, stats):
        middle = self.shard * OWN + jnp.where(self.side == 0, 0, OWN)
        facts = functools.partial(label_stats, stats, self.block_count, self.shard)
        label = facts(middle - 1)[1]
        ahead = lax.while_loop(
            lambda n: (n < jnp.minimum(middle, SPANS - 1)) & (facts(middle - 1 - n)[1] == label),
            lambda n: n + 1,
            jnp.int32(0),
        )
        behind = lax.while_loop(
            lambda n: (n < jnp.minimum(self.block_count - middle, SPANS - 1))
            & (facts(middle + n)[0] == label),
            lambda n: n + 1,
            jnp.int32(0),
        )
        return behind - ahead

    def first_column(self, near, lean):
        half = lax.shift_right_arithmetic(lean, 1)
        even = lean - 2 * half == 0
        behind = near + half + jnp.where(even & (lax.rem(near, 2) == 1), 0, 1)
        equal = near - half
        tie = even & (lax.rem(equal + 32, 2) == 1)
        ahead = equal + jnp.where(tie, 1, 0)
        return jnp.clip(jnp.where(self.side == 0, behind, ahead), 1, MOVED + 1)

    def list_tasks(self, tasks, stats, holder, bits=None):
        count = jnp.int32(0)
        lean = self.lean(stats)
        for which in range(2):
            moved = self.start(stats, which)
            near, before, present, _ = moved
            last = jnp.where(present, jnp.minimum(OWN, SPANS - near), 0)

            def shares(state, moved=moved, last=last):
                m, _ = state
                return (m <= last) & self.shares(stats, moved, m)

            def visit(state, which=which, moved=moved, near=near, before=before):
                m, count = state
                column, offset = self.local(m), near + m - 1
                moved_flag = True if bits is None else has_bit(bits[which], offset)
                column_flag = holder[column * SPANS + offset] != REPS
                listed = (before & moved_flag) | (jnp.logical_not(before) & column_flag)
                area = self.area(stats, moved, m)
                count = put_task(
                    tasks, count, listed, which, column, *area, which, column, offset
                )
                return m + 1, count

            first = self.first_column(near, lean)
            _, count = lax.while_loop(shares, visit, (first, count))
        return count

    def keep_listed(self, found, tasks, bits):
        def visit(index, count):
            task = [found[index * FIELDS + field] for field in range(FIELDS)]
            listed = has_bit(jnp.where(task[0] == 0, bits[0], bits[1]), task[8])
            return put_task(tasks, count, (self.side == 1) | listed, *task)

        count = lax.fori_loop(0, found[EDGE_TASKS], visit, jnp.int32(0))
        pad_tasks(tasks, count)
        return count


def own_kernel(
    block_count, place, holder, stats, best, units, mine, far_list, row_acc, col_acc, tasks
):
    col_acc[...] = jnp.full(col_acc.shape, -1.0, jnp.float32)
    row_acc[...] = jnp.full(row_acc.shape, -1.0, jnp.float32)
    shard, rep = place[0], place[1]

    def label_facts(block):
        return label_stats(stats, block_count, shard, shard * OWN + block)

    count = jnp.int32(0)
    for turn in range(3):
        block = local_class(rep, turn)
        b_first, _, b_count, _ = label_facts(block)

        def shares(state, b_first=b_first):
            other, _ = state
            return (other >= 0) & (label_facts(jnp.maximum(other, 0))[1] == b_first)

        def visit(state, block=block, turn=turn, b_count=b_count):
            other, count = state
            listed = holder[other * SPANS + (block - other)] != REPS
            a_start = label_facts(other)[3]
            count = put_task(
                tasks, count, listed, block, other, 0, b_count, a_start, BLOCK, turn, other,
                block - other,
            )
            return other - 1, count

        _, count = lax.while_loop(shares, visit, (block - 1, count))
    pad_tasks(tasks, count)
    run_tasks(tasks, count, units, units, row_acc, col_acc)
    mine[...] = jnp.maximum(best[...], jnp.max(col_acc[...], axis=1))
    for turn in range(3):
        here = (pl.ds(local_class(place[1], turn), 1), slice(None))
        found = as_lanes(jnp.max(row_acc[turn], axis=1, keepdims=True))
        mine[here] = jnp.maximum(mine[here], found)
    edge = Boundary(True, block_count, place)
    far_list[EDGE_TASKS] = edge.list_tasks(far_list, stats, holder)
    moved = edge.start(stats, 0)
    bridged = moved[2] & edge.shares(stats, moved, OWN + 1)
    far_list[EDGE_TASKS + 1] = bridged.astype(jnp.int32)


def far_kernel(
    block_count, place, far_list, best, units, far, mine, returned, row_acc, col_acc, tasks
):
    edge = Boundary(True, block_count, place)
    col_acc[...] = jnp.full(col_acc.shape, -1.0, jnp.float32)
    row_acc[...] = jnp.full(row_acc.shape, -1.0, jnp.float32)
    tail = far[pl.ds(FAR_SLOTS * BLOCK, TAIL), :]
    bits = [flag_bits(tail, slot) for slot in range(2)]
    count = edge.keep_listed(far_list, tasks, bits)
    run_tasks(tasks, count, far, units, row_acc, col_acc)
    mine[...] = jnp.maximum(best[...], jnp.max(col_acc[...], axis=1))
    for which in range(2):
        returned[which : which + 1, :] = as_lanes(
            jnp.max(row_acc[which], axis=1, keepdims=True)
        )


def bridge_kernel(block_count, place, far_list, stats, found_in, far, chip, returned, other):
    returned[...] = found_in[...]
    other[...] = jnp.full(other.shape, -1.0, jnp.float32)

    @pl.when(far_list[EDGE_TASKS + 1] > 0)
    def _():
        edge = Boundary(True, block_count, place)
        far_bits = flag_bits(far[pl.ds(FAR_SLOTS * BLOCK, TAIL), :], 0)
        tail = chip[pl.ds(CHIP_SLOTS * BLOCK, TAIL), :]
        moved = edge.start(stats, 0)
        rows, cols = [], []
        slots = (0, 2, 3, 4)
        for slot in slots:
            m = OWN + chip_index(edge.rep, slot)
            offset, area = moved[0] + m - 1, edge.area(stats, moved, m)
            active = moved[2] & (offset < SPANS) & edge.shares(stats, moved, m)
            offset = jnp.minimum(offset, SPANS - 1)
            bits = jnp.where(edge.side == 0, far_bits, flag_bits(tail, slot))
            listed = has_bit(bits, offset)
            scored = inside(similarity(far[0:BLOCK, :], chip[rows_of(slot), :]), *area)
            scored = jnp.where(active & listed, scored, -1.0)
            rows.append(fold_rows(scored))
            cols.append(fold_cols(scored))
        for slot, found in zip(slots, cols):
            block = chip_local(1 - edge.core, chip_index(edge.rep, slot))
            other[pl.ds(block, 1), :] = jnp.max(found, axis=0, keepdims=True)
        best = functools.reduce(jnp.maximum, rows)
        best = as_lanes(jnp.max(best, axis=1, keepdims=True))
        returned[0:1, :] = jnp.maximum(returned[0:1, :], best)


def chip_kernel(
    block_count, place, holder, stats, mine_in, other_in, units, chip,
    mine, other, row_acc, col_acc, tasks,
):
    edge = Boundary(False, block_count, place)
    col_acc[...] = jnp.full(col_acc.shape, -1.0, jnp.float32)
    row_acc[...] = jnp.full(row_acc.shape, -1.0, jnp.float32)
    tail = chip[pl.ds(CHIP_SLOTS * BLOCK, TAIL), :]
    bits = [flag_bits(tail, slot) for slot in range(2)]
    count = edge.list_tasks(tasks, stats, holder, bits)
    pad_tasks(tasks, count)
    run_tasks(tasks, count, chip, units, row_acc, col_acc)
    mine[...] = jnp.maximum(mine_in[...], jnp.max(col_acc[...], axis=1))
    other[...] = other_in[...]
    for which in range(2):
        here = (pl.ds(chip_local(1 - edge.core, edge.near(which)), 1), slice(None))
        found = as_lanes(jnp.max(row_acc[which], axis=1, keepdims=True))
        other[here] = jnp.maximum(other[here], found)


BEST = pltpu.VMEM((OWN, BLOCK), jnp.float32)
LIST = jax.ShapeDtypeStruct((EDGE_TASKS + 2,), jnp.int32)
RETURNED = pltpu.VMEM((2, BLOCK), jnp.float32)


def pair_call(kernel, name, estimate, outs, scalars, scratch, args):
    return pl.pallas_call(
        kernel,
        out_shape=outs,
        in_specs=[SMEM] * scalars + [VMEM] * (len(args) - scalars),
        out_specs=tuple(SMEM if out is LIST else VMEM for out in outs),
        scratch_shapes=scratch,
        compiler_params=PARAMS,
        cost_estimate=estimate,
        name=name,
    )(*args)


OWN_SCRATCH = [
    pltpu.VMEM((3, BLOCK, 128), jnp.float32),
    pltpu.VMEM((OWN, 8, BLOCK), jnp.float32),
    pltpu.SMEM((OWN_TASKS,), jnp.int32),
]
EDGE_SCRATCH = [
    pltpu.VMEM((2, BLOCK, 128), jnp.float32),
    pltpu.VMEM((OWN, 8, BLOCK), jnp.float32),
    pltpu.SMEM((EDGE_TASKS,), jnp.int32),
]


def finish_kernel(block_count, place, mine, other, back, outgoing, merged):
    shard, rep = place[0], place[1]
    core = lax.rem(shard, 2)
    has_far = (shard > 0) & (shard < block_count // OWN - 1)
    merged[...] = mine[...]
    for which in range(2):
        here = (pl.ds(far_local(core, far_index(rep, which)), 1), slice(None))
        found = jnp.where(has_far, back[which : which + 1, :], -1.0)
        merged[here] = jnp.maximum(merged[here], found)
    for target in range(2):
        share = jnp.where(core == target, merged[...], other[...])
        for copy in range(REPS):
            at = target * REPS + copy
            outgoing[at, pl.ds(0, OWN, stride=2), :] = share[:, 0:128]
            outgoing[at, pl.ds(1, OWN, stride=2), :] = share[:, 128:256]


def finish(block_count, place, mine, other, back):
    return pl.pallas_call(
        functools.partial(finish_kernel, block_count),
        out_shape=jax.ShapeDtypeStruct((2 * REPS, OWN * 2, 128), jnp.float32),
        in_specs=[SMEM, VMEM, VMEM, VMEM],
        out_specs=VMEM,
        scratch_shapes=[pltpu.VMEM((OWN, BLOCK), jnp.float32)],
        compiler_params=PARAMS,
        cost_estimate=cost(1),
        name="finish",
    )(place, mine, other, back)


def shards(embeddings, labels, holder):
    count = lax.axis_size("shard")
    block_count = count * OWN
    place = jnp.stack([lax.axis_index("shard"), lax.axis_index("rep")]).astype(jnp.int32)
    listing = holder.reshape(-1)
    labels = pltpu.with_memory_space_constraint(labels.reshape(-1, 128), pltpu.HBM)
    embeddings = pltpu.with_memory_space_constraint(embeddings, pltpu.HBM)
    across = [(s, s + 1) for s in range(1, count - 1, 2)]
    across = across + [(b, a) for a, b in across]
    within = [(s, s ^ 1) for s in range(count)]

    def in_vmem(array):
        return pltpu.with_memory_space_constraint(array, pltpu.VMEM)

    far_out = far_rows(place, listing, embeddings)
    far_in = in_vmem(lax.ppermute(far_out, "shard", across))
    units, chip_out, best, stats = own_rows(
        block_count, place, listing, labels, far_out, embeddings
    )
    chip_in = in_vmem(lax.ppermute(chip_out, "shard", within))

    mine, far_list = pair_call(
        functools.partial(own_kernel, block_count), "own_pairs", cost(3), (BEST, LIST),
        3, OWN_SCRATCH, (place, listing, stats, best, units),
    )
    mine, found = pair_call(
        functools.partial(far_kernel, block_count), "far_pairs", cost(4, 10**11),
        (BEST, RETURNED), 2, EDGE_SCRATCH, (place, far_list, mine, units, far_in),
    )
    returned, other = pair_call(
        functools.partial(bridge_kernel, block_count), "bridge_pairs", cost(1),
        (RETURNED, BEST), 3, [], (place, far_list, stats, found, far_in, chip_in),
    )
    back = lax.ppermute(returned, "shard", across)
    mine, other = pair_call(
        functools.partial(chip_kernel, block_count), "chip_pairs", cost(4), (BEST, BEST),
        3, EDGE_SCRATCH, (place, listing, stats, mine, other, units, chip_in),
    )
    outgoing = finish(block_count, place, mine, other, back)
    groups = [list(range(c * 2 * REPS, (c + 1) * 2 * REPS)) for c in range(count // 2)]
    parts = lax.all_to_all(outgoing, ("shard", "rep"), 0, 0, axis_index_groups=groups)
    return jnp.max(parts, axis=0).reshape(OWN * BLOCK)


def solution(mesh):
    return jax.shard_map(
        shards,
        mesh=mesh,
        in_specs=(P("shard", None), P(), P("shard", None)),
        out_specs=P("shard"),
        check_vma=False,
    )
```

```python
import functools

import jax
import jax.numpy as jnp
from jax import lax
from jax.experimental import pallas as pl
from jax.experimental.pallas import tpu as pltpu
from jax.sharding import PartitionSpec as P

BLOCK = 256
SPANS = 17
WIDTH = 1024
OWN = 12
REPS = 4
MOVED = 8
ROW = 16
NEAR = 4
CHIP_SLOTS = 2 + NEAR - 1
FAR_SLOTS = 2
TAIL = 16
FAR_ROWS = FAR_SLOTS * BLOCK + TAIL
CHIP_ROWS = CHIP_SLOTS * BLOCK + TAIL
WINDOW = OWN + 2 * (SPANS - 1)
GROUP = 8 * 128 // BLOCK
CHUNK = 128
WIDE, NARROW = 8, 4
FIELDS = 9
EPS = 1e-6
VMEM_LIMIT = 20 * 1024 * 1024

HBM = pl.BlockSpec(memory_space=pltpu.HBM)
ANY = pl.BlockSpec(memory_space=pl.ANY)
SMEM = pl.BlockSpec(memory_space=pltpu.SMEM)
VMEM = pl.BlockSpec(memory_space=pltpu.VMEM)


def cost(us, flops=0):
    return pl.CostEstimate(flops=flops, bytes_accessed=us * 3_000_000, transcendentals=0)


PARAMS = pltpu.CompilerParams(vmem_limit_bytes=VMEM_LIMIT)


def rows_of(slot, count=BLOCK):
    return pl.ds(pl.multiple_of(slot * BLOCK, BLOCK), count)


def unit_rows(rows):
    squares = jnp.sum(rows * rows, axis=1, keepdims=True)
    return (rows * lax.rsqrt(squares + EPS)).astype(jnp.bfloat16)


def normalise(raw, raw_slot, out, out_slot):
    for step in range(BLOCK // CHUNK):
        source = pl.ds(pl.multiple_of(raw_slot * BLOCK + step * CHUNK, CHUNK), CHUNK)
        target = pl.ds(pl.multiple_of(out_slot * BLOCK + step * CHUNK, CHUNK), CHUNK)
        out[target, :] = unit_rows(raw[source, :])


def far_local(core, m):
    return jnp.where(core == 0, m - 1, OWN - m)


def chip_local(core, m):
    return jnp.where(core == 0, OWN - m, m - 1)


def far_index(rep, slot):
    return jnp.where(slot == 0, rep + 1, MOVED - rep)


def chip_index(rep, slot):
    if slot < 2:
        return far_index(rep, slot)
    return slot - 1 + (slot - 1 > rep).astype(jnp.int32)


def flag_rows(holder, locals_of_slots):
    lane = lax.broadcasted_iota(jnp.int32, (TAIL, 128), 1)
    row = lax.broadcasted_iota(jnp.int32, (TAIL, 128), 0)
    flags = jnp.zeros((TAIL, 128), jnp.float32)
    for slot, local in enumerate(locals_of_slots):
        for k in range(SPANS):
            listed = jnp.where(holder[local * SPANS + k] != REPS, 1.0, 0.0)
            flags = jnp.where((row == slot) & (lane == k), listed, flags)
    return flags.astype(jnp.bfloat16)


def far_rows_kernel(place, holder_hbm, emb, far_out, raw, holder, sems, holder_sem):
    core, rep = place[0] % 2, place[1]
    local = [far_local(core, far_index(rep, slot)) for slot in range(FAR_SLOTS)]
    listing = pltpu.make_async_copy(holder_hbm, holder, holder_sem)
    listing.start()
    fetches = []
    for slot in range(FAR_SLOTS):
        for step in range(BLOCK // CHUNK):
            source = pl.ds(pl.multiple_of(local[slot] * BLOCK + step * CHUNK, CHUNK), CHUNK)
            part = pl.ds(slot * BLOCK + step * CHUNK, CHUNK)
            sem = sems.at[len(fetches)]
            fetches.append((part, pltpu.make_async_copy(emb.at[source], raw.at[part], sem)))
    for _, fetch in fetches:
        fetch.start()
    far_out[FAR_SLOTS * BLOCK :, :] = jnp.zeros((TAIL, WIDTH), jnp.bfloat16)
    for part, fetch in fetches:
        fetch.wait()
        far_out[part, :] = unit_rows(raw[part, :])
    listing.wait()
    far_out[pl.ds(FAR_SLOTS * BLOCK, TAIL), 0:128] = flag_rows(holder, local)


def far_rows(place, holder, emb):
    return pl.pallas_call(
        far_rows_kernel,
        out_shape=pltpu.VMEM((FAR_ROWS, WIDTH), jnp.bfloat16),
        in_specs=[SMEM, HBM, HBM],
        out_specs=VMEM,
        scratch_shapes=[
            pltpu.VMEM((FAR_SLOTS * BLOCK, WIDTH), jnp.float32),
            pltpu.SMEM(holder.shape, jnp.int32),
            pltpu.SemaphoreType.DMA((FAR_SLOTS * BLOCK // CHUNK,)),
            pltpu.SemaphoreType.DMA,
        ],
        compiler_params=PARAMS,
        cost_estimate=cost(1),
        name="far_rows",
    )(place, pltpu.with_memory_space_constraint(holder, pltpu.HBM), emb)


def similarity(left, right):
    return lax.dot_general(
        left, right, (((1,), (1,)), ((), ())), preferred_element_type=jnp.float32
    )


def inside(scored, row_low, row_end, col_low, col_end):
    rows = lax.broadcasted_iota(jnp.int32, (BLOCK, BLOCK), 0)
    cols = lax.broadcasted_iota(jnp.int32, (BLOCK, BLOCK), 1)
    keep = (rows >= row_low) & (rows < row_end) & (cols >= col_low) & (cols < col_end)
    return jnp.where(keep, scored, -1.0)


def fold_rows(scored):
    return jnp.maximum(scored[:, 0:128], scored[:, 128:256])


def fold_cols(scored):
    return jnp.max(scored.reshape(BLOCK // 8, 8, BLOCK), axis=0)


def as_lanes(column):
    rows = lax.broadcasted_iota(jnp.int32, (BLOCK, BLOCK), 0)
    cols = lax.broadcasted_iota(jnp.int32, (BLOCK, BLOCK), 1)
    return jnp.max(jnp.where(rows == cols, column, -1.0), axis=0, keepdims=True)


def first_group(shard, block_count):
    own = OWN // GROUP
    return jnp.clip(
        shard * own - (SPANS - 1) // GROUP, 0, (block_count - WINDOW) // GROUP
    )


def label_stats(stats, block_count, shard, block):
    slot = jnp.clip(block - first_group(shard, block_count) * GROUP, 0, WINDOW - 1)
    return [stats[part, slot] for part in range(4)]


def write_stats(tags, table):
    halves = [tags[pl.ds(half, WINDOW, stride=2), :].astype(jnp.float32) for half in range(2)]
    first, last = halves[0][:, 0:1], halves[1][:, 127:128]
    of_first = sum(jnp.where(half == first, 1.0, 0.0) for half in halves)
    before_last = sum(jnp.where(half < last, 1.0, 0.0) for half in halves)
    columns = [
        first,
        last,
        jnp.sum(of_first, axis=1, keepdims=True),
        jnp.sum(before_last, axis=1, keepdims=True),
    ]
    lane = lax.broadcasted_iota(jnp.int32, (WINDOW, 128), 1)
    spread = jnp.zeros((WINDOW, 128), jnp.float32)
    for part, column in enumerate(columns):
        spread = jnp.where(lane == part, column, spread)
    spread = jnp.concatenate([spread, jnp.zeros((128 - WINDOW, 128), jnp.float32)], axis=0)
    table[...] = spread.T[0:8, :].astype(jnp.int32)


def put_task(tasks, count, active, *fields):
    for place, field in enumerate(fields):
        tasks[count * FIELDS + place] = field
    return count + active.astype(jnp.int32)


def pad_tasks(tasks, count):
    for extra in range(WIDE - 1):
        for field in range(FIELDS):
            tasks[(count + extra) * FIELDS + field] = 0


def run_tasks(tasks, count, left, right, row_acc, col_acc):

    def run(first, width):
        found = []
        for lane in range(width):
            base = (first + lane) * FIELDS
            task = [tasks[base + field] for field in range(FIELDS)]
            scored = similarity(left[rows_of(task[0]), :], right[rows_of(task[1]), :])
            scored = inside(scored, *task[2:6])
            found.append((task[6], task[7], fold_rows(scored), fold_cols(scored)))
        for row_slot, col_slot, rows, cols in found:
            row_acc[row_slot] = jnp.maximum(row_acc[row_slot], rows)
            col_acc[col_slot] = jnp.maximum(col_acc[col_slot], cols)

    steps = (count + WIDE - NARROW - 1) // WIDE

    @pl.loop(0, steps)
    def _(step):
        run(step * WIDE, WIDE)

    @pl.when(count > steps * WIDE)
    def _():
        run(steps * WIDE, NARROW)


def task_words(most):
    return (most + WIDE) * FIELDS


OWN_TASKS = task_words(OWN * (OWN - 1) // 2)
EDGE_TASKS = task_words(2 * OWN)


def local_class(rep, turn):
    return (rep, 7 - rep, 8 + rep)[turn]


def rows_kernel(
    block_count, place, holder, labels, far, emb,
    units, chip_out, best, stats,
    raw, tags, sems, tag_sem,
):
    shard, rep = place[0], place[1]
    core = lax.rem(shard, 2)
    group = first_group(shard, block_count)
    sent = [far_local(core, far_index(rep, slot)) for slot in range(FAR_SLOTS)]
    local = [chip_local(core, chip_index(rep, slot)) for slot in range(CHIP_SLOTS)]

    def fetch(block):
        return pltpu.make_async_copy(
            emb.at[rows_of(block)], raw.at[rows_of(block)], sems.at[block]
        )

    def is_new(block):
        return (block != sent[0]) & (block != sent[1])

    window = pl.ds(pl.multiple_of(group * 8, 8), WINDOW * 2)
    fetch_tags = pltpu.make_async_copy(labels.at[window], tags, tag_sem)
    fetch_tags.start()

    def request(m):
        block = chip_local(core, m)
        pl.when(is_new(block))(lambda: fetch(block).start())

    pl.loop(1, 5)(request)
    chip_out[CHIP_SLOTS * BLOCK :, :] = jnp.zeros((TAIL, WIDTH), jnp.bfloat16)
    chip_out[CHIP_SLOTS * BLOCK :, 0:128] = flag_rows(holder, local)
    best[...] = jnp.full(best.shape, -1.0, jnp.float32)
    for slot in range(FAR_SLOTS):
        units[rows_of(sent[slot]), :] = far[rows_of(slot), :]
    fetch_tags.wait()
    write_stats(tags, stats)
    pl.loop(5, OWN + 1)(request)

    def diagonal(block):
        at = (shard * OWN + block - group * GROUP) * 2
        tag_row = jnp.concatenate([tags[pl.ds(at, 1), :], tags[pl.ds(at + 1, 1), :]], axis=1)
        tag_row = tag_row.astype(jnp.float32)
        rows = lax.broadcasted_iota(jnp.int32, (BLOCK, BLOCK), 0)
        cols = lax.broadcasted_iota(jnp.int32, (BLOCK, BLOCK), 1)
        spread = jnp.broadcast_to(tag_row, (BLOCK, BLOCK))
        tag_col = jnp.max(jnp.where(rows == cols, spread, -1.0), axis=1, keepdims=True)
        scored = similarity(units[rows_of(block), :], units[rows_of(block), :])
        keep = (tag_col == tag_row) & (rows != cols)
        found = jnp.max(jnp.where(keep, scored, -1.0), axis=0, keepdims=True)
        best[pl.ds(block, 1), :] = jnp.where(holder[block * SPANS] != REPS, found, -1.0)

    def arrive(m):
        block = chip_local(core, m)

        @pl.when(is_new(block))
        def _():
            fetch(block).wait()
            normalise(raw, block, units, block)

        mine = block == local_class(rep, 0)
        for turn in range(1, 3):
            mine = mine | (block == local_class(rep, turn))
        pl.when(mine)(lambda: diagonal(block))

    def arrive_and_send(m):
        arrive(m)
        block = chip_local(core, m)
        for slot in range(CHIP_SLOTS):

            @pl.when(block == local[slot])
            def _(slot=slot):
                chip_out[rows_of(slot), :] = units[rows_of(block), :]

    pl.loop(1, MOVED + 1)(arrive_and_send)
    pl.loop(MOVED + 1, OWN + 1)(arrive)


def own_rows(block_count, place, holder, labels, far, emb):
    return pl.pallas_call(
        functools.partial(rows_kernel, block_count),
        out_shape=(
            pltpu.VMEM((OWN * BLOCK, WIDTH), jnp.bfloat16),
            pltpu.VMEM((CHIP_ROWS, WIDTH), jnp.bfloat16),
            pltpu.VMEM((OWN, BLOCK), jnp.float32),
            pltpu.VMEM((8, 128), jnp.int32),
        ),
        in_specs=[SMEM, SMEM, HBM, VMEM, HBM],
        out_specs=(VMEM, VMEM, VMEM, VMEM),
        scratch_shapes=[
            pltpu.VMEM((OWN * BLOCK, WIDTH), jnp.float32),
            pltpu.VMEM((WINDOW * 2, 128), jnp.int32),
            pltpu.SemaphoreType.DMA((OWN,)),
            pltpu.SemaphoreType.DMA,
        ],
        compiler_params=PARAMS,
        cost_estimate=cost(5),
        name="own_rows",
    )(place, holder, labels, far, emb)


def flag_bits(tail, slot):
    lane = lax.broadcasted_iota(jnp.int32, (TAIL, 128), 1)
    row = lax.broadcasted_iota(jnp.int32, (TAIL, 128), 0)
    weight = lax.shift_left(jnp.int32(1), jnp.minimum(lane, SPANS)).astype(jnp.float32)
    weight = jnp.where((row == slot) & (lane < SPANS), weight, 0.0)
    return jnp.sum(tail[:, 0:128].astype(jnp.float32) * weight).astype(jnp.int32)


def has_bit(bits, offset):
    return lax.rem(lax.shift_right_logical(bits, offset), 2) == 1


class Boundary:
    def __init__(self, far, block_count, place):
        self.far, self.block_count = far, block_count
        self.shard, self.rep = place[0], place[1]
        self.core = lax.rem(self.shard, 2)
        self.side = self.core if far else 1 - self.core

    def local(self, m):
        return far_local(self.core, m) if self.far else chip_local(self.core, m)

    def near(self, which):
        return far_index(self.rep, which) if self.far else chip_index(self.rep, which)

    def start(self, stats, which):
        first_block = self.shard * OWN
        near = self.near(which)
        before = self.side == 0
        block = jnp.where(before, first_block - near, first_block + OWN - 1 + near)
        facts = label_stats(stats, self.block_count, self.shard, block)
        present = (block >= 0) & (block < self.block_count)
        return near, before, present, facts

    def shares(self, stats, moved, m):
        _, before, _, (m_first, m_last, _, _) = moved
        c_first, c_last, _, _ = self.column(stats, m)
        return jnp.where(before, m_last == c_first, c_last == m_first)

    def column(self, stats, m):
        first_block = self.shard * OWN
        block = jnp.where(self.side == 0, first_block + m - 1, first_block + OWN - m)
        return label_stats(stats, self.block_count, self.shard, block)

    def area(self, stats, moved, m):
        _, before, _, (_, _, m_count, m_start) = moved
        _, _, c_count, c_start = self.column(stats, m)
        return (
            jnp.where(before, m_start, 0), jnp.where(before, BLOCK, m_count),
            jnp.where(before, 0, c_start), jnp.where(before, c_count, BLOCK),
        )

    def lean(self, stats):
        middle = self.shard * OWN + jnp.where(self.side == 0, 0, OWN)
        facts = functools.partial(label_stats, stats, self.block_count, self.shard)
        label = facts(middle - 1)[1]
        ahead = lax.while_loop(
            lambda n: (n < jnp.minimum(middle, SPANS - 1)) & (facts(middle - 1 - n)[1] == label),
            lambda n: n + 1,
            jnp.int32(0),
        )
        behind = lax.while_loop(
            lambda n: (n < jnp.minimum(self.block_count - middle, SPANS - 1))
            & (facts(middle + n)[0] == label),
            lambda n: n + 1,
            jnp.int32(0),
        )
        return behind - ahead

    def first_column(self, near, lean):
        half = lax.shift_right_arithmetic(lean, 1)
        even = lean - 2 * half == 0
        behind = near + half + jnp.where(even & (lax.rem(near, 2) == 1), 0, 1)
        equal = near - half
        tie = even & (lax.rem(equal + 32, 2) == 1)
        ahead = equal + jnp.where(tie, 1, 0)
        return jnp.clip(jnp.where(self.side == 0, behind, ahead), 1, MOVED + 1)

    def list_tasks(self, tasks, stats, holder, bits=None):
        count = jnp.int32(0)
        lean = self.lean(stats)
        for which in range(2):
            moved = self.start(stats, which)
            near, before, present, _ = moved
            last = jnp.where(present, jnp.minimum(OWN, SPANS - near), 0)

            def shares(state, moved=moved, last=last):
                m, _ = state
                return (m <= last) & self.shares(stats, moved, m)

            def visit(state, which=which, moved=moved, near=near, before=before):
                m, count = state
                column, offset = self.local(m), near + m - 1
                moved_flag = True if bits is None else has_bit(bits[which], offset)
                column_flag = holder[column * SPANS + offset] != REPS
                listed = (before & moved_flag) | (jnp.logical_not(before) & column_flag)
                area = self.area(stats, moved, m)
                count = put_task(
                    tasks, count, listed, which, column, *area, which, column, offset
                )
                return m + 1, count

            first = self.first_column(near, lean)
            _, count = lax.while_loop(shares, visit, (first, count))
        return count

    def keep_listed(self, found, tasks, bits):
        def visit(index, count):
            task = [found[index * FIELDS + field] for field in range(FIELDS)]
            listed = has_bit(jnp.where(task[0] == 0, bits[0], bits[1]), task[8])
            return put_task(tasks, count, (self.side == 1) | listed, *task)

        count = lax.fori_loop(0, found[EDGE_TASKS], visit, jnp.int32(0))
        pad_tasks(tasks, count)
        return count


def own_kernel(
    block_count, place, holder, stats, best, units, mine, far_list, row_acc, col_acc, tasks
):
    col_acc[...] = jnp.full(col_acc.shape, -1.0, jnp.float32)
    row_acc[...] = jnp.full(row_acc.shape, -1.0, jnp.float32)
    shard, rep = place[0], place[1]

    def label_facts(block):
        return label_stats(stats, block_count, shard, shard * OWN + block)

    count = jnp.int32(0)
    for turn in range(3):
        block = local_class(rep, turn)
        b_first, _, b_count, _ = label_facts(block)

        def shares(state, b_first=b_first):
            other, _ = state
            return (other >= 0) & (label_facts(jnp.maximum(other, 0))[1] == b_first)

        def visit(state, block=block, turn=turn, b_count=b_count):
            other, count = state
            listed = holder[other * SPANS + (block - other)] != REPS
            a_start = label_facts(other)[3]
            count = put_task(
                tasks, count, listed, block, other, 0, b_count, a_start, BLOCK, turn, other,
                block - other,
            )
            return other - 1, count

        _, count = lax.while_loop(shares, visit, (block - 1, count))
    pad_tasks(tasks, count)
    run_tasks(tasks, count, units, units, row_acc, col_acc)
    mine[...] = jnp.maximum(best[...], jnp.max(col_acc[...], axis=1))
    for turn in range(3):
        here = (pl.ds(local_class(place[1], turn), 1), slice(None))
        found = as_lanes(jnp.max(row_acc[turn], axis=1, keepdims=True))
        mine[here] = jnp.maximum(mine[here], found)
    edge = Boundary(True, block_count, place)
    far_list[EDGE_TASKS] = edge.list_tasks(far_list, stats, holder)
    moved = edge.start(stats, 0)
    bridged = moved[2] & edge.shares(stats, moved, OWN + 1)
    far_list[EDGE_TASKS + 1] = bridged.astype(jnp.int32)


def far_kernel(
    block_count, place, far_list, best, units, far, mine, returned, row_acc, col_acc, tasks
):
    edge = Boundary(True, block_count, place)
    col_acc[...] = jnp.full(col_acc.shape, -1.0, jnp.float32)
    row_acc[...] = jnp.full(row_acc.shape, -1.0, jnp.float32)
    tail = far[pl.ds(FAR_SLOTS * BLOCK, TAIL), :]
    bits = [flag_bits(tail, slot) for slot in range(2)]
    count = edge.keep_listed(far_list, tasks, bits)
    run_tasks(tasks, count, far, units, row_acc, col_acc)
    mine[...] = jnp.maximum(best[...], jnp.max(col_acc[...], axis=1))
    for which in range(2):
        returned[which : which + 1, :] = as_lanes(
            jnp.max(row_acc[which], axis=1, keepdims=True)
        )


def pairs_chip_early(shard):
    return lax.rem(shard, ROW) == 0


def compare_chip(edge, holder, stats, units, chip, mine, other, row_acc, col_acc, tasks):
    col_acc[...] = jnp.full(col_acc.shape, -1.0, jnp.float32)
    row_acc[...] = jnp.full(row_acc.shape, -1.0, jnp.float32)
    tail = chip[pl.ds(CHIP_SLOTS * BLOCK, TAIL), :]
    bits = [flag_bits(tail, slot) for slot in range(2)]
    count = edge.list_tasks(tasks, stats, holder, bits)
    pad_tasks(tasks, count)
    run_tasks(tasks, count, chip, units, row_acc, col_acc)
    mine[...] = jnp.maximum(mine[...], jnp.max(col_acc[...], axis=1))
    for which in range(2):
        here = (pl.ds(chip_local(1 - edge.core, edge.near(which)), 1), slice(None))
        found = as_lanes(jnp.max(row_acc[which], axis=1, keepdims=True))
        other[here] = jnp.maximum(other[here], found)


def bridge_kernel(
    block_count, place, holder, far_list, stats, found_in, mine_in, units, far, chip,
    returned, mine, other, row_acc, col_acc, tasks,
):
    returned[...] = found_in[...]
    mine[...] = mine_in[...]
    other[...] = jnp.full(other.shape, -1.0, jnp.float32)

    @pl.when(far_list[EDGE_TASKS + 1] > 0)
    def _():
        edge = Boundary(True, block_count, place)
        far_bits = flag_bits(far[pl.ds(FAR_SLOTS * BLOCK, TAIL), :], 0)
        tail = chip[pl.ds(CHIP_SLOTS * BLOCK, TAIL), :]
        moved = edge.start(stats, 0)
        rows, cols = [], []
        slots = (0, 2, 3, 4)
        for slot in slots:
            m = OWN + chip_index(edge.rep, slot)
            offset, area = moved[0] + m - 1, edge.area(stats, moved, m)
            active = moved[2] & (offset < SPANS) & edge.shares(stats, moved, m)
            offset = jnp.minimum(offset, SPANS - 1)
            bits = jnp.where(edge.side == 0, far_bits, flag_bits(tail, slot))
            listed = has_bit(bits, offset)
            scored = inside(similarity(far[0:BLOCK, :], chip[rows_of(slot), :]), *area)
            scored = jnp.where(active & listed, scored, -1.0)
            rows.append(fold_rows(scored))
            cols.append(fold_cols(scored))
        for slot, found in zip(slots, cols):
            block = chip_local(1 - edge.core, chip_index(edge.rep, slot))
            other[pl.ds(block, 1), :] = jnp.max(found, axis=0, keepdims=True)
        best = functools.reduce(jnp.maximum, rows)
        best = as_lanes(jnp.max(best, axis=1, keepdims=True))
        returned[0:1, :] = jnp.maximum(returned[0:1, :], best)

    @pl.when(pairs_chip_early(place[0]))
    def _():
        edge = Boundary(False, block_count, place)
        compare_chip(edge, holder, stats, units, chip, mine, other, row_acc, col_acc, tasks)


def chip_kernel(
    block_count, place, holder, stats, mine_in, other_in, units, chip,
    mine, other, row_acc, col_acc, tasks,
):
    mine[...] = mine_in[...]
    other[...] = other_in[...]

    @pl.when(jnp.logical_not(pairs_chip_early(place[0])))
    def _():
        edge = Boundary(False, block_count, place)
        compare_chip(edge, holder, stats, units, chip, mine, other, row_acc, col_acc, tasks)


BEST = pltpu.VMEM((OWN, BLOCK), jnp.float32)
LIST = jax.ShapeDtypeStruct((EDGE_TASKS + 2,), jnp.int32)
RETURNED = pltpu.VMEM((2, BLOCK), jnp.float32)


def pair_call(kernel, name, estimate, outs, scalars, scratch, args):
    return pl.pallas_call(
        kernel,
        out_shape=outs,
        in_specs=[SMEM] * scalars + [VMEM] * (len(args) - scalars),
        out_specs=tuple(SMEM if out is LIST else VMEM for out in outs),
        scratch_shapes=scratch,
        compiler_params=PARAMS,
        cost_estimate=estimate,
        name=name,
    )(*args)


OWN_SCRATCH = [
    pltpu.VMEM((3, BLOCK, 128), jnp.float32),
    pltpu.VMEM((OWN, 8, BLOCK), jnp.float32),
    pltpu.SMEM((OWN_TASKS,), jnp.int32),
]
EDGE_SCRATCH = [
    pltpu.VMEM((2, BLOCK, 128), jnp.float32),
    pltpu.VMEM((OWN, 8, BLOCK), jnp.float32),
    pltpu.SMEM((EDGE_TASKS,), jnp.int32),
]


def finish_kernel(block_count, place, mine, other, back, outgoing, merged):
    shard, rep = place[0], place[1]
    core = lax.rem(shard, 2)
    has_far = (shard > 0) & (shard < block_count // OWN - 1)
    merged[...] = mine[...]
    for which in range(2):
        here = (pl.ds(far_local(core, far_index(rep, which)), 1), slice(None))
        found = jnp.where(has_far, back[which : which + 1, :], -1.0)
        merged[here] = jnp.maximum(merged[here], found)
    for target in range(2):
        share = jnp.where(core == target, merged[...], other[...])
        for copy in range(REPS):
            at = target * REPS + copy
            outgoing[at, pl.ds(0, OWN, stride=2), :] = share[:, 0:128]
            outgoing[at, pl.ds(1, OWN, stride=2), :] = share[:, 128:256]


def finish(block_count, place, mine, other, back):
    return pl.pallas_call(
        functools.partial(finish_kernel, block_count),
        out_shape=jax.ShapeDtypeStruct((2 * REPS, OWN * 2, 128), jnp.float32),
        in_specs=[SMEM, VMEM, VMEM, VMEM],
        out_specs=VMEM,
        scratch_shapes=[pltpu.VMEM((OWN, BLOCK), jnp.float32)],
        compiler_params=PARAMS,
        cost_estimate=cost(1),
        name="finish",
    )(place, mine, other, back)


def shards(embeddings, labels, holder):
    count = lax.axis_size("shard")
    block_count = count * OWN
    place = jnp.stack([lax.axis_index("shard"), lax.axis_index("rep")]).astype(jnp.int32)
    listing = holder.reshape(-1)
    labels = pltpu.with_memory_space_constraint(labels.reshape(-1, 128), pltpu.HBM)
    embeddings = pltpu.with_memory_space_constraint(embeddings, pltpu.HBM)
    across = [(s, s + 1) for s in range(1, count - 1, 2)]
    across = across + [(b, a) for a, b in across]
    within = [(s, s ^ 1) for s in range(count)]

    def in_vmem(array):
        return pltpu.with_memory_space_constraint(array, pltpu.VMEM)

    far_out = far_rows(place, listing, embeddings)
    far_in = in_vmem(lax.ppermute(far_out, "shard", across))
    units, chip_out, best, stats = own_rows(
        block_count, place, listing, labels, far_out, embeddings
    )
    chip_in = in_vmem(lax.ppermute(chip_out, "shard", within))

    mine, far_list = pair_call(
        functools.partial(own_kernel, block_count), "own_pairs", cost(3), (BEST, LIST),
        3, OWN_SCRATCH, (place, listing, stats, best, units),
    )
    mine, found = pair_call(
        functools.partial(far_kernel, block_count), "far_pairs", cost(4, 10**11),
        (BEST, RETURNED), 2, EDGE_SCRATCH, (place, far_list, mine, units, far_in),
    )
    returned, mine, other = pair_call(
        functools.partial(bridge_kernel, block_count), "bridge_pairs", cost(1),
        (RETURNED, BEST, BEST), 4, EDGE_SCRATCH,
        (place, listing, far_list, stats, found, mine, units, far_in, chip_in),
    )
    back = lax.ppermute(returned, "shard", across)
    mine, other = pair_call(
        functools.partial(chip_kernel, block_count), "chip_pairs", cost(4), (BEST, BEST),
        3, EDGE_SCRATCH, (place, listing, stats, mine, other, units, chip_in),
    )
    outgoing = finish(block_count, place, mine, other, back)
    groups = [list(range(c * 2 * REPS, (c + 1) * 2 * REPS)) for c in range(count // 2)]
    parts = lax.all_to_all(outgoing, ("shard", "rep"), 0, 0, axis_index_groups=groups)
    return jnp.max(parts, axis=0).reshape(OWN * BLOCK)


def solution(mesh):
    return jax.shard_map(
        shards,
        mesh=mesh,
        in_specs=(P("shard", None), P(), P("shard", None)),
        out_specs=P("shard"),
        check_vma=False,
    )
```

```python
import functools

import jax
import jax.numpy as jnp
from jax import lax
from jax.experimental import pallas as pl
from jax.experimental.pallas import tpu as pltpu
from jax.sharding import PartitionSpec as P

BLOCK = 256
SPANS = 17
WIDTH = 1024
OWN = 12
REPS = 4
MOVED = 8
NEAR = 4
CHIP_SLOTS = 2 + NEAR - 1
FAR_SLOTS = 2
TAIL = 16
FAR_ROWS = FAR_SLOTS * BLOCK + TAIL
CHIP_ROWS = CHIP_SLOTS * BLOCK + TAIL
WINDOW = OWN + 2 * (SPANS - 1)
GROUP = 8 * 128 // BLOCK
CHUNK = 128
WIDE, NARROW = 8, 4
FIELDS = 9
EPS = 1e-6
VMEM_LIMIT = 20 * 1024 * 1024

HBM = pl.BlockSpec(memory_space=pltpu.HBM)
ANY = pl.BlockSpec(memory_space=pl.ANY)
SMEM = pl.BlockSpec(memory_space=pltpu.SMEM)
VMEM = pl.BlockSpec(memory_space=pltpu.VMEM)


def cost(us, flops=0):
    return pl.CostEstimate(flops=flops, bytes_accessed=us * 3_000_000, transcendentals=0)


PARAMS = pltpu.CompilerParams(vmem_limit_bytes=VMEM_LIMIT)


def rows_of(slot, count=BLOCK):
    return pl.ds(pl.multiple_of(slot * BLOCK, BLOCK), count)


def unit_rows(rows):
    squares = jnp.sum(rows * rows, axis=1, keepdims=True)
    return (rows * lax.rsqrt(squares + EPS)).astype(jnp.bfloat16)


def normalise(raw, raw_slot, out, out_slot):
    for step in range(BLOCK // CHUNK):
        source = pl.ds(pl.multiple_of(raw_slot * BLOCK + step * CHUNK, CHUNK), CHUNK)
        target = pl.ds(pl.multiple_of(out_slot * BLOCK + step * CHUNK, CHUNK), CHUNK)
        out[target, :] = unit_rows(raw[source, :])


def far_local(core, m):
    return jnp.where(core == 0, m - 1, OWN - m)


def chip_local(core, m):
    return jnp.where(core == 0, OWN - m, m - 1)


def far_index(rep, slot):
    return jnp.where(slot == 0, rep + 1, MOVED - rep)


def chip_index(rep, slot):
    if slot < 2:
        return far_index(rep, slot)
    return slot - 1 + (slot - 1 > rep).astype(jnp.int32)


def flag_rows(holder, locals_of_slots):
    lane = lax.broadcasted_iota(jnp.int32, (TAIL, 128), 1)
    row = lax.broadcasted_iota(jnp.int32, (TAIL, 128), 0)
    flags = jnp.zeros((TAIL, 128), jnp.float32)
    for slot, local in enumerate(locals_of_slots):
        for k in range(SPANS):
            listed = jnp.where(holder[local * SPANS + k] != REPS, 1.0, 0.0)
            flags = jnp.where((row == slot) & (lane == k), listed, flags)
    return flags.astype(jnp.bfloat16)


def far_rows_kernel(place, holder_hbm, emb, far_out, raw, holder, sems, holder_sem):
    core, rep = place[0] % 2, place[1]
    local = [far_local(core, far_index(rep, slot)) for slot in range(FAR_SLOTS)]
    listing = pltpu.make_async_copy(holder_hbm, holder, holder_sem)
    listing.start()
    fetches = []
    for slot in range(FAR_SLOTS):
        for step in range(BLOCK // CHUNK):
            source = pl.ds(pl.multiple_of(local[slot] * BLOCK + step * CHUNK, CHUNK), CHUNK)
            part = pl.ds(slot * BLOCK + step * CHUNK, CHUNK)
            sem = sems.at[len(fetches)]
            fetches.append((part, pltpu.make_async_copy(emb.at[source], raw.at[part], sem)))
    for _, fetch in fetches:
        fetch.start()
    far_out[FAR_SLOTS * BLOCK :, :] = jnp.zeros((TAIL, WIDTH), jnp.bfloat16)
    for part, fetch in fetches:
        fetch.wait()
        far_out[part, :] = unit_rows(raw[part, :])
    listing.wait()
    far_out[pl.ds(FAR_SLOTS * BLOCK, TAIL), 0:128] = flag_rows(holder, local)


def far_rows(place, holder, emb):
    return pl.pallas_call(
        far_rows_kernel,
        out_shape=pltpu.VMEM((FAR_ROWS, WIDTH), jnp.bfloat16),
        in_specs=[SMEM, HBM, HBM],
        out_specs=VMEM,
        scratch_shapes=[
            pltpu.VMEM((FAR_SLOTS * BLOCK, WIDTH), jnp.float32),
            pltpu.SMEM(holder.shape, jnp.int32),
            pltpu.SemaphoreType.DMA((FAR_SLOTS * BLOCK // CHUNK,)),
            pltpu.SemaphoreType.DMA,
        ],
        compiler_params=PARAMS,
        cost_estimate=cost(1),
        name="far_rows",
    )(place, pltpu.with_memory_space_constraint(holder, pltpu.HBM), emb)


def similarity(left, right):
    return lax.dot_general(
        left, right, (((1,), (1,)), ((), ())), preferred_element_type=jnp.float32
    )


def inside(scored, row_low, row_end, col_low, col_end):
    rows = lax.broadcasted_iota(jnp.int32, (BLOCK, BLOCK), 0)
    cols = lax.broadcasted_iota(jnp.int32, (BLOCK, BLOCK), 1)
    keep = (rows >= row_low) & (rows < row_end) & (cols >= col_low) & (cols < col_end)
    return jnp.where(keep, scored, -1.0)


def fold_rows(scored):
    return jnp.maximum(scored[:, 0:128], scored[:, 128:256])


def fold_cols(scored):
    return jnp.max(scored.reshape(BLOCK // 8, 8, BLOCK), axis=0)


def as_lanes(column):
    rows = lax.broadcasted_iota(jnp.int32, (BLOCK, BLOCK), 0)
    cols = lax.broadcasted_iota(jnp.int32, (BLOCK, BLOCK), 1)
    return jnp.max(jnp.where(rows == cols, column, -1.0), axis=0, keepdims=True)


def first_group(shard, block_count):
    own = OWN // GROUP
    return jnp.clip(
        shard * own - (SPANS - 1) // GROUP, 0, (block_count - WINDOW) // GROUP
    )


def label_stats(stats, block_count, shard, block):
    slot = jnp.clip(block - first_group(shard, block_count) * GROUP, 0, WINDOW - 1)
    return [stats[part, slot] for part in range(4)]


def write_stats(tags, table):
    halves = [tags[pl.ds(half, WINDOW, stride=2), :].astype(jnp.float32) for half in range(2)]
    first, last = halves[0][:, 0:1], halves[1][:, 127:128]
    of_first = sum(jnp.where(half == first, 1.0, 0.0) for half in halves)
    before_last = sum(jnp.where(half < last, 1.0, 0.0) for half in halves)
    columns = [
        first,
        last,
        jnp.sum(of_first, axis=1, keepdims=True),
        jnp.sum(before_last, axis=1, keepdims=True),
    ]
    lane = lax.broadcasted_iota(jnp.int32, (WINDOW, 128), 1)
    spread = jnp.zeros((WINDOW, 128), jnp.float32)
    for part, column in enumerate(columns):
        spread = jnp.where(lane == part, column, spread)
    spread = jnp.concatenate([spread, jnp.zeros((128 - WINDOW, 128), jnp.float32)], axis=0)
    table[...] = spread.T[0:8, :].astype(jnp.int32)


def put_task(tasks, count, active, *fields):
    for place, field in enumerate(fields):
        tasks[count * FIELDS + place] = field
    return count + active.astype(jnp.int32)


def pad_tasks(tasks, count):
    for extra in range(WIDE - 1):
        for field in range(FIELDS):
            tasks[(count + extra) * FIELDS + field] = 0


def run_tasks(tasks, count, left, right, row_acc, col_acc):

    def run(first, width):
        found = []
        for lane in range(width):
            base = (first + lane) * FIELDS
            task = [tasks[base + field] for field in range(FIELDS)]
            scored = similarity(left[rows_of(task[0]), :], right[rows_of(task[1]), :])
            scored = inside(scored, *task[2:6])
            found.append((task[6], task[7], fold_rows(scored), fold_cols(scored)))
        for row_slot, col_slot, rows, cols in found:
            row_acc[row_slot] = jnp.maximum(row_acc[row_slot], rows)
            col_acc[col_slot] = jnp.maximum(col_acc[col_slot], cols)

    steps = (count + WIDE - NARROW - 1) // WIDE

    @pl.loop(0, steps)
    def _(step):
        run(step * WIDE, WIDE)

    @pl.when(count > steps * WIDE)
    def _():
        run(steps * WIDE, NARROW)


def task_words(most):
    return (most + WIDE) * FIELDS


OWN_TASKS = task_words(OWN * (OWN - 1) // 2)
EDGE_TASKS = task_words(2 * OWN)


def local_class(rep, turn):
    return (rep, 7 - rep, 8 + rep)[turn]


def rows_kernel(
    block_count, place, holder, labels, far, emb,
    units, chip_out, best, stats,
    raw, tags, sems, tag_sem,
):
    shard, rep = place[0], place[1]
    core = lax.rem(shard, 2)
    group = first_group(shard, block_count)
    sent = [far_local(core, far_index(rep, slot)) for slot in range(FAR_SLOTS)]
    local = [chip_local(core, chip_index(rep, slot)) for slot in range(CHIP_SLOTS)]

    def fetch(block):
        return pltpu.make_async_copy(
            emb.at[rows_of(block)], raw.at[rows_of(block)], sems.at[block]
        )

    def is_new(block):
        return (block != sent[0]) & (block != sent[1])

    window = pl.ds(pl.multiple_of(group * 8, 8), WINDOW * 2)
    fetch_tags = pltpu.make_async_copy(labels.at[window], tags, tag_sem)
    fetch_tags.start()

    def request(m):
        block = chip_local(core, m)
        pl.when(is_new(block))(lambda: fetch(block).start())

    pl.loop(1, 5)(request)
    chip_out[CHIP_SLOTS * BLOCK :, :] = jnp.zeros((TAIL, WIDTH), jnp.bfloat16)
    chip_out[CHIP_SLOTS * BLOCK :, 0:128] = flag_rows(holder, local)
    best[...] = jnp.full(best.shape, -1.0, jnp.float32)
    for slot in range(FAR_SLOTS):
        units[rows_of(sent[slot]), :] = far[rows_of(slot), :]
    fetch_tags.wait()
    write_stats(tags, stats)
    pl.loop(5, OWN + 1)(request)

    def diagonal(block):
        at = (shard * OWN + block - group * GROUP) * 2
        tag_row = jnp.concatenate([tags[pl.ds(at, 1), :], tags[pl.ds(at + 1, 1), :]], axis=1)
        tag_row = tag_row.astype(jnp.float32)
        rows = lax.broadcasted_iota(jnp.int32, (BLOCK, BLOCK), 0)
        cols = lax.broadcasted_iota(jnp.int32, (BLOCK, BLOCK), 1)
        spread = jnp.broadcast_to(tag_row, (BLOCK, BLOCK))
        tag_col = jnp.max(jnp.where(rows == cols, spread, -1.0), axis=1, keepdims=True)
        scored = similarity(units[rows_of(block), :], units[rows_of(block), :])
        keep = (tag_col == tag_row) & (rows != cols)
        found = jnp.max(jnp.where(keep, scored, -1.0), axis=0, keepdims=True)
        best[pl.ds(block, 1), :] = jnp.where(holder[block * SPANS] != REPS, found, -1.0)

    def arrive(m):
        block = chip_local(core, m)

        @pl.when(is_new(block))
        def _():
            fetch(block).wait()
            normalise(raw, block, units, block)

        mine = block == local_class(rep, 0)
        for turn in range(1, 3):
            mine = mine | (block == local_class(rep, turn))
        pl.when(mine)(lambda: diagonal(block))

    def arrive_and_send(m):
        arrive(m)
        block = chip_local(core, m)
        for slot in range(CHIP_SLOTS):

            @pl.when(block == local[slot])
            def _(slot=slot):
                chip_out[rows_of(slot), :] = units[rows_of(block), :]

    pl.loop(1, MOVED + 1)(arrive_and_send)
    pl.loop(MOVED + 1, OWN + 1)(arrive)


def own_rows(block_count, place, holder, labels, far, emb):
    return pl.pallas_call(
        functools.partial(rows_kernel, block_count),
        out_shape=(
            pltpu.VMEM((OWN * BLOCK, WIDTH), jnp.bfloat16),
            pltpu.VMEM((CHIP_ROWS, WIDTH), jnp.bfloat16),
            pltpu.VMEM((OWN, BLOCK), jnp.float32),
            pltpu.VMEM((8, 128), jnp.int32),
        ),
        in_specs=[SMEM, SMEM, HBM, VMEM, HBM],
        out_specs=(VMEM, VMEM, VMEM, VMEM),
        scratch_shapes=[
            pltpu.VMEM((OWN * BLOCK, WIDTH), jnp.float32),
            pltpu.VMEM((WINDOW * 2, 128), jnp.int32),
            pltpu.SemaphoreType.DMA((OWN,)),
            pltpu.SemaphoreType.DMA,
        ],
        compiler_params=PARAMS,
        cost_estimate=cost(5),
        name="own_rows",
    )(place, holder, labels, far, emb)


def flag_bits(tail, slot):
    lane = lax.broadcasted_iota(jnp.int32, (TAIL, 128), 1)
    row = lax.broadcasted_iota(jnp.int32, (TAIL, 128), 0)
    weight = lax.shift_left(jnp.int32(1), jnp.minimum(lane, SPANS)).astype(jnp.float32)
    weight = jnp.where((row == slot) & (lane < SPANS), weight, 0.0)
    return jnp.sum(tail[:, 0:128].astype(jnp.float32) * weight).astype(jnp.int32)


def has_bit(bits, offset):
    return lax.rem(lax.shift_right_logical(bits, offset), 2) == 1


class Boundary:
    def __init__(self, far, block_count, place):
        self.far, self.block_count = far, block_count
        self.shard, self.rep = place[0], place[1]
        self.core = lax.rem(self.shard, 2)
        self.side = self.core if far else 1 - self.core

    def local(self, m):
        return far_local(self.core, m) if self.far else chip_local(self.core, m)

    def near(self, which):
        return far_index(self.rep, which) if self.far else chip_index(self.rep, which)

    def start(self, stats, which):
        first_block = self.shard * OWN
        near = self.near(which)
        before = self.side == 0
        block = jnp.where(before, first_block - near, first_block + OWN - 1 + near)
        facts = label_stats(stats, self.block_count, self.shard, block)
        present = (block >= 0) & (block < self.block_count)
        return near, before, present, facts

    def shares(self, stats, moved, m):
        _, before, _, (m_first, m_last, _, _) = moved
        c_first, c_last, _, _ = self.column(stats, m)
        return jnp.where(before, m_last == c_first, c_last == m_first)

    def column(self, stats, m):
        first_block = self.shard * OWN
        block = jnp.where(self.side == 0, first_block + m - 1, first_block + OWN - m)
        return label_stats(stats, self.block_count, self.shard, block)

    def area(self, stats, moved, m):
        _, before, _, (_, _, m_count, m_start) = moved
        _, _, c_count, c_start = self.column(stats, m)
        return (
            jnp.where(before, m_start, 0), jnp.where(before, BLOCK, m_count),
            jnp.where(before, 0, c_start), jnp.where(before, c_count, BLOCK),
        )

    def lean(self, stats):
        middle = self.shard * OWN + jnp.where(self.side == 0, 0, OWN)
        facts = functools.partial(label_stats, stats, self.block_count, self.shard)
        label = facts(middle - 1)[1]
        ahead = lax.while_loop(
            lambda n: (n < jnp.minimum(middle, SPANS - 1)) & (facts(middle - 1 - n)[1] == label),
            lambda n: n + 1,
            jnp.int32(0),
        )
        behind = lax.while_loop(
            lambda n: (n < jnp.minimum(self.block_count - middle, SPANS - 1))
            & (facts(middle + n)[0] == label),
            lambda n: n + 1,
            jnp.int32(0),
        )
        return behind - ahead

    def first_column(self, near, lean):
        half = lax.shift_right_arithmetic(lean, 1)
        even = lean - 2 * half == 0
        behind = near + half + jnp.where(even & (lax.rem(near, 2) == 1), 0, 1)
        equal = near - half
        tie = even & (lax.rem(equal + 32, 2) == 1)
        ahead = equal + jnp.where(tie, 1, 0)
        return jnp.clip(jnp.where(self.side == 0, behind, ahead), 1, MOVED + 1)

    def list_tasks(self, tasks, stats, holder, bits=None):
        count = jnp.int32(0)
        lean = self.lean(stats)
        for which in range(2):
            moved = self.start(stats, which)
            near, before, present, _ = moved
            last = jnp.where(present, jnp.minimum(OWN, SPANS - near), 0)

            def shares(state, moved=moved, last=last):
                m, _ = state
                return (m <= last) & self.shares(stats, moved, m)

            def visit(state, which=which, moved=moved, near=near, before=before):
                m, count = state
                column, offset = self.local(m), near + m - 1
                moved_flag = True if bits is None else has_bit(bits[which], offset)
                column_flag = holder[column * SPANS + offset] != REPS
                listed = (before & moved_flag) | (jnp.logical_not(before) & column_flag)
                area = self.area(stats, moved, m)
                count = put_task(
                    tasks, count, listed, which, column, *area, which, column, offset
                )
                return m + 1, count

            first = self.first_column(near, lean)
            _, count = lax.while_loop(shares, visit, (first, count))
        return count

    def keep_listed(self, found, tasks, bits):
        def visit(index, count):
            task = [found[index * FIELDS + field] for field in range(FIELDS)]
            listed = has_bit(jnp.where(task[0] == 0, bits[0], bits[1]), task[8])
            return put_task(tasks, count, (self.side == 1) | listed, *task)

        count = lax.fori_loop(0, found[EDGE_TASKS], visit, jnp.int32(0))
        pad_tasks(tasks, count)
        return count


def own_kernel(
    block_count, place, holder, stats, best, units, mine, far_list, row_acc, col_acc, tasks
):
    col_acc[...] = jnp.full(col_acc.shape, -1.0, jnp.float32)
    row_acc[...] = jnp.full(row_acc.shape, -1.0, jnp.float32)
    shard, rep = place[0], place[1]

    def label_facts(block):
        return label_stats(stats, block_count, shard, shard * OWN + block)

    count = jnp.int32(0)
    for turn in range(3):
        block = local_class(rep, turn)
        b_first, _, b_count, _ = label_facts(block)

        def shares(state, b_first=b_first):
            other, _ = state
            return (other >= 0) & (label_facts(jnp.maximum(other, 0))[1] == b_first)

        def visit(state, block=block, turn=turn, b_count=b_count):
            other, count = state
            listed = holder[other * SPANS + (block - other)] != REPS
            a_start = label_facts(other)[3]
            count = put_task(
                tasks, count, listed, block, other, 0, b_count, a_start, BLOCK, turn, other,
                block - other,
            )
            return other - 1, count

        _, count = lax.while_loop(shares, visit, (block - 1, count))
    pad_tasks(tasks, count)
    run_tasks(tasks, count, units, units, row_acc, col_acc)
    mine[...] = jnp.maximum(best[...], jnp.max(col_acc[...], axis=1))
    for turn in range(3):
        here = (pl.ds(local_class(place[1], turn), 1), slice(None))
        found = as_lanes(jnp.max(row_acc[turn], axis=1, keepdims=True))
        mine[here] = jnp.maximum(mine[here], found)
    edge = Boundary(True, block_count, place)
    far_list[EDGE_TASKS] = edge.list_tasks(far_list, stats, holder)
    moved = edge.start(stats, 0)
    bridged = moved[2] & edge.shares(stats, moved, OWN + 1)
    far_list[EDGE_TASKS + 1] = bridged.astype(jnp.int32)


def far_kernel(
    block_count, place, far_list, best, units, far, mine, returned, row_acc, col_acc, tasks
):
    mine[...] = best[...]
    returned[...] = jnp.full(returned.shape, -1.0, jnp.float32)

    @pl.when(far_list[EDGE_TASKS] > 0)
    def _():
        edge = Boundary(True, block_count, place)
        col_acc[...] = jnp.full(col_acc.shape, -1.0, jnp.float32)
        row_acc[...] = jnp.full(row_acc.shape, -1.0, jnp.float32)
        tail = far[pl.ds(FAR_SLOTS * BLOCK, TAIL), :]
        bits = [flag_bits(tail, slot) for slot in range(2)]
        count = edge.keep_listed(far_list, tasks, bits)
        run_tasks(tasks, count, far, units, row_acc, col_acc)
        mine[...] = jnp.maximum(best[...], jnp.max(col_acc[...], axis=1))
        for which in range(2):
            returned[which : which + 1, :] = as_lanes(
                jnp.max(row_acc[which], axis=1, keepdims=True)
            )


def bridge_kernel(block_count, place, far_list, stats, found_in, far, chip, returned, other):
    returned[...] = found_in[...]
    other[...] = jnp.full(other.shape, -1.0, jnp.float32)

    @pl.when(far_list[EDGE_TASKS + 1] > 0)
    def _():
        edge = Boundary(True, block_count, place)
        far_bits = flag_bits(far[pl.ds(FAR_SLOTS * BLOCK, TAIL), :], 0)
        tail = chip[pl.ds(CHIP_SLOTS * BLOCK, TAIL), :]
        moved = edge.start(stats, 0)
        rows, cols = [], []
        slots = (0, 2, 3, 4)
        for slot in slots:
            m = OWN + chip_index(edge.rep, slot)
            offset, area = moved[0] + m - 1, edge.area(stats, moved, m)
            active = moved[2] & (offset < SPANS) & edge.shares(stats, moved, m)
            offset = jnp.minimum(offset, SPANS - 1)
            bits = jnp.where(edge.side == 0, far_bits, flag_bits(tail, slot))
            listed = has_bit(bits, offset)
            scored = inside(similarity(far[0:BLOCK, :], chip[rows_of(slot), :]), *area)
            scored = jnp.where(active & listed, scored, -1.0)
            rows.append(fold_rows(scored))
            cols.append(fold_cols(scored))
        for slot, found in zip(slots, cols):
            block = chip_local(1 - edge.core, chip_index(edge.rep, slot))
            other[pl.ds(block, 1), :] = jnp.max(found, axis=0, keepdims=True)
        best = functools.reduce(jnp.maximum, rows)
        best = as_lanes(jnp.max(best, axis=1, keepdims=True))
        returned[0:1, :] = jnp.maximum(returned[0:1, :], best)


def chip_kernel(
    block_count, place, holder, stats, mine_in, other_in, units, chip,
    mine, other, row_acc, col_acc, tasks,
):
    edge = Boundary(False, block_count, place)
    col_acc[...] = jnp.full(col_acc.shape, -1.0, jnp.float32)
    row_acc[...] = jnp.full(row_acc.shape, -1.0, jnp.float32)
    tail = chip[pl.ds(CHIP_SLOTS * BLOCK, TAIL), :]
    bits = [flag_bits(tail, slot) for slot in range(2)]
    count = edge.list_tasks(tasks, stats, holder, bits)
    pad_tasks(tasks, count)
    run_tasks(tasks, count, chip, units, row_acc, col_acc)
    mine[...] = jnp.maximum(mine_in[...], jnp.max(col_acc[...], axis=1))
    other[...] = other_in[...]
    for which in range(2):
        here = (pl.ds(chip_local(1 - edge.core, edge.near(which)), 1), slice(None))
        found = as_lanes(jnp.max(row_acc[which], axis=1, keepdims=True))
        other[here] = jnp.maximum(other[here], found)


BEST = pltpu.VMEM((OWN, BLOCK), jnp.float32)
LIST = jax.ShapeDtypeStruct((EDGE_TASKS + 2,), jnp.int32)
RETURNED = pltpu.VMEM((2, BLOCK), jnp.float32)


def pair_call(kernel, name, estimate, outs, scalars, scratch, args):
    return pl.pallas_call(
        kernel,
        out_shape=outs,
        in_specs=[SMEM] * scalars + [VMEM] * (len(args) - scalars),
        out_specs=tuple(SMEM if out is LIST else VMEM for out in outs),
        scratch_shapes=scratch,
        compiler_params=PARAMS,
        cost_estimate=estimate,
        name=name,
    )(*args)


OWN_SCRATCH = [
    pltpu.VMEM((3, BLOCK, 128), jnp.float32),
    pltpu.VMEM((OWN, 8, BLOCK), jnp.float32),
    pltpu.SMEM((OWN_TASKS,), jnp.int32),
]
EDGE_SCRATCH = [
    pltpu.VMEM((2, BLOCK, 128), jnp.float32),
    pltpu.VMEM((OWN, 8, BLOCK), jnp.float32),
    pltpu.SMEM((EDGE_TASKS,), jnp.int32),
]


def finish_kernel(block_count, place, mine, other, back, outgoing, merged):
    shard, rep = place[0], place[1]
    core = lax.rem(shard, 2)
    has_far = (shard > 0) & (shard < block_count // OWN - 1)
    merged[...] = mine[...]
    for which in range(2):
        here = (pl.ds(far_local(core, far_index(rep, which)), 1), slice(None))
        found = jnp.where(has_far, back[which : which + 1, :], -1.0)
        merged[here] = jnp.maximum(merged[here], found)
    for target in range(2):
        share = jnp.where(core == target, merged[...], other[...])
        for copy in range(REPS):
            at = target * REPS + copy
            outgoing[at, pl.ds(0, OWN, stride=2), :] = share[:, 0:128]
            outgoing[at, pl.ds(1, OWN, stride=2), :] = share[:, 128:256]


def finish(block_count, place, mine, other, back):
    return pl.pallas_call(
        functools.partial(finish_kernel, block_count),
        out_shape=jax.ShapeDtypeStruct((2 * REPS, OWN * 2, 128), jnp.float32),
        in_specs=[SMEM, VMEM, VMEM, VMEM],
        out_specs=VMEM,
        scratch_shapes=[pltpu.VMEM((OWN, BLOCK), jnp.float32)],
        compiler_params=PARAMS,
        cost_estimate=cost(1),
        name="finish",
    )(place, mine, other, back)


def shards(embeddings, labels, holder):
    count = lax.axis_size("shard")
    block_count = count * OWN
    place = jnp.stack([lax.axis_index("shard"), lax.axis_index("rep")]).astype(jnp.int32)
    listing = holder.reshape(-1)
    labels = pltpu.with_memory_space_constraint(labels.reshape(-1, 128), pltpu.HBM)
    embeddings = pltpu.with_memory_space_constraint(embeddings, pltpu.HBM)
    across = [(s, s + 1) for s in range(1, count - 1, 2)]
    across = across + [(b, a) for a, b in across]
    within = [(s, s ^ 1) for s in range(count)]

    def in_vmem(array):
        return pltpu.with_memory_space_constraint(array, pltpu.VMEM)

    far_out = far_rows(place, listing, embeddings)
    far_in = in_vmem(lax.ppermute(far_out, "shard", across))
    units, chip_out, best, stats = own_rows(
        block_count, place, listing, labels, far_out, embeddings
    )
    chip_in = in_vmem(lax.ppermute(chip_out, "shard", within))

    mine, far_list = pair_call(
        functools.partial(own_kernel, block_count), "own_pairs", cost(3), (BEST, LIST),
        3, OWN_SCRATCH, (place, listing, stats, best, units),
    )
    mine, found = pair_call(
        functools.partial(far_kernel, block_count), "far_pairs", cost(4, 10**11),
        (BEST, RETURNED), 2, EDGE_SCRATCH, (place, far_list, mine, units, far_in),
    )
    returned, other = pair_call(
        functools.partial(bridge_kernel, block_count), "bridge_pairs", cost(1),
        (RETURNED, BEST), 3, [], (place, far_list, stats, found, far_in, chip_in),
    )
    back = lax.ppermute(returned, "shard", across)
    mine, other = pair_call(
        functools.partial(chip_kernel, block_count), "chip_pairs", cost(4), (BEST, BEST),
        3, EDGE_SCRATCH, (place, listing, stats, mine, other, units, chip_in),
    )
    outgoing = finish(block_count, place, mine, other, back)
    groups = [list(range(c * 2 * REPS, (c + 1) * 2 * REPS)) for c in range(count // 2)]
    parts = lax.all_to_all(outgoing, ("shard", "rep"), 0, 0, axis_index_groups=groups)
    best = functools.reduce(jnp.maximum, [parts[i] for i in range(2 * REPS)])
    return best.reshape(OWN * BLOCK)


def solution(mesh):
    return jax.shard_map(
        shards,
        mesh=mesh,
        in_specs=(P("shard", None), P(), P("shard", None)),
        out_specs=P("shard"),
        check_vma=False,
    )
```

```python
import functools

import jax
import jax.numpy as jnp
from jax import lax
from jax.experimental import pallas as pl
from jax.experimental.pallas import tpu as pltpu
from jax.sharding import PartitionSpec as P

BLOCK = 256
SPANS = 17
WIDTH = 1024
OWN = 12
REPS = 4
MOVED = 8
NEAR = 4
CHIP_SLOTS = 2 + NEAR - 1
FAR_SLOTS = 2
TAIL = 16
FAR_ROWS = FAR_SLOTS * BLOCK + TAIL
CHIP_ROWS = CHIP_SLOTS * BLOCK + TAIL
WINDOW = OWN + 2 * (SPANS - 1)
GROUP = 8 * 128 // BLOCK
CHUNK = 128
WIDE, NARROW = 8, 4
FIELDS = 9
EPS = 1e-6
VMEM_LIMIT = 20 * 1024 * 1024

HBM = pl.BlockSpec(memory_space=pltpu.HBM)
ANY = pl.BlockSpec(memory_space=pl.ANY)
SMEM = pl.BlockSpec(memory_space=pltpu.SMEM)
VMEM = pl.BlockSpec(memory_space=pltpu.VMEM)


def cost(us, flops=0):
    return pl.CostEstimate(flops=flops, bytes_accessed=us * 3_000_000, transcendentals=0)


PARAMS = pltpu.CompilerParams(vmem_limit_bytes=VMEM_LIMIT)


def rows_of(slot, count=BLOCK):
    return pl.ds(pl.multiple_of(slot * BLOCK, BLOCK), count)


def unit_rows(rows):
    squares = jnp.sum(rows * rows, axis=1, keepdims=True)
    return (rows * lax.rsqrt(squares + EPS)).astype(jnp.bfloat16)


def normalise(raw, raw_slot, out, out_slot):
    for step in range(BLOCK // CHUNK):
        source = pl.ds(pl.multiple_of(raw_slot * BLOCK + step * CHUNK, CHUNK), CHUNK)
        target = pl.ds(pl.multiple_of(out_slot * BLOCK + step * CHUNK, CHUNK), CHUNK)
        out[target, :] = unit_rows(raw[source, :])


def far_local(core, m):
    return jnp.where(core == 0, m - 1, OWN - m)


def chip_local(core, m):
    return jnp.where(core == 0, OWN - m, m - 1)


def far_index(rep, slot):
    return jnp.where(slot == 0, rep + 1, MOVED - rep)


def chip_index(rep, slot):
    if slot < 2:
        return far_index(rep, slot)
    return slot - 1 + (slot - 1 > rep).astype(jnp.int32)


def flag_rows(holder, locals_of_slots):
    lane = lax.broadcasted_iota(jnp.int32, (TAIL, 128), 1)
    row = lax.broadcasted_iota(jnp.int32, (TAIL, 128), 0)
    flags = jnp.zeros((TAIL, 128), jnp.float32)
    for slot, local in enumerate(locals_of_slots):
        for k in range(SPANS):
            listed = jnp.where(holder[local * SPANS + k] != REPS, 1.0, 0.0)
            flags = jnp.where((row == slot) & (lane == k), listed, flags)
    return flags.astype(jnp.bfloat16)


def far_rows_kernel(place, holder_hbm, emb, far_out, raw, holder, sems, holder_sem):
    core, rep = place[0] % 2, place[1]
    local = [far_local(core, far_index(rep, slot)) for slot in range(FAR_SLOTS)]
    listing = pltpu.make_async_copy(holder_hbm, holder, holder_sem)
    listing.start()
    fetches = []
    for slot in range(FAR_SLOTS):
        for step in range(BLOCK // CHUNK):
            source = pl.ds(pl.multiple_of(local[slot] * BLOCK + step * CHUNK, CHUNK), CHUNK)
            part = pl.ds(slot * BLOCK + step * CHUNK, CHUNK)
            sem = sems.at[len(fetches)]
            fetches.append((part, pltpu.make_async_copy(emb.at[source], raw.at[part], sem)))
    for _, fetch in fetches:
        fetch.start()
    far_out[FAR_SLOTS * BLOCK :, :] = jnp.zeros((TAIL, WIDTH), jnp.bfloat16)
    for part, fetch in fetches:
        fetch.wait()
        far_out[part, :] = unit_rows(raw[part, :])
    listing.wait()
    far_out[pl.ds(FAR_SLOTS * BLOCK, TAIL), 0:128] = flag_rows(holder, local)


def far_rows(place, holder, emb):
    return pl.pallas_call(
        far_rows_kernel,
        out_shape=pltpu.VMEM((FAR_ROWS, WIDTH), jnp.bfloat16),
        in_specs=[SMEM, HBM, HBM],
        out_specs=VMEM,
        scratch_shapes=[
            pltpu.VMEM((FAR_SLOTS * BLOCK, WIDTH), jnp.float32),
            pltpu.SMEM(holder.shape, jnp.int32),
            pltpu.SemaphoreType.DMA((FAR_SLOTS * BLOCK // CHUNK,)),
            pltpu.SemaphoreType.DMA,
        ],
        compiler_params=PARAMS,
        cost_estimate=cost(1),
        name="far_rows",
    )(place, pltpu.with_memory_space_constraint(holder, pltpu.HBM), emb)


def similarity(left, right):
    return lax.dot_general(
        left, right, (((1,), (1,)), ((), ())), preferred_element_type=jnp.float32
    )


def inside(scored, row_low, row_end, col_low, col_end):
    rows = lax.broadcasted_iota(jnp.int32, (BLOCK, BLOCK), 0)
    cols = lax.broadcasted_iota(jnp.int32, (BLOCK, BLOCK), 1)
    keep = (rows >= row_low) & (rows < row_end) & (cols >= col_low) & (cols < col_end)
    return jnp.where(keep, scored, -1.0)


def fold_rows(scored):
    return jnp.maximum(scored[:, 0:128], scored[:, 128:256])


def fold_cols(scored):
    return jnp.max(scored.reshape(BLOCK // 8, 8, BLOCK), axis=0)


def as_lanes(column):
    rows = lax.broadcasted_iota(jnp.int32, (BLOCK, BLOCK), 0)
    cols = lax.broadcasted_iota(jnp.int32, (BLOCK, BLOCK), 1)
    return jnp.max(jnp.where(rows == cols, column, -1.0), axis=0, keepdims=True)


def first_group(shard, block_count):
    own = OWN // GROUP
    return jnp.clip(
        shard * own - (SPANS - 1) // GROUP, 0, (block_count - WINDOW) // GROUP
    )


def label_stats(stats, block_count, shard, block):
    slot = jnp.clip(block - first_group(shard, block_count) * GROUP, 0, WINDOW - 1)
    return [stats[part, slot] for part in range(4)]


def write_stats(tags, table):
    halves = [tags[pl.ds(half, WINDOW, stride=2), :].astype(jnp.float32) for half in range(2)]
    first, last = halves[0][:, 0:1], halves[1][:, 127:128]
    of_first = sum(jnp.where(half == first, 1.0, 0.0) for half in halves)
    before_last = sum(jnp.where(half < last, 1.0, 0.0) for half in halves)
    columns = [
        first,
        last,
        jnp.sum(of_first, axis=1, keepdims=True),
        jnp.sum(before_last, axis=1, keepdims=True),
    ]
    lane = lax.broadcasted_iota(jnp.int32, (WINDOW, 128), 1)
    spread = jnp.zeros((WINDOW, 128), jnp.float32)
    for part, column in enumerate(columns):
        spread = jnp.where(lane == part, column, spread)
    spread = jnp.concatenate([spread, jnp.zeros((128 - WINDOW, 128), jnp.float32)], axis=0)
    table[...] = spread.T[0:8, :].astype(jnp.int32)


def put_task(tasks, count, active, *fields):
    for place, field in enumerate(fields):
        tasks[count * FIELDS + place] = field
    return count + active.astype(jnp.int32)


def pad_tasks(tasks, count):
    for extra in range(WIDE - 1):
        for field in range(FIELDS):
            tasks[(count + extra) * FIELDS + field] = 0


def run_tasks(tasks, count, left, right, row_acc, col_acc):

    def run(first, width):
        found = []
        for lane in range(width):
            base = (first + lane) * FIELDS
            task = [tasks[base + field] for field in range(FIELDS)]
            scored = similarity(left[rows_of(task[0]), :], right[rows_of(task[1]), :])
            scored = inside(scored, *task[2:6])
            found.append((task[6], task[7], fold_rows(scored), fold_cols(scored)))
        for row_slot, col_slot, rows, cols in found:
            row_acc[row_slot] = jnp.maximum(row_acc[row_slot], rows)
            col_acc[col_slot] = jnp.maximum(col_acc[col_slot], cols)

    steps = (count + WIDE - NARROW - 1) // WIDE

    @pl.loop(0, steps)
    def _(step):
        run(step * WIDE, WIDE)

    @pl.when(count > steps * WIDE)
    def _():
        run(steps * WIDE, NARROW)


def task_words(most):
    return (most + WIDE) * FIELDS


OWN_TASKS = task_words(OWN * (OWN - 1) // 2)
EDGE_TASKS = task_words(2 * OWN)


def local_class(rep, turn):
    return (rep, 7 - rep, 8 + rep)[turn]


def rows_kernel(
    block_count, place, holder, labels, far, emb,
    units, chip_out, best, stats,
    raw, tags, sems, tag_sem,
):
    shard, rep = place[0], place[1]
    core = lax.rem(shard, 2)
    group = first_group(shard, block_count)
    sent = [far_local(core, far_index(rep, slot)) for slot in range(FAR_SLOTS)]
    local = [chip_local(core, chip_index(rep, slot)) for slot in range(CHIP_SLOTS)]

    def fetch(block):
        return pltpu.make_async_copy(
            emb.at[rows_of(block)], raw.at[rows_of(block)], sems.at[block]
        )

    def is_new(block):
        return (block != sent[0]) & (block != sent[1])

    window = pl.ds(pl.multiple_of(group * 8, 8), WINDOW * 2)
    fetch_tags = pltpu.make_async_copy(labels.at[window], tags, tag_sem)
    fetch_tags.start()

    def request(m):
        block = chip_local(core, m)
        pl.when(is_new(block))(lambda: fetch(block).start())

    pl.loop(1, 5)(request)
    chip_out[CHIP_SLOTS * BLOCK :, :] = jnp.zeros((TAIL, WIDTH), jnp.bfloat16)
    chip_out[CHIP_SLOTS * BLOCK :, 0:128] = flag_rows(holder, local)
    best[...] = jnp.full(best.shape, -1.0, jnp.float32)
    for slot in range(FAR_SLOTS):
        units[rows_of(sent[slot]), :] = far[rows_of(slot), :]
    fetch_tags.wait()
    write_stats(tags, stats)
    pl.loop(5, OWN + 1)(request)

    def diagonal(block):
        at = (shard * OWN + block - group * GROUP) * 2
        tag_row = jnp.concatenate([tags[pl.ds(at, 1), :], tags[pl.ds(at + 1, 1), :]], axis=1)
        tag_row = tag_row.astype(jnp.float32)
        rows = lax.broadcasted_iota(jnp.int32, (BLOCK, BLOCK), 0)
        cols = lax.broadcasted_iota(jnp.int32, (BLOCK, BLOCK), 1)
        spread = jnp.broadcast_to(tag_row, (BLOCK, BLOCK))
        tag_col = jnp.max(jnp.where(rows == cols, spread, -1.0), axis=1, keepdims=True)
        scored = similarity(units[rows_of(block), :], units[rows_of(block), :])
        keep = (tag_col == tag_row) & (rows != cols)
        found = jnp.max(jnp.where(keep, scored, -1.0), axis=0, keepdims=True)
        best[pl.ds(block, 1), :] = jnp.where(holder[block * SPANS] != REPS, found, -1.0)

    def arrive(m):
        block = chip_local(core, m)

        @pl.when(is_new(block))
        def _():
            fetch(block).wait()
            normalise(raw, block, units, block)

        mine = block == local_class(rep, 0)
        for turn in range(1, 3):
            mine = mine | (block == local_class(rep, turn))
        pl.when(mine)(lambda: diagonal(block))

    def arrive_and_send(m):
        arrive(m)
        block = chip_local(core, m)
        for slot in range(CHIP_SLOTS):

            @pl.when(block == local[slot])
            def _(slot=slot):
                chip_out[rows_of(slot), :] = units[rows_of(block), :]

    pl.loop(1, MOVED + 1)(arrive_and_send)
    pl.loop(MOVED + 1, OWN + 1)(arrive)


def own_rows(block_count, place, holder, labels, far, emb):
    return pl.pallas_call(
        functools.partial(rows_kernel, block_count),
        out_shape=(
            pltpu.VMEM((OWN * BLOCK, WIDTH), jnp.bfloat16),
            pltpu.VMEM((CHIP_ROWS, WIDTH), jnp.bfloat16),
            pltpu.VMEM((OWN, BLOCK), jnp.float32),
            pltpu.VMEM((8, 128), jnp.int32),
        ),
        in_specs=[SMEM, SMEM, HBM, VMEM, HBM],
        out_specs=(VMEM, VMEM, VMEM, VMEM),
        scratch_shapes=[
            pltpu.VMEM((OWN * BLOCK, WIDTH), jnp.float32),
            pltpu.VMEM((WINDOW * 2, 128), jnp.int32),
            pltpu.SemaphoreType.DMA((OWN,)),
            pltpu.SemaphoreType.DMA,
        ],
        compiler_params=PARAMS,
        cost_estimate=cost(5),
        name="own_rows",
    )(place, holder, labels, far, emb)


def flag_bits(tail, slot):
    lane = lax.broadcasted_iota(jnp.int32, (TAIL, 128), 1)
    row = lax.broadcasted_iota(jnp.int32, (TAIL, 128), 0)
    weight = lax.shift_left(jnp.int32(1), jnp.minimum(lane, SPANS)).astype(jnp.float32)
    weight = jnp.where((row == slot) & (lane < SPANS), weight, 0.0)
    return jnp.sum(tail[:, 0:128].astype(jnp.float32) * weight).astype(jnp.int32)


def has_bit(bits, offset):
    return lax.rem(lax.shift_right_logical(bits, offset), 2) == 1


class Boundary:
    def __init__(self, far, block_count, place):
        self.far, self.block_count = far, block_count
        self.shard, self.rep = place[0], place[1]
        self.core = lax.rem(self.shard, 2)
        self.side = self.core if far else 1 - self.core

    def local(self, m):
        return far_local(self.core, m) if self.far else chip_local(self.core, m)

    def near(self, which):
        return far_index(self.rep, which) if self.far else chip_index(self.rep, which)

    def start(self, stats, which):
        first_block = self.shard * OWN
        near = self.near(which)
        before = self.side == 0
        block = jnp.where(before, first_block - near, first_block + OWN - 1 + near)
        facts = label_stats(stats, self.block_count, self.shard, block)
        present = (block >= 0) & (block < self.block_count)
        return near, before, present, facts

    def shares(self, stats, moved, m):
        _, before, _, (m_first, m_last, _, _) = moved
        c_first, c_last, _, _ = self.column(stats, m)
        return jnp.where(before, m_last == c_first, c_last == m_first)

    def column(self, stats, m):
        first_block = self.shard * OWN
        block = jnp.where(self.side == 0, first_block + m - 1, first_block + OWN - m)
        return label_stats(stats, self.block_count, self.shard, block)

    def area(self, stats, moved, m):
        _, before, _, (_, _, m_count, m_start) = moved
        _, _, c_count, c_start = self.column(stats, m)
        return (
            jnp.where(before, m_start, 0), jnp.where(before, BLOCK, m_count),
            jnp.where(before, 0, c_start), jnp.where(before, c_count, BLOCK),
        )

    def lean(self, stats):
        middle = self.shard * OWN + jnp.where(self.side == 0, 0, OWN)
        facts = functools.partial(label_stats, stats, self.block_count, self.shard)
        label = facts(middle - 1)[1]
        ahead = lax.while_loop(
            lambda n: (n < jnp.minimum(middle, SPANS - 1)) & (facts(middle - 1 - n)[1] == label),
            lambda n: n + 1,
            jnp.int32(0),
        )
        behind = lax.while_loop(
            lambda n: (n < jnp.minimum(self.block_count - middle, SPANS - 1))
            & (facts(middle + n)[0] == label),
            lambda n: n + 1,
            jnp.int32(0),
        )
        return behind - ahead

    def first_column(self, near, lean):
        half = lax.shift_right_arithmetic(lean, 1)
        even = lean - 2 * half == 0
        behind = near + half + jnp.where(even & (lax.rem(near, 2) == 1), 0, 1)
        equal = near - half
        tie = even & (lax.rem(equal + 32, 2) == 1)
        ahead = equal + jnp.where(tie, 1, 0)
        return jnp.clip(jnp.where(self.side == 0, behind, ahead), 1, MOVED + 1)

    def list_tasks(self, tasks, stats, holder, bits=None):
        count = jnp.int32(0)
        lean = self.lean(stats)
        for which in range(2):
            moved = self.start(stats, which)
            near, before, present, _ = moved
            last = jnp.where(present, jnp.minimum(OWN, SPANS - near), 0)

            def shares(state, moved=moved, last=last):
                m, _ = state
                return (m <= last) & self.shares(stats, moved, m)

            def visit(state, which=which, moved=moved, near=near, before=before):
                m, count = state
                column, offset = self.local(m), near + m - 1
                moved_flag = True if bits is None else has_bit(bits[which], offset)
                column_flag = holder[column * SPANS + offset] != REPS
                listed = (before & moved_flag) | (jnp.logical_not(before) & column_flag)
                area = self.area(stats, moved, m)
                count = put_task(
                    tasks, count, listed, which, column, *area, which, column, offset
                )
                return m + 1, count

            first = self.first_column(near, lean)
            _, count = lax.while_loop(shares, visit, (first, count))
        return count

    def keep_listed(self, found, tasks, bits):
        def visit(index, count):
            task = [found[index * FIELDS + field] for field in range(FIELDS)]
            listed = has_bit(jnp.where(task[0] == 0, bits[0], bits[1]), task[8])
            return put_task(tasks, count, (self.side == 1) | listed, *task)

        count = lax.fori_loop(0, found[EDGE_TASKS], visit, jnp.int32(0))
        pad_tasks(tasks, count)
        return count


def own_kernel(
    block_count, place, holder, stats, best, units, mine, far_list, chip_list,
    row_acc, col_acc, tasks,
):
    col_acc[...] = jnp.full(col_acc.shape, -1.0, jnp.float32)
    row_acc[...] = jnp.full(row_acc.shape, -1.0, jnp.float32)
    shard, rep = place[0], place[1]

    def label_facts(block):
        return label_stats(stats, block_count, shard, shard * OWN + block)

    count = jnp.int32(0)
    for turn in range(3):
        block = local_class(rep, turn)
        b_first, _, b_count, _ = label_facts(block)

        def shares(state, b_first=b_first):
            other, _ = state
            return (other >= 0) & (label_facts(jnp.maximum(other, 0))[1] == b_first)

        def visit(state, block=block, turn=turn, b_count=b_count):
            other, count = state
            listed = holder[other * SPANS + (block - other)] != REPS
            a_start = label_facts(other)[3]
            count = put_task(
                tasks, count, listed, block, other, 0, b_count, a_start, BLOCK, turn, other,
                block - other,
            )
            return other - 1, count

        _, count = lax.while_loop(shares, visit, (block - 1, count))
    pad_tasks(tasks, count)
    run_tasks(tasks, count, units, units, row_acc, col_acc)
    mine[...] = jnp.maximum(best[...], jnp.max(col_acc[...], axis=1))
    for turn in range(3):
        here = (pl.ds(local_class(place[1], turn), 1), slice(None))
        found = as_lanes(jnp.max(row_acc[turn], axis=1, keepdims=True))
        mine[here] = jnp.maximum(mine[here], found)
    edge = Boundary(True, block_count, place)
    far_list[EDGE_TASKS] = edge.list_tasks(far_list, stats, holder)
    near = Boundary(False, block_count, place)
    chip_list[EDGE_TASKS] = near.list_tasks(chip_list, stats, holder)
    moved = edge.start(stats, 0)
    bridged = moved[2] & edge.shares(stats, moved, OWN + 1)
    far_list[EDGE_TASKS + 1] = bridged.astype(jnp.int32)


def far_kernel(
    block_count, place, far_list, best, units, far, mine, returned, row_acc, col_acc, tasks
):
    edge = Boundary(True, block_count, place)
    col_acc[...] = jnp.full(col_acc.shape, -1.0, jnp.float32)
    row_acc[...] = jnp.full(row_acc.shape, -1.0, jnp.float32)
    tail = far[pl.ds(FAR_SLOTS * BLOCK, TAIL), :]
    bits = [flag_bits(tail, slot) for slot in range(2)]
    count = edge.keep_listed(far_list, tasks, bits)
    run_tasks(tasks, count, far, units, row_acc, col_acc)
    mine[...] = jnp.maximum(best[...], jnp.max(col_acc[...], axis=1))
    for which in range(2):
        returned[which : which + 1, :] = as_lanes(
            jnp.max(row_acc[which], axis=1, keepdims=True)
        )


def bridge_kernel(block_count, place, far_list, stats, found_in, far, chip, returned, other):
    returned[...] = found_in[...]
    other[...] = jnp.full(other.shape, -1.0, jnp.float32)

    @pl.when(far_list[EDGE_TASKS + 1] > 0)
    def _():
        edge = Boundary(True, block_count, place)
        far_bits = flag_bits(far[pl.ds(FAR_SLOTS * BLOCK, TAIL), :], 0)
        tail = chip[pl.ds(CHIP_SLOTS * BLOCK, TAIL), :]
        moved = edge.start(stats, 0)
        rows, cols = [], []
        slots = (0, 2, 3, 4)
        for slot in slots:
            m = OWN + chip_index(edge.rep, slot)
            offset, area = moved[0] + m - 1, edge.area(stats, moved, m)
            active = moved[2] & (offset < SPANS) & edge.shares(stats, moved, m)
            offset = jnp.minimum(offset, SPANS - 1)
            bits = jnp.where(edge.side == 0, far_bits, flag_bits(tail, slot))
            listed = has_bit(bits, offset)
            scored = inside(similarity(far[0:BLOCK, :], chip[rows_of(slot), :]), *area)
            scored = jnp.where(active & listed, scored, -1.0)
            rows.append(fold_rows(scored))
            cols.append(fold_cols(scored))
        for slot, found in zip(slots, cols):
            block = chip_local(1 - edge.core, chip_index(edge.rep, slot))
            other[pl.ds(block, 1), :] = jnp.max(found, axis=0, keepdims=True)
        best = functools.reduce(jnp.maximum, rows)
        best = as_lanes(jnp.max(best, axis=1, keepdims=True))
        returned[0:1, :] = jnp.maximum(returned[0:1, :], best)


def chip_kernel(
    block_count, place, chip_list, mine_in, other_in, units, chip,
    mine, other, row_acc, col_acc, tasks,
):
    edge = Boundary(False, block_count, place)
    col_acc[...] = jnp.full(col_acc.shape, -1.0, jnp.float32)
    row_acc[...] = jnp.full(row_acc.shape, -1.0, jnp.float32)
    tail = chip[pl.ds(CHIP_SLOTS * BLOCK, TAIL), :]
    bits = [flag_bits(tail, slot) for slot in range(2)]
    count = edge.keep_listed(chip_list, tasks, bits)
    run_tasks(tasks, count, chip, units, row_acc, col_acc)
    mine[...] = jnp.maximum(mine_in[...], jnp.max(col_acc[...], axis=1))
    other[...] = other_in[...]
    for which in range(2):
        here = (pl.ds(chip_local(1 - edge.core, edge.near(which)), 1), slice(None))
        found = as_lanes(jnp.max(row_acc[which], axis=1, keepdims=True))
        other[here] = jnp.maximum(other[here], found)


BEST = pltpu.VMEM((OWN, BLOCK), jnp.float32)
LIST = jax.ShapeDtypeStruct((EDGE_TASKS + 2,), jnp.int32)
RETURNED = pltpu.VMEM((2, BLOCK), jnp.float32)


def pair_call(kernel, name, estimate, outs, scalars, scratch, args):
    return pl.pallas_call(
        kernel,
        out_shape=outs,
        in_specs=[SMEM] * scalars + [VMEM] * (len(args) - scalars),
        out_specs=tuple(SMEM if out is LIST else VMEM for out in outs),
        scratch_shapes=scratch,
        compiler_params=PARAMS,
        cost_estimate=estimate,
        name=name,
    )(*args)


OWN_SCRATCH = [
    pltpu.VMEM((3, BLOCK, 128), jnp.float32),
    pltpu.VMEM((OWN, 8, BLOCK), jnp.float32),
    pltpu.SMEM((OWN_TASKS,), jnp.int32),
]
EDGE_SCRATCH = [
    pltpu.VMEM((2, BLOCK, 128), jnp.float32),
    pltpu.VMEM((OWN, 8, BLOCK), jnp.float32),
    pltpu.SMEM((EDGE_TASKS,), jnp.int32),
]


def finish_kernel(block_count, place, mine, other, back, outgoing, merged):
    shard, rep = place[0], place[1]
    core = lax.rem(shard, 2)
    has_far = (shard > 0) & (shard < block_count // OWN - 1)
    merged[...] = mine[...]
    for which in range(2):
        here = (pl.ds(far_local(core, far_index(rep, which)), 1), slice(None))
        found = jnp.where(has_far, back[which : which + 1, :], -1.0)
        merged[here] = jnp.maximum(merged[here], found)
    for target in range(2):
        share = jnp.where(core == target, merged[...], other[...])
        for copy in range(REPS):
            at = target * REPS + copy
            outgoing[at, pl.ds(0, OWN, stride=2), :] = share[:, 0:128]
            outgoing[at, pl.ds(1, OWN, stride=2), :] = share[:, 128:256]


def finish(block_count, place, mine, other, back):
    return pl.pallas_call(
        functools.partial(finish_kernel, block_count),
        out_shape=jax.ShapeDtypeStruct((2 * REPS, OWN * 2, 128), jnp.float32),
        in_specs=[SMEM, VMEM, VMEM, VMEM],
        out_specs=VMEM,
        scratch_shapes=[pltpu.VMEM((OWN, BLOCK), jnp.float32)],
        compiler_params=PARAMS,
        cost_estimate=cost(1),
        name="finish",
    )(place, mine, other, back)


def shards(embeddings, labels, holder):
    count = lax.axis_size("shard")
    block_count = count * OWN
    place = jnp.stack([lax.axis_index("shard"), lax.axis_index("rep")]).astype(jnp.int32)
    listing = holder.reshape(-1)
    labels = pltpu.with_memory_space_constraint(labels.reshape(-1, 128), pltpu.HBM)
    embeddings = pltpu.with_memory_space_constraint(embeddings, pltpu.HBM)
    across = [(s, s + 1) for s in range(1, count - 1, 2)]
    across = across + [(b, a) for a, b in across]
    within = [(s, s ^ 1) for s in range(count)]

    def in_vmem(array):
        return pltpu.with_memory_space_constraint(array, pltpu.VMEM)

    far_out = far_rows(place, listing, embeddings)
    far_in = in_vmem(lax.ppermute(far_out, "shard", across))
    units, chip_out, best, stats = own_rows(
        block_count, place, listing, labels, far_out, embeddings
    )
    chip_in = in_vmem(lax.ppermute(chip_out, "shard", within))

    mine, far_list, chip_list = pair_call(
        functools.partial(own_kernel, block_count), "own_pairs", cost(3), (BEST, LIST, LIST),
        3, OWN_SCRATCH, (place, listing, stats, best, units),
    )
    mine, found = pair_call(
        functools.partial(far_kernel, block_count), "far_pairs", cost(4, 10**11),
        (BEST, RETURNED), 2, EDGE_SCRATCH, (place, far_list, mine, units, far_in),
    )
    returned, other = pair_call(
        functools.partial(bridge_kernel, block_count), "bridge_pairs", cost(1),
        (RETURNED, BEST), 3, [], (place, far_list, stats, found, far_in, chip_in),
    )
    back = lax.ppermute(returned, "shard", across)
    mine, other = pair_call(
        functools.partial(chip_kernel, block_count), "chip_pairs", cost(4), (BEST, BEST),
        2, EDGE_SCRATCH, (place, chip_list, mine, other, units, chip_in),
    )
    outgoing = finish(block_count, place, mine, other, back)
    groups = [list(range(c * 2 * REPS, (c + 1) * 2 * REPS)) for c in range(count // 2)]
    parts = lax.all_to_all(outgoing, ("shard", "rep"), 0, 0, axis_index_groups=groups)
    return jnp.max(parts, axis=0).reshape(OWN * BLOCK)


def solution(mesh):
    return jax.shard_map(
        shards,
        mesh=mesh,
        in_specs=(P("shard", None), P(), P("shard", None)),
        out_specs=P("shard"),
        check_vma=False,
    )
```

```python
import functools

import jax
import jax.numpy as jnp
from jax import lax
from jax.experimental import pallas as pl
from jax.experimental.pallas import tpu as pltpu
from jax.sharding import PartitionSpec as P

BLOCK = 256
SPANS = 17
WIDTH = 1024
OWN = 12
REPS = 4
MOVED = 8
NEAR = 4
CHIP_SLOTS = 2 + NEAR - 1
FAR_SLOTS = 2
TAIL = 16
FAR_ROWS = FAR_SLOTS * BLOCK + TAIL
CHIP_ROWS = CHIP_SLOTS * BLOCK + TAIL
WINDOW = OWN + 2 * (SPANS - 1)
GROUP = 8 * 128 // BLOCK
CHUNK = 128
WIDE, NARROW = 8, 4
FIELDS = 9
EPS = 1e-6
VMEM_LIMIT = 20 * 1024 * 1024

HBM = pl.BlockSpec(memory_space=pltpu.HBM)
ANY = pl.BlockSpec(memory_space=pl.ANY)
SMEM = pl.BlockSpec(memory_space=pltpu.SMEM)
VMEM = pl.BlockSpec(memory_space=pltpu.VMEM)


def cost(us, flops=0):
    return pl.CostEstimate(flops=flops, bytes_accessed=us * 3_000_000, transcendentals=0)


PARAMS = pltpu.CompilerParams(vmem_limit_bytes=VMEM_LIMIT)


def rows_of(slot, count=BLOCK):
    return pl.ds(pl.multiple_of(slot * BLOCK, BLOCK), count)


def unit_rows(rows):
    squares = jnp.sum(rows * rows, axis=1, keepdims=True)
    return (rows * lax.rsqrt(squares + EPS)).astype(jnp.bfloat16)


def normalise(raw, raw_slot, out, out_slot):
    for step in range(BLOCK // CHUNK):
        source = pl.ds(pl.multiple_of(raw_slot * BLOCK + step * CHUNK, CHUNK), CHUNK)
        target = pl.ds(pl.multiple_of(out_slot * BLOCK + step * CHUNK, CHUNK), CHUNK)
        out[target, :] = unit_rows(raw[source, :])


def far_local(core, m):
    return jnp.where(core == 0, m - 1, OWN - m)


def chip_local(core, m):
    return jnp.where(core == 0, OWN - m, m - 1)


def far_index(rep, slot):
    return jnp.where(slot == 0, rep + 1, MOVED - rep)


def chip_index(rep, slot):
    if slot < 2:
        return far_index(rep, slot)
    return slot - 1 + (slot - 1 > rep).astype(jnp.int32)


def flag_rows(holder, locals_of_slots):
    lane = lax.broadcasted_iota(jnp.int32, (TAIL, 128), 1)
    row = lax.broadcasted_iota(jnp.int32, (TAIL, 128), 0)
    flags = jnp.zeros((TAIL, 128), jnp.float32)
    for slot, local in enumerate(locals_of_slots):
        for k in range(SPANS):
            listed = jnp.where(holder[local * SPANS + k] != REPS, 1.0, 0.0)
            flags = jnp.where((row == slot) & (lane == k), listed, flags)
    return flags.astype(jnp.bfloat16)


def far_rows_kernel(place, holder_hbm, emb, far_out, raw, holder, sems, holder_sem):
    core, rep = place[0] % 2, place[1]
    local = [far_local(core, far_index(rep, slot)) for slot in range(FAR_SLOTS)]
    listing = pltpu.make_async_copy(holder_hbm, holder, holder_sem)
    listing.start()
    fetches = []
    for slot in range(FAR_SLOTS):
        for step in range(BLOCK // CHUNK):
            source = pl.ds(pl.multiple_of(local[slot] * BLOCK + step * CHUNK, CHUNK), CHUNK)
            part = pl.ds(slot * BLOCK + step * CHUNK, CHUNK)
            sem = sems.at[len(fetches)]
            fetches.append((part, pltpu.make_async_copy(emb.at[source], raw.at[part], sem)))
    for _, fetch in fetches:
        fetch.start()
    far_out[FAR_SLOTS * BLOCK :, :] = jnp.zeros((TAIL, WIDTH), jnp.bfloat16)
    for part, fetch in fetches:
        fetch.wait()
        far_out[part, :] = unit_rows(raw[part, :])
    listing.wait()
    far_out[pl.ds(FAR_SLOTS * BLOCK, TAIL), 0:128] = flag_rows(holder, local)


def far_rows(place, holder, emb):
    return pl.pallas_call(
        far_rows_kernel,
        out_shape=pltpu.VMEM((FAR_ROWS, WIDTH), jnp.bfloat16),
        in_specs=[SMEM, HBM, HBM],
        out_specs=VMEM,
        scratch_shapes=[
            pltpu.VMEM((FAR_SLOTS * BLOCK, WIDTH), jnp.float32),
            pltpu.SMEM(holder.shape, jnp.int32),
            pltpu.SemaphoreType.DMA((FAR_SLOTS * BLOCK // CHUNK,)),
            pltpu.SemaphoreType.DMA,
        ],
        compiler_params=PARAMS,
        cost_estimate=cost(1),
        name="far_rows",
    )(place, pltpu.with_memory_space_constraint(holder, pltpu.HBM), emb)


def similarity(left, right):
    return lax.dot_general(
        left, right, (((1,), (1,)), ((), ())), preferred_element_type=jnp.float32
    )


def inside(scored, row_low, row_end, col_low, col_end):
    rows = lax.broadcasted_iota(jnp.int32, (BLOCK, BLOCK), 0)
    cols = lax.broadcasted_iota(jnp.int32, (BLOCK, BLOCK), 1)
    keep = (rows >= row_low) & (rows < row_end) & (cols >= col_low) & (cols < col_end)
    return jnp.where(keep, scored, -1.0)


def fold_rows(scored):
    return jnp.maximum(scored[:, 0:128], scored[:, 128:256])


def fold_cols(scored):
    return jnp.max(scored.reshape(BLOCK // 8, 8, BLOCK), axis=0)


def as_lanes(column):
    rows = lax.broadcasted_iota(jnp.int32, (BLOCK, BLOCK), 0)
    cols = lax.broadcasted_iota(jnp.int32, (BLOCK, BLOCK), 1)
    return jnp.max(jnp.where(rows == cols, column, -1.0), axis=0, keepdims=True)


def first_group(shard, block_count):
    own = OWN // GROUP
    return jnp.clip(
        shard * own - (SPANS - 1) // GROUP, 0, (block_count - WINDOW) // GROUP
    )


def label_stats(stats, block_count, shard, block):
    slot = jnp.clip(block - first_group(shard, block_count) * GROUP, 0, WINDOW - 1)
    return [stats[part, slot] for part in range(4)]


def write_stats(tags, table):
    halves = [tags[pl.ds(half, WINDOW, stride=2), :].astype(jnp.float32) for half in range(2)]
    first, last = halves[0][:, 0:1], halves[1][:, 127:128]
    of_first = sum(jnp.where(half == first, 1.0, 0.0) for half in halves)
    before_last = sum(jnp.where(half < last, 1.0, 0.0) for half in halves)
    columns = [
        first,
        last,
        jnp.sum(of_first, axis=1, keepdims=True),
        jnp.sum(before_last, axis=1, keepdims=True),
    ]
    lane = lax.broadcasted_iota(jnp.int32, (WINDOW, 128), 1)
    spread = jnp.zeros((WINDOW, 128), jnp.float32)
    for part, column in enumerate(columns):
        spread = jnp.where(lane == part, column, spread)
    spread = jnp.concatenate([spread, jnp.zeros((128 - WINDOW, 128), jnp.float32)], axis=0)
    table[...] = spread.T[0:8, :].astype(jnp.int32)


def put_task(tasks, count, active, *fields):
    for place, field in enumerate(fields):
        tasks[count * FIELDS + place] = field
    return count + active.astype(jnp.int32)


def pad_tasks(tasks, count):
    for extra in range(WIDE - 1):
        for field in range(FIELDS):
            tasks[(count + extra) * FIELDS + field] = 0


def run_tasks(tasks, count, left, right, row_acc, col_acc):

    def run(first, width):
        found = []
        for lane in range(width):
            base = (first + lane) * FIELDS
            task = [tasks[base + field] for field in range(FIELDS)]
            scored = similarity(left[rows_of(task[0]), :], right[rows_of(task[1]), :])
            scored = inside(scored, *task[2:6])
            found.append((task[6], task[7], fold_rows(scored), fold_cols(scored)))
        for row_slot, col_slot, rows, cols in found:
            row_acc[row_slot] = jnp.maximum(row_acc[row_slot], rows)
            col_acc[col_slot] = jnp.maximum(col_acc[col_slot], cols)

    steps = (count + WIDE - NARROW - 1) // WIDE

    @pl.loop(0, steps)
    def _(step):
        run(step * WIDE, WIDE)

    @pl.when(count > steps * WIDE)
    def _():
        run(steps * WIDE, NARROW)


def task_words(most):
    return (most + WIDE) * FIELDS


OWN_TASKS = task_words(OWN * (OWN - 1) // 2)
EDGE_TASKS = task_words(2 * OWN)


def local_class(rep, turn):
    return (rep, 7 - rep, 8 + rep)[turn]


def rows_kernel(
    block_count, place, holder, labels, far, emb,
    units, chip_out, best, stats,
    raw, tags, sems, tag_sem,
):
    shard, rep = place[0], place[1]
    core = lax.rem(shard, 2)
    group = first_group(shard, block_count)
    sent = [far_local(core, far_index(rep, slot)) for slot in range(FAR_SLOTS)]
    local = [chip_local(core, chip_index(rep, slot)) for slot in range(CHIP_SLOTS)]

    def fetch(block):
        return pltpu.make_async_copy(
            emb.at[rows_of(block)], raw.at[rows_of(block)], sems.at[block]
        )

    def is_new(block):
        return (block != sent[0]) & (block != sent[1])

    window = pl.ds(pl.multiple_of(group * 8, 8), WINDOW * 2)
    fetch_tags = pltpu.make_async_copy(labels.at[window], tags, tag_sem)
    fetch_tags.start()

    def request(m):
        block = chip_local(core, m)
        pl.when(is_new(block))(lambda: fetch(block).start())

    pl.loop(1, 5)(request)
    chip_out[CHIP_SLOTS * BLOCK :, :] = jnp.zeros((TAIL, WIDTH), jnp.bfloat16)
    chip_out[CHIP_SLOTS * BLOCK :, 0:128] = flag_rows(holder, local)
    best[...] = jnp.full(best.shape, -1.0, jnp.float32)
    for slot in range(FAR_SLOTS):
        units[rows_of(sent[slot]), :] = far[rows_of(slot), :]
    fetch_tags.wait()
    write_stats(tags, stats)
    pl.loop(5, OWN + 1)(request)

    def diagonal(block):
        at = (shard * OWN + block - group * GROUP) * 2
        tag_row = jnp.concatenate([tags[pl.ds(at, 1), :], tags[pl.ds(at + 1, 1), :]], axis=1)
        tag_row = tag_row.astype(jnp.float32)
        rows = lax.broadcasted_iota(jnp.int32, (BLOCK, BLOCK), 0)
        cols = lax.broadcasted_iota(jnp.int32, (BLOCK, BLOCK), 1)
        spread = jnp.broadcast_to(tag_row, (BLOCK, BLOCK))
        tag_col = jnp.max(jnp.where(rows == cols, spread, -1.0), axis=1, keepdims=True)
        scored = similarity(units[rows_of(block), :], units[rows_of(block), :])
        keep = (tag_col == tag_row) & (rows != cols)
        found = jnp.max(jnp.where(keep, scored, -1.0), axis=0, keepdims=True)
        best[pl.ds(block, 1), :] = jnp.where(holder[block * SPANS] != REPS, found, -1.0)

    def arrive(m):
        block = chip_local(core, m)

        @pl.when(is_new(block))
        def _():
            fetch(block).wait()
            normalise(raw, block, units, block)

        mine = block == local_class(rep, 0)
        for turn in range(1, 3):
            mine = mine | (block == local_class(rep, turn))
        pl.when(mine)(lambda: diagonal(block))

    def arrive_and_send(m):
        arrive(m)
        block = chip_local(core, m)
        for slot in range(CHIP_SLOTS):

            @pl.when(block == local[slot])
            def _(slot=slot):
                chip_out[rows_of(slot), :] = units[rows_of(block), :]

    pl.loop(1, MOVED + 1)(arrive_and_send)
    pl.loop(MOVED + 1, OWN + 1)(arrive)


def own_rows(block_count, place, holder, labels, far, emb):
    return pl.pallas_call(
        functools.partial(rows_kernel, block_count),
        out_shape=(
            pltpu.VMEM((OWN * BLOCK, WIDTH), jnp.bfloat16),
            pltpu.VMEM((CHIP_ROWS, WIDTH), jnp.bfloat16),
            pltpu.VMEM((OWN, BLOCK), jnp.float32),
            pltpu.VMEM((8, 128), jnp.int32),
        ),
        in_specs=[SMEM, SMEM, HBM, VMEM, HBM],
        out_specs=(VMEM, VMEM, VMEM, VMEM),
        scratch_shapes=[
            pltpu.VMEM((OWN * BLOCK, WIDTH), jnp.float32),
            pltpu.VMEM((WINDOW * 2, 128), jnp.int32),
            pltpu.SemaphoreType.DMA((OWN,)),
            pltpu.SemaphoreType.DMA,
        ],
        compiler_params=PARAMS,
        cost_estimate=cost(5),
        name="own_rows",
    )(place, holder, labels, far, emb)


def flag_bits(tail, slot):
    lane = lax.broadcasted_iota(jnp.int32, (TAIL, 128), 1)
    row = lax.broadcasted_iota(jnp.int32, (TAIL, 128), 0)
    weight = lax.shift_left(jnp.int32(1), jnp.minimum(lane, SPANS)).astype(jnp.float32)
    weight = jnp.where((row == slot) & (lane < SPANS), weight, 0.0)
    return jnp.sum(tail[:, 0:128].astype(jnp.float32) * weight).astype(jnp.int32)


def has_bit(bits, offset):
    return lax.rem(lax.shift_right_logical(bits, offset), 2) == 1


class Boundary:
    def __init__(self, far, block_count, place):
        self.far, self.block_count = far, block_count
        self.shard, self.rep = place[0], place[1]
        self.core = lax.rem(self.shard, 2)
        self.side = self.core if far else 1 - self.core

    def local(self, m):
        return far_local(self.core, m) if self.far else chip_local(self.core, m)

    def near(self, which):
        return far_index(self.rep, which) if self.far else chip_index(self.rep, which)

    def start(self, stats, which):
        first_block = self.shard * OWN
        near = self.near(which)
        before = self.side == 0
        block = jnp.where(before, first_block - near, first_block + OWN - 1 + near)
        facts = label_stats(stats, self.block_count, self.shard, block)
        present = (block >= 0) & (block < self.block_count)
        return near, before, present, facts

    def shares(self, stats, moved, m):
        _, before, _, (m_first, m_last, _, _) = moved
        c_first, c_last, _, _ = self.column(stats, m)
        return jnp.where(before, m_last == c_first, c_last == m_first)

    def column(self, stats, m):
        first_block = self.shard * OWN
        block = jnp.where(self.side == 0, first_block + m - 1, first_block + OWN - m)
        return label_stats(stats, self.block_count, self.shard, block)

    def area(self, stats, moved, m):
        _, before, _, (_, _, m_count, m_start) = moved
        _, _, c_count, c_start = self.column(stats, m)
        return (
            jnp.where(before, m_start, 0), jnp.where(before, BLOCK, m_count),
            jnp.where(before, 0, c_start), jnp.where(before, c_count, BLOCK),
        )

    def lean(self, stats):
        middle = self.shard * OWN + jnp.where(self.side == 0, 0, OWN)
        facts = functools.partial(label_stats, stats, self.block_count, self.shard)
        label = facts(middle - 1)[1]
        ahead = lax.while_loop(
            lambda n: (n < jnp.minimum(middle, SPANS - 1)) & (facts(middle - 1 - n)[1] == label),
            lambda n: n + 1,
            jnp.int32(0),
        )
        behind = lax.while_loop(
            lambda n: (n < jnp.minimum(self.block_count - middle, SPANS - 1))
            & (facts(middle + n)[0] == label),
            lambda n: n + 1,
            jnp.int32(0),
        )
        return behind - ahead

    def first_column(self, near, lean):
        half = lax.shift_right_arithmetic(lean, 1)
        even = lean - 2 * half == 0
        behind = near + half + jnp.where(even & (lax.rem(near, 2) == 1), 0, 1)
        equal = near - half
        tie = even & (lax.rem(equal + 32, 2) == 1)
        ahead = equal + jnp.where(tie, 1, 0)
        return jnp.clip(jnp.where(self.side == 0, behind, ahead), 1, MOVED + 1)

    def list_tasks(self, tasks, stats, holder, bits=None):
        count = jnp.int32(0)
        lean = self.lean(stats)
        for which in range(2):
            moved = self.start(stats, which)
            near, before, present, _ = moved
            last = jnp.where(present, jnp.minimum(OWN, SPANS - near), 0)

            def shares(state, moved=moved, last=last):
                m, _ = state
                return (m <= last) & self.shares(stats, moved, m)

            def visit(state, which=which, moved=moved, near=near, before=before):
                m, count = state
                column, offset = self.local(m), near + m - 1
                moved_flag = True if bits is None else has_bit(bits[which], offset)
                column_flag = holder[column * SPANS + offset] != REPS
                listed = (before & moved_flag) | (jnp.logical_not(before) & column_flag)
                area = self.area(stats, moved, m)
                count = put_task(
                    tasks, count, listed, which, column, *area, which, column, offset
                )
                return m + 1, count

            first = self.first_column(near, lean)
            _, count = lax.while_loop(shares, visit, (first, count))
        return count

    def keep_listed(self, found, tasks, bits):
        def visit(index, count):
            task = [found[index * FIELDS + field] for field in range(FIELDS)]
            listed = has_bit(jnp.where(task[0] == 0, bits[0], bits[1]), task[8])
            return put_task(tasks, count, (self.side == 1) | listed, *task)

        count = lax.fori_loop(0, found[EDGE_TASKS], visit, jnp.int32(0))
        pad_tasks(tasks, count)
        return count


def own_kernel(
    block_count, place, holder, stats, best, units, mine, far_list, chip_list,
    row_acc, col_acc, tasks,
):
    col_acc[...] = jnp.full(col_acc.shape, -1.0, jnp.float32)
    row_acc[...] = jnp.full(row_acc.shape, -1.0, jnp.float32)
    shard, rep = place[0], place[1]

    def label_facts(block):
        return label_stats(stats, block_count, shard, shard * OWN + block)

    count = jnp.int32(0)
    for turn in range(3):
        block = local_class(rep, turn)
        b_first, _, b_count, _ = label_facts(block)

        def shares(state, b_first=b_first):
            other, _ = state
            return (other >= 0) & (label_facts(jnp.maximum(other, 0))[1] == b_first)

        def visit(state, block=block, turn=turn, b_count=b_count):
            other, count = state
            listed = holder[other * SPANS + (block - other)] != REPS
            a_start = label_facts(other)[3]
            count = put_task(
                tasks, count, listed, block, other, 0, b_count, a_start, BLOCK, turn, other,
                block - other,
            )
            return other - 1, count

        _, count = lax.while_loop(shares, visit, (block - 1, count))
    pad_tasks(tasks, count)
    run_tasks(tasks, count, units, units, row_acc, col_acc)
    mine[...] = jnp.maximum(best[...], jnp.max(col_acc[...], axis=1))
    for turn in range(3):
        here = (pl.ds(local_class(place[1], turn), 1), slice(None))
        found = as_lanes(jnp.max(row_acc[turn], axis=1, keepdims=True))
        mine[here] = jnp.maximum(mine[here], found)
    edge = Boundary(True, block_count, place)
    far_list[EDGE_TASKS] = edge.list_tasks(far_list, stats, holder)
    near = Boundary(False, block_count, place)
    chip_list[EDGE_TASKS] = near.list_tasks(chip_list, stats, holder)
    moved = edge.start(stats, 0)
    bridged = moved[2] & edge.shares(stats, moved, OWN + 1)
    far_list[EDGE_TASKS + 1] = bridged.astype(jnp.int32)


def far_kernel(
    block_count, place, far_list, best, units, far, mine, returned, row_acc, col_acc, tasks
):
    mine[...] = best[...]
    returned[...] = jnp.full(returned.shape, -1.0, jnp.float32)

    @pl.when(far_list[EDGE_TASKS] > 0)
    def _():
        edge = Boundary(True, block_count, place)
        col_acc[...] = jnp.full(col_acc.shape, -1.0, jnp.float32)
        row_acc[...] = jnp.full(row_acc.shape, -1.0, jnp.float32)
        tail = far[pl.ds(FAR_SLOTS * BLOCK, TAIL), :]
        bits = [flag_bits(tail, slot) for slot in range(2)]
        count = edge.keep_listed(far_list, tasks, bits)
        run_tasks(tasks, count, far, units, row_acc, col_acc)
        mine[...] = jnp.maximum(best[...], jnp.max(col_acc[...], axis=1))
        for which in range(2):
            returned[which : which + 1, :] = as_lanes(
                jnp.max(row_acc[which], axis=1, keepdims=True)
            )


def bridge_kernel(block_count, place, far_list, stats, found_in, far, chip, returned, other):
    returned[...] = found_in[...]
    other[...] = jnp.full(other.shape, -1.0, jnp.float32)

    @pl.when(far_list[EDGE_TASKS + 1] > 0)
    def _():
        edge = Boundary(True, block_count, place)
        far_bits = flag_bits(far[pl.ds(FAR_SLOTS * BLOCK, TAIL), :], 0)
        tail = chip[pl.ds(CHIP_SLOTS * BLOCK, TAIL), :]
        moved = edge.start(stats, 0)
        rows, cols = [], []
        slots = (0, 2, 3, 4)
        for slot in slots:
            m = OWN + chip_index(edge.rep, slot)
            offset, area = moved[0] + m - 1, edge.area(stats, moved, m)
            active = moved[2] & (offset < SPANS) & edge.shares(stats, moved, m)
            offset = jnp.minimum(offset, SPANS - 1)
            bits = jnp.where(edge.side == 0, far_bits, flag_bits(tail, slot))
            listed = has_bit(bits, offset)
            scored = inside(similarity(far[0:BLOCK, :], chip[rows_of(slot), :]), *area)
            scored = jnp.where(active & listed, scored, -1.0)
            rows.append(fold_rows(scored))
            cols.append(fold_cols(scored))
        for slot, found in zip(slots, cols):
            block = chip_local(1 - edge.core, chip_index(edge.rep, slot))
            other[pl.ds(block, 1), :] = jnp.max(found, axis=0, keepdims=True)
        best = functools.reduce(jnp.maximum, rows)
        best = as_lanes(jnp.max(best, axis=1, keepdims=True))
        returned[0:1, :] = jnp.maximum(returned[0:1, :], best)


def chip_kernel(
    block_count, place, chip_list, mine_in, other_in, units, chip,
    mine, other, row_acc, col_acc, tasks,
):
    edge = Boundary(False, block_count, place)
    col_acc[...] = jnp.full(col_acc.shape, -1.0, jnp.float32)
    row_acc[...] = jnp.full(row_acc.shape, -1.0, jnp.float32)
    tail = chip[pl.ds(CHIP_SLOTS * BLOCK, TAIL), :]
    bits = [flag_bits(tail, slot) for slot in range(2)]
    count = edge.keep_listed(chip_list, tasks, bits)
    run_tasks(tasks, count, chip, units, row_acc, col_acc)
    mine[...] = jnp.maximum(mine_in[...], jnp.max(col_acc[...], axis=1))
    other[...] = other_in[...]
    for which in range(2):
        here = (pl.ds(chip_local(1 - edge.core, edge.near(which)), 1), slice(None))
        found = as_lanes(jnp.max(row_acc[which], axis=1, keepdims=True))
        other[here] = jnp.maximum(other[here], found)


BEST = pltpu.VMEM((OWN, BLOCK), jnp.float32)
LIST = jax.ShapeDtypeStruct((EDGE_TASKS + 2,), jnp.int32)
RETURNED = pltpu.VMEM((2, BLOCK), jnp.float32)


def pair_call(kernel, name, estimate, outs, scalars, scratch, args):
    return pl.pallas_call(
        kernel,
        out_shape=outs,
        in_specs=[SMEM] * scalars + [VMEM] * (len(args) - scalars),
        out_specs=tuple(SMEM if out is LIST else VMEM for out in outs),
        scratch_shapes=scratch,
        compiler_params=PARAMS,
        cost_estimate=estimate,
        name=name,
    )(*args)


OWN_SCRATCH = [
    pltpu.VMEM((3, BLOCK, 128), jnp.float32),
    pltpu.VMEM((OWN, 8, BLOCK), jnp.float32),
    pltpu.SMEM((OWN_TASKS,), jnp.int32),
]
EDGE_SCRATCH = [
    pltpu.VMEM((2, BLOCK, 128), jnp.float32),
    pltpu.VMEM((OWN, 8, BLOCK), jnp.float32),
    pltpu.SMEM((EDGE_TASKS,), jnp.int32),
]


def finish_kernel(block_count, place, mine, other, back, outgoing, merged):
    shard, rep = place[0], place[1]
    core = lax.rem(shard, 2)
    has_far = (shard > 0) & (shard < block_count // OWN - 1)
    merged[...] = mine[...]
    for which in range(2):
        here = (pl.ds(far_local(core, far_index(rep, which)), 1), slice(None))
        found = jnp.where(has_far, back[which : which + 1, :], -1.0)
        merged[here] = jnp.maximum(merged[here], found)
    for target in range(2):
        share = jnp.where(core == target, merged[...], other[...])
        for copy in range(REPS):
            at = target * REPS + copy
            outgoing[at, pl.ds(0, OWN, stride=2), :] = share[:, 0:128]
            outgoing[at, pl.ds(1, OWN, stride=2), :] = share[:, 128:256]


def finish(block_count, place, mine, other, back):
    return pl.pallas_call(
        functools.partial(finish_kernel, block_count),
        out_shape=jax.ShapeDtypeStruct((2 * REPS, OWN * 2, 128), jnp.float32),
        in_specs=[SMEM, VMEM, VMEM, VMEM],
        out_specs=VMEM,
        scratch_shapes=[pltpu.VMEM((OWN, BLOCK), jnp.float32)],
        compiler_params=PARAMS,
        cost_estimate=cost(1),
        name="finish",
    )(place, mine, other, back)


def shards(embeddings, labels, holder):
    count = lax.axis_size("shard")
    block_count = count * OWN
    place = jnp.stack([lax.axis_index("shard"), lax.axis_index("rep")]).astype(jnp.int32)
    listing = holder.reshape(-1)
    labels = pltpu.with_memory_space_constraint(labels.reshape(-1, 128), pltpu.HBM)
    embeddings = pltpu.with_memory_space_constraint(embeddings, pltpu.HBM)
    across = [(s, s + 1) for s in range(1, count - 1, 2)]
    across = across + [(b, a) for a, b in across]
    within = [(s, s ^ 1) for s in range(count)]

    def in_vmem(array):
        return pltpu.with_memory_space_constraint(array, pltpu.VMEM)

    far_out = far_rows(place, listing, embeddings)
    far_in = in_vmem(lax.ppermute(far_out, "shard", across))
    units, chip_out, best, stats = own_rows(
        block_count, place, listing, labels, far_out, embeddings
    )
    chip_in = in_vmem(lax.ppermute(chip_out, "shard", within))

    mine, far_list, chip_list = pair_call(
        functools.partial(own_kernel, block_count), "own_pairs", cost(3), (BEST, LIST, LIST),
        3, OWN_SCRATCH, (place, listing, stats, best, units),
    )
    mine, found = pair_call(
        functools.partial(far_kernel, block_count), "far_pairs", cost(4, 10**11),
        (BEST, RETURNED), 2, EDGE_SCRATCH, (place, far_list, mine, units, far_in),
    )
    returned, other = pair_call(
        functools.partial(bridge_kernel, block_count), "bridge_pairs", cost(1),
        (RETURNED, BEST), 3, [], (place, far_list, stats, found, far_in, chip_in),
    )
    back = lax.ppermute(returned, "shard", across)
    mine, other = pair_call(
        functools.partial(chip_kernel, block_count), "chip_pairs", cost(4), (BEST, BEST),
        2, EDGE_SCRATCH, (place, chip_list, mine, other, units, chip_in),
    )
    outgoing = finish(block_count, place, mine, other, back)
    groups = [list(range(c * 2 * REPS, (c + 1) * 2 * REPS)) for c in range(count // 2)]
    parts = lax.all_to_all(outgoing, ("shard", "rep"), 0, 0, axis_index_groups=groups)
    return jnp.max(parts, axis=0).reshape(OWN * BLOCK)


def solution(mesh):
    return jax.shard_map(
        shards,
        mesh=mesh,
        in_specs=(P("shard", None), P(), P("shard", None)),
        out_specs=P("shard"),
        check_vma=False,
    )
```
